32 devices in a mesh: grp: 4 (over y, core), rep: 8 (over z, x).
Axes of the slice: x: 2, y: 2, z: 4, core: 2. Of those that a mesh axis runs over, the one named last changes fastest.
Arguments:
- tokens: bfloat16 [4096, 2048], P(('grp', 'rep')), may hold values from -6 to 6
- cotangent: bfloat16 [4096, 2048], P(('grp', 'rep')), may hold values from -6 to 6
- gain_attn: float32 [2048], replicated, may hold values from 0.5 to 1.5
- gain_ffn: float32 [2048], replicated, may hold values from 0.5 to 1.5
- w_query: bfloat16 [2048, 2048], P('grp'), may hold values from -0.125 to 0.125
- w_out: bfloat16 [2048, 2048], P('grp'), may hold values from -1 to 1
- w_gate: bfloat16 [2048, 5504], P('grp'), may hold values from -0.125 to 0.125
- w_up: bfloat16 [2048, 5504], P('grp'), may hold values from -0.125 to 0.125
- w_down: bfloat16 [5504, 2048], P('grp'), may hold values from -0.078125 to 0.078125
- keys: bfloat16 [4096, 512], P(('grp', 'rep')), may hold values from -6 to 6
- values: bfloat16 [4096, 512], P(('grp', 'rep')), may hold values from -6 to 6
- starts: int32 [8], replicated, may hold values from 0 to 4095, as said below
Outputs:
- output: bfloat16 [4096, 2048], P(('grp', 'rep'))
- d_tokens: bfloat16 [4096, 2048], P(('grp', 'rep'))
- d_gain_attn: float32 [2048], P(('grp', 'rep'))
- d_gain_ffn: float32 [2048], P(('grp', 'rep'))
- d_w_query: float32 [2048, 2048], P(('grp', 'rep'))
- d_w_out: float32 [2048, 2048], P(('grp', 'rep'))
- d_w_gate: float32 [2048, 5504], P(('grp', 'rep'))
- d_w_up: float32 [2048, 5504], P(('grp', 'rep'))
- d_w_down: float32 [5504, 2048], P(('grp', 'rep'))
- d_keys: bfloat16 [4096, 512], P(('grp', 'rep'))
- d_values: bfloat16 [4096, 512], P(('grp', 'rep'))
The draws below stay inside these ranges and needn't reach their ends.
Inputs may be any that keep to these rules, and one draw needn't show every extreme that they name: `starts`: strictly increasing with first entry 0; every document (from one start to the next, the last one to 4096) holds at most min(4096, 2048) tokens, and one holds exactly that many.
All inputs are finite; a program needn't handle non-finite values.
Results may differ from the reference program's by a relative error of at most 0.03.
Values may be sent and summed in bfloat16 or wider, within the bound.
No kernel may reach another device: no remote copies, remote signals or barrier semaphores. Data moves between devices by JAX's collectives and lax.ppermute only.
A program may use at most 448 MiB of HBM per device.

```python
import jax
import jax.numpy as jnp
from jax import lax

D = 2048
H = 16
HD = 128
KVH = 4
FF = 5504
MAXDOC = 4096
TOKENS = 4096
DOCS = 8


def draw_starts(key, part):
    subkeys = jax.random.split(key, 2)
    longest = min(MAXDOC, TOKENS // 2)
    remaining = TOKENS - longest
    weights = jax.random.randint(subkeys[0], (DOCS - 1,), 1000, 2001).astype(jnp.int32)
    others = remaining * weights // jnp.sum(weights)
    others = others.at[DOCS - 2].add(remaining - jnp.sum(others))
    place = jax.random.randint(subkeys[1], (), 0, DOCS).astype(jnp.int32)
    index = jnp.arange(DOCS, dtype=jnp.int32)
    pick = jnp.clip(jnp.where(index < place, index, index - 1), 0, DOCS - 2)
    lengths = jnp.where(index == place, longest, others[pick]).astype(jnp.int32)
    leading = jnp.zeros((1,), jnp.int32)
    return jnp.concatenate([leading, jnp.cumsum(lengths)[:-1].astype(jnp.int32)]).astype(jnp.int32)


def raised(drawn, key, source, target, parts, factor):
    owner, partner = [(jnp.arange(drawn.shape[axis_at]) // (drawn.shape[axis_at] // parts)).reshape([-1 if axis == axis_at else 1 for axis in range(drawn.ndim)]) for axis_at in (source, target)]
    chosen = jax.random.permutation(key, parts)[partner]
    strong = (owner == chosen) | (owner == (partner + parts // 2) % parts)
    return jnp.where(strong, factor * drawn, drawn)


def steps_of(rng, dims, shards, least, high):
    def one(position, blocks):
        steps = jax.random.uniform(jax.random.fold_in(jax.random.fold_in(rng, 6), position), (blocks,), jnp.float32, least / len(shards), high / len(shards))
        return jnp.repeat(jnp.exp(steps), dims[position] // blocks).reshape((-1,) + (1,) * (len(dims) - position - 1))

    factor_of = one(*shards[0])
    for cut in shards[1:]:
        factor_of = factor_of * one(*cut)
    return factor_of


def bell_draw(stream_key, extent, deviation, reach, shards=(), kind=jnp.bfloat16):
    result = jax.random.normal(stream_key, extent, jnp.float32) * deviation
    if len(shards) > 0:
        result = steps_of(stream_key, extent, shards, -0.22, 0.18) * result
    return jnp.clip(result, min=-reach, max=reach).astype(kind)


def noise_with(own_key, dims, deviation, most, cuts, heavy, kind=jnp.bfloat16):
    result = deviation * jax.random.normal(own_key, dims, jnp.float32)
    if cuts:
        result = result * steps_of(own_key, dims, cuts, -0.22, 0.18)
    return jnp.clip(raised(result, jax.random.fold_in(own_key, 3), *heavy), -most, most).astype(kind)


def setup_inputs(seed: int = 0) -> dict:
    seeds = jax.random.split(jax.random.key(seed), 13)
    tokens = noise_with(seeds[0], (TOKENS, D), 1.0, 6.0, ((0, 32),), (0, 1, 32, 2.75))
    cotangent = bell_draw(seeds[1], (TOKENS, D), 1.0, 6.0, ((0, 32),))
    gain_attn = jnp.clip(1.0 + 0.1 * jax.random.normal(seeds[2], (D,), jnp.float32), 0.5, 1.5)
    gain_ffn = jnp.clip(1.0 + 0.1 * jax.random.normal(seeds[3], (D,), jnp.float32), 0.5, 1.5)
    w_query = bell_draw(seeds[4], (D, D), D ** -0.5, 0.125, ((0, 4),))
    w_out = bell_draw(seeds[5], (D, D), (D // 64) ** -0.5, 1.0, ((0, 4),))
    w_gate = bell_draw(seeds[6], (D, FF), D ** -0.5, 0.125, ((0, 4),))
    w_up = bell_draw(seeds[7], (D, FF), D ** -0.5, 0.125, ((0, 4),))
    w_down = bell_draw(seeds[8], (FF, D), FF ** -0.5, 0.078125, ((0, 4),))
    keys = bell_draw(seeds[9], (TOKENS, KVH * HD), 1.0, 6.0, ((0, 32),))
    values = bell_draw(seeds[10], (TOKENS, KVH * HD), 1.0, 6.0, ((0, 32),))
    starts = draw_starts(jax.random.fold_in(seeds[12], 71), 0)
    return dict(tokens=tokens, cotangent=cotangent, gain_attn=gain_attn, gain_ffn=gain_ffn, w_query=w_query, w_out=w_out, w_gate=w_gate, w_up=w_up, w_down=w_down, keys=keys, values=values, starts=starts)


@jax.custom_vjp
def low(v):
    return lax.optimization_barrier(v.astype(jnp.bfloat16)).astype(jnp.float32)

@jax.custom_vjp
def low_back(v):
    return v

def low_keep(v):
    return (low(v), None)

def low_pass(kept, grad):
    return (grad,)

def back_keep(v):
    return (v, None)

def back_low(kept, grad):
    return (low(grad),)
low.defvjp(low_keep, low_pass)
low_back.defvjp(back_keep, back_low)
EPSILON = 1e-06
NEGATIVE = -1e+30
HIGHEST = lax.Precision.HIGHEST

def matmul(left, right):
    return jnp.dot(left, right, precision=HIGHEST, preferred_element_type=jnp.float32)

def forward(x, gain_attn, gain_ffn, w_query, w_out, w_gate, w_up, w_down, keys, values, starts):
    inv_one = lax.rsqrt(lax.optimization_barrier(jnp.mean(x * x, axis=1, keepdims=True)) + EPSILON)
    h_one = low(x * inv_one * gain_attn)
    query = low_back(low(matmul(h_one, w_query)))
    positions = jnp.arange(TOKENS, dtype=jnp.int32)
    docs = lax.optimization_barrier(jnp.sum((starts[None, :] <= positions[:, None]).astype(jnp.int32), axis=1)) - 1
    keys_three = keys.reshape(TOKENS, KVH, HD)
    values_three = values.reshape(TOKENS, KVH, HD)
    row_block = 256
    blocks = TOKENS // row_block
    share = H // KVH
    scale = HD ** (-0.5)
    query_blocks = query.reshape(blocks, row_block, KVH, share, HD)
    pos_blocks = positions.reshape(blocks, row_block)
    doc_blocks = docs.reshape(blocks, row_block)

    def one_block(items):
        query_block, query_pos, query_doc = items
        scores = jnp.einsum('qgsd,kgd->gsqk', query_block, keys_three, precision=HIGHEST)
        scores = low_back(scores * scale)
        allowed = (docs[None, :] == query_doc[:, None]) & (positions[None, :] <= query_pos[:, None])
        scores = jnp.where(allowed[None, None], scores, NEGATIVE)
        probs = jax.nn.softmax(scores, axis=3)
        mixed = jnp.einsum('gsqk,kgd->qgsd', low(probs), values_three, precision=HIGHEST)
        return mixed.reshape(row_block, D)
    attended = lax.map(jax.checkpoint(one_block), (query_blocks, pos_blocks, doc_blocks)).reshape(TOKENS, D)
    attn_low = low_back(low(attended))
    branch = low_back(matmul(attn_low, w_out))
    resid = x + branch
    inv_two = lax.rsqrt(lax.optimization_barrier(jnp.mean(resid * resid, axis=1, keepdims=True)) + EPSILON)
    h_two = low(resid * inv_two * gain_ffn)
    gate = low_back(matmul(h_two, w_gate))
    upper = low_back(matmul(h_two, w_up))
    hidden = low(jax.nn.silu(gate) * upper)
    return resid + matmul(hidden, w_down)

def reference(tokens, cotangent, gain_attn, gain_ffn, w_query, w_out, w_gate, w_up, w_down, keys, values, starts):
    floats = tuple((item.astype(jnp.float32) for item in (tokens, gain_attn, gain_ffn, w_query, w_out, w_gate, w_up, w_down, keys, values)))

    def wrapped(x, g_one, g_two, wq_full, wo_full, wg_full, wu_full, wd_full, key_all, value_all):
        return forward(x, g_one, g_two, wq_full, wo_full, wg_full, wu_full, wd_full, key_all, value_all, starts)
    output, pullback = jax.vjp(wrapped, *floats)
    grads = pullback(cotangent.astype(jnp.float32))
    d_tok, d_g_one, d_g_two, d_wq, d_wo, d_wg, d_wu, d_wd, d_key, d_value = grads
    return (output.astype(jnp.bfloat16), d_tok.astype(jnp.bfloat16), d_g_one, d_g_two, d_wq, d_wo, d_wg, d_wu, d_wd, d_key.astype(jnp.bfloat16), d_value.astype(jnp.bfloat16))
```

```python
import functools

import jax
import jax.numpy as jnp
from jax import lax
from jax.experimental import pallas as pl
from jax.experimental.pallas import tpu as pltpu
from jax.sharding import PartitionSpec as P

HD = 128
EPSILON = 1e-06
NEGATIVE = -1e30
F32 = jnp.float32
BF16 = jnp.bfloat16
BOTH = ("grp", "rep")


def swap(value, mask):
    count = lax.axis_size(BOTH)
    return lax.ppermute(value, BOTH, [(i, i ^ mask) for i in range(count)])


def after(value, *earlier):
    return lax.optimization_barrier((value,) + earlier)[0]


def dot(a, b):
    return jnp.dot(a, b, preferred_element_type=F32)


def dot_t(a, b):
    return lax.dot_general(a, b, (((1,), (1,)), ((), ())), preferred_element_type=F32)


def t_dot(a, b):
    return lax.dot_general(a, b, (((0,), (0,)), ((), ())), preferred_element_type=F32)


def pick(value, index, axis):
    return lax.dynamic_index_in_dim(value, index, axis, keepdims=False)


def gather_four(block, core, yy):
    over_y = swap(block, yy)
    over_c = swap(block, core)
    diagonal = swap(over_y, core)
    return jnp.stack([block, over_c, over_y, diagonal])


def scatter_four(parts, core, yy):
    parts = parts.reshape((2, 2) + parts.shape[1:])
    got = swap(parts[:, 1].astype(BF16), core)
    parts = parts[:, 0] + got.astype(F32)
    got = swap(parts[1].astype(BF16), yy)
    return parts[0] + got.astype(F32)


def gather_eight(block, core, yy, zz):
    half = block.shape[0] // 2
    over_y = swap(block, yy)
    over_z = swap(block, zz)
    low = swap(over_y[:half], zz)
    high = swap(over_z[half:], yy)
    near = jnp.stack([block, over_y])
    far = jnp.stack([over_z, jnp.concatenate([low, high])])
    near_c = swap(near, core)
    far_c = swap(far, core)
    whole = jnp.stack([jnp.stack([near, near_c], 1), jnp.stack([far, far_c], 1)])
    return whole.reshape((8,) + block.shape)


def scatter_eight(parts, core, yy, zz):
    rows = parts.shape[1]
    half = rows // 2
    parts = parts.reshape((2, 2, 2) + parts.shape[1:])
    got = swap(parts[:, :, 1].astype(BF16), core)
    parts = parts[:, :, 0] + got.astype(F32)
    corner = parts[1, 1].astype(BF16)
    to_z = swap(corner[:half], yy)
    to_y = swap(corner[half:], zz)
    for_z = jnp.concatenate([parts[1, 0, :half] + to_z.astype(F32), parts[1, 0, half:]])
    for_y = jnp.concatenate([parts[0, 1, :half], parts[0, 1, half:] + to_y.astype(F32)])
    from_z = swap(for_z.astype(BF16), zz)
    from_y = swap(for_y.astype(BF16), yy)
    return parts[0, 0] + from_z.astype(F32) + from_y.astype(F32)


def exchange_four(pieces, core, yy):
    from_y = swap(jnp.stack([pieces[2], pieces[3]]), yy)
    from_c = swap(jnp.stack([pieces[1], from_y[1]]), core)
    return [pieces[0], from_c[0], from_y[0], from_c[1]]


def absolute(pieces, g):
    odd, upper = (g & 1) == 1, (g >> 1) == 1
    a = jnp.where(odd, pieces[1], pieces[0])
    b = jnp.where(odd, pieces[0], pieces[1])
    c = jnp.where(odd, pieces[3], pieces[2])
    d = jnp.where(odd, pieces[2], pieces[3])
    return [
        jnp.where(upper, c, a),
        jnp.where(upper, d, b),
        jnp.where(upper, a, c),
        jnp.where(upper, b, d),
    ]


def halve(value, bit, mask, axis):
    got = swap(pick(value, 1 - bit, axis).astype(BF16), mask)
    return pick(value, bit, axis).astype(F32) + got.astype(F32)


def block_bounds(info_ref, starts_ref, j, reps):
    place = ((info_ref[0] ^ j) * reps + info_ref[1]) * HD
    docs = starts_ref.shape[0]
    first = jnp.int32(0)
    for d in range(docs):
        first = jnp.maximum(first, jnp.where(starts_ref[d] <= place, starts_ref[d], 0))
    position = place + lax.broadcasted_iota(jnp.int32, (4, HD, 1), 1).reshape(4 * HD, 1)
    lowest = jnp.zeros_like(position)
    for d in range(docs):
        lowest = jnp.maximum(lowest, jnp.where(starts_ref[d] <= position, starts_ref[d], 0))
    return place, first, position, lowest


def key_tile(info_ref, kv_ref, tile, reps):
    per = reps // 4
    member = (tile // per) ^ info_ref[0]
    piece = kv_ref[pl.ds(4 * (tile % per), 4), member]
    piece = piece.reshape(4 * HD, 2 * HD)
    return piece[:, :HD], piece[:, HD:]


def head_rows(ref):
    return jnp.concatenate([ref[0, :, h * HD : (h + 1) * HD] for h in range(4)], axis=0)


def attend_kernel(reps, info_ref, starts_ref, q_ref, kv_ref, o_ref, lse_ref):
    j = pl.program_id(0)
    place, first, position, lowest = block_bounds(info_ref, starts_ref, j, reps)
    query = head_rows(q_ref)
    rows = 4 * HD
    scale = HD ** (-0.5)

    def step(tile, carry):
        best, total, accum = carry
        key, value = key_tile(info_ref, kv_ref, tile, reps)
        scores = dot_t(query, key) * scale
        at = tile * 512 + lax.broadcasted_iota(jnp.int32, (1, 512), 1)
        scores = jnp.where((at >= lowest) & (at <= position), scores, NEGATIVE)
        new_best = jnp.maximum(best, jnp.max(scores, axis=1, keepdims=True))
        weights = jnp.exp(scores - new_best)
        factor = jnp.exp(best - new_best)
        total = total * factor + jnp.sum(weights, axis=1, keepdims=True)
        accum = accum * factor + dot(weights.astype(BF16), value)
        return new_best, total, accum

    init = (
        jnp.full((rows, 1), NEGATIVE, F32),
        jnp.zeros((rows, 1), F32),
        jnp.zeros((rows, HD), F32),
    )
    best, total, accum = lax.fori_loop(first // 512, place // 512 + 1, step, init)
    out = accum / total
    for h in range(4):
        o_ref[0, :, h * HD : (h + 1) * HD] = out[h * HD : (h + 1) * HD].astype(BF16)
    lse_ref[0] = best + jnp.log(total)


def attend(info, starts, query, kv):
    reps = kv.shape[0]
    return pl.pallas_call(
        functools.partial(attend_kernel, reps),
        grid=(4,),
        in_specs=[
            pl.BlockSpec(memory_space=pltpu.SMEM),
            pl.BlockSpec(memory_space=pltpu.SMEM),
            pl.BlockSpec((1, HD, 4 * HD), lambda j: (j, 0, 0)),
            pl.BlockSpec(kv.shape, lambda j: (0, 0, 0, 0)),
        ],
        out_specs=[
            pl.BlockSpec((1, HD, 4 * HD), lambda j: (j, 0, 0)),
            pl.BlockSpec((1, 4 * HD, 1), lambda j: (j, 0, 0)),
        ],
        out_shape=[
            jax.ShapeDtypeStruct((4, HD, 4 * HD), BF16),
            jax.ShapeDtypeStruct((4, 4 * HD, 1), F32),
        ],
        compiler_params=pltpu.CompilerParams(vmem_limit_bytes=48 << 20),
        name="attend",
    )(info, starts, query, kv)


def attend_back_kernel(
    reps, info_ref, starts_ref, q_ref, do_ref, o_ref, lse_ref, kv_ref, dq_ref, dkv_ref, sums
):
    j = pl.program_id(0)

    @pl.when(j == 0)
    def _():
        sums[...] = jnp.zeros_like(sums)

    place, first, position, lowest = block_bounds(info_ref, starts_ref, j, reps)
    query = head_rows(q_ref)
    d_out = head_rows(do_ref)
    out = head_rows(o_ref)
    lse = lse_ref[0]
    delta = jnp.sum(d_out.astype(F32) * out.astype(F32), axis=1, keepdims=True)
    scale = HD ** (-0.5)
    per = reps // 4

    def step(tile, d_query):
        key, value = key_tile(info_ref, kv_ref, tile, reps)
        scores = dot_t(query, key) * scale
        at = tile * 512 + lax.broadcasted_iota(jnp.int32, (1, 512), 1)
        probs = jnp.where((at >= lowest) & (at <= position), jnp.exp(scores - lse), 0.0)
        d_probs = dot_t(d_out, value)
        d_scores = (probs * (d_probs - delta)).astype(BF16)
        d_query = d_query + dot(d_scores, key)
        d_key = t_dot(d_scores, query) * scale
        d_value = t_dot(probs.astype(BF16), d_out)
        where = (pl.ds(4 * (tile % per), 4), (tile // per) ^ info_ref[0])
        both = jnp.concatenate([d_key, d_value], axis=1)
        sums[where] = sums[where] + both.reshape(4, HD, 2 * HD)
        return d_query

    d_query = lax.fori_loop(
        first // 512, place // 512 + 1, step, jnp.zeros((4 * HD, HD), F32)
    )
    d_query = (d_query * scale).astype(BF16)
    for h in range(4):
        dq_ref[0, :, h * HD : (h + 1) * HD] = d_query[h * HD : (h + 1) * HD]

    @pl.when(j == 3)
    def _():
        dkv_ref[...] = sums[...].astype(BF16)


def attend_back(info, starts, query, d_out, out, lse, kv):
    reps = kv.shape[0]
    rows = pl.BlockSpec((1, HD, 4 * HD), lambda j: (j, 0, 0))
    whole = pl.BlockSpec(kv.shape, lambda j: (0, 0, 0, 0))
    return pl.pallas_call(
        functools.partial(attend_back_kernel, reps),
        grid=(4,),
        in_specs=[
            pl.BlockSpec(memory_space=pltpu.SMEM),
            pl.BlockSpec(memory_space=pltpu.SMEM),
            rows,
            rows,
            rows,
            pl.BlockSpec((1, 4 * HD, 1), lambda j: (j, 0, 0)),
            whole,
        ],
        out_specs=[rows, whole],
        out_shape=[
            jax.ShapeDtypeStruct((4, HD, 4 * HD), BF16),
            jax.ShapeDtypeStruct(kv.shape, BF16),
        ],
        scratch_shapes=[pltpu.VMEM(kv.shape, F32)],
        compiler_params=pltpu.CompilerParams(vmem_limit_bytes=60 << 20),
        name="attend_back",
    )(info, starts, query, d_out, out, lse, kv)


def on_device(
    tokens,
    cotangent,
    gain_attn,
    gain_ffn,
    w_query,
    w_out,
    w_gate,
    w_up,
    w_down,
    keys,
    values,
    starts,
):
    reps = lax.axis_size("rep")
    rows, width = tokens.shape
    hidden_all = w_gate.shape[1]
    g = lax.axis_index("grp")
    r = lax.axis_index("rep")
    core, yy, xx, zz = reps, 2 * reps, 1, 2
    high = [1 << k for k in range(2, 16) if (1 << k) < reps]
    outer = reps // 4
    x_bit, z_bit = r & 1, (r >> 1) & 1
    share = width // 4
    out_rows = width // (4 * reps)
    chunk = hidden_all // (4 * reps)
    run = 2 * chunk
    mine = outer * run
    info = jnp.stack([g, r]).astype(jnp.int32)

    x_full = tokens.astype(F32)
    inv_one = lax.rsqrt(jnp.mean(x_full * x_full, axis=1, keepdims=True) + EPSILON)
    normed_one = x_full * inv_one
    h_one = (normed_one * gain_attn).astype(BF16)

    kv_parts = [
        jnp.concatenate(
            [
                lax.dynamic_slice_in_dim(keys, (g ^ j) * HD, HD, 1),
                lax.dynamic_slice_in_dim(values, (g ^ j) * HD, HD, 1),
            ],
            axis=1,
        )
        for j in range(4)
    ]
    kv_own = jnp.stack(exchange_four(kv_parts, core, yy))
    kv = lax.all_gather(kv_own, "rep", axis=0, tiled=False)

    h_group = gather_four(h_one, core, yy).reshape(4 * rows, width)
    wq_parts = exchange_four(
        [lax.dynamic_slice_in_dim(w_query, (g ^ j) * share, share, 1) for j in range(4)], core, yy
    )
    wq_cols = jnp.concatenate(absolute(wq_parts, g), axis=0)
    query = dot(h_group, wq_cols).astype(BF16).reshape(4, rows, share)

    def columns(weight):
        def of(member, bit):
            base = member * (hidden_all // 4)
            return jnp.concatenate(
                [
                    weight[:, base + o * 2 * run + bit * run : base + o * 2 * run + (bit + 1) * run]
                    for o in range(outer)
                ],
                axis=1,
            )

        packed = jnp.stack([jnp.where(z_bit == 1, of(m, 1), of(m, 0)) for m in range(4)])
        packed = after(packed, h_group, wq_cols)
        got = exchange_four([pick(packed, g ^ j, 0) for j in range(4)], core, yy)
        return jnp.concatenate(absolute(got, g), axis=0)

    wg = columns(w_gate)
    wu = columns(w_up)
    wd = pick(w_down.reshape(outer, 2, run, width), z_bit, 1).reshape(mine, width)
    dy_group = gather_eight(after(cotangent, query), core, yy, zz).reshape(8 * rows, width)

    attn, lse = attend(info, starts, query, kv)
    attn_rows = attn.reshape(4 * rows, share)
    branch = scatter_four(dot(attn_rows, w_out).reshape(4, rows, width), core, yy)
    resid = x_full + branch
    inv_two = lax.rsqrt(jnp.mean(resid * resid, axis=1, keepdims=True) + EPSILON)
    normed_two = resid * inv_two
    h_two = (normed_two * gain_ffn).astype(BF16)

    h_eight = gather_eight(h_two, core, yy, zz).reshape(8 * rows, width)
    d_hidden = dot_t(dy_group, wd)
    gate = dot(h_eight, wg)
    upper = dot(h_eight, wu)
    sigma = jax.nn.sigmoid(gate)
    swish = gate * sigma
    hidden = (swish * upper).astype(BF16)
    d_gate = (d_hidden * upper * sigma * (1.0 + gate * (1.0 - sigma))).astype(BF16)
    d_upper = (d_hidden * swish).astype(BF16)
    d_h_parts = dot_t(d_gate, wg) + dot_t(d_upper, wu)
    d_h_two = scatter_eight(d_h_parts.reshape(8, rows, width), core, yy, zz)

    d_wdown = t_dot(hidden, dy_group).reshape(outer, 2, chunk, width)
    d_wdown = halve(d_wdown, x_bit, xx, 1)
    d_wg = t_dot(h_eight, d_gate).reshape(4 * outer * 2, 2, out_rows, mine)
    d_wg = halve(d_wg, x_bit, xx, 1)
    d_wu = t_dot(h_eight, d_upper).reshape(4 * outer * 2, 2, out_rows, mine)
    d_wu = halve(d_wu, x_bit, xx, 1)
    d_gu = jnp.stack([d_wg, d_wu]).reshape(2, 4, outer, 2, out_rows, mine)
    size = outer
    for mask in reversed(high):
        size //= 2
        bit = (r & mask) // mask
        d_wdown = halve(d_wdown.reshape(2, size, chunk, width), bit, mask, 0)
        d_gu = halve(d_gu.reshape(2, 4, 2, size, 2, out_rows, mine), bit, mask, 2)
    d_wdown = d_wdown.reshape(chunk, width)
    d_gu = d_gu.reshape(2, 4, 2, out_rows, mine).astype(BF16)
    other = swap(pick(d_gu, 1 - z_bit, 2), zz)
    d_gu = jnp.stack([pick(d_gu, z_bit, 2), other], axis=2)
    got = exchange_four([pick(d_gu, g ^ j, 1) for j in range(4)], core, yy)
    got = absolute(got, g)

    def assemble(which):
        out = []
        for member in range(4):
            near, far = got[member][which, 0], got[member][which, 1]
            low = jnp.where(z_bit == 0, near, far)
            upp = jnp.where(z_bit == 0, far, near)
            for o in range(outer):
                out.append(low[:, o * run : (o + 1) * run])
                out.append(upp[:, o * run : (o + 1) * run])
        return jnp.concatenate(out, axis=1).astype(F32)

    d_wgate, d_wup = assemble(0), assemble(1)

    output = (
        resid + scatter_eight(dot(hidden, wd).reshape(8, rows, width), core, yy, zz)
    ).astype(BF16)

    d_gain_two = jnp.sum(d_h_two * normed_two, axis=0)
    scaled_two = d_h_two * gain_ffn
    d_resid = cotangent.astype(F32) + inv_two * (
        scaled_two - normed_two * jnp.mean(scaled_two * normed_two, axis=1, keepdims=True)
    )

    d_group = gather_four(d_resid.astype(BF16), core, yy).reshape(4 * rows, width)
    d_attn = dot_t(d_group, w_out).astype(BF16).reshape(4, rows, share)
    d_query, d_kv = attend_back(info, starts, query, d_attn, attn, lse, kv)
    d_query = d_query.reshape(4 * rows, share)
    d_h_one = scatter_four(dot_t(d_query, wq_cols).reshape(4, rows, width), core, yy)
    d_wout = lax.psum_scatter(
        t_dot(attn_rows, d_group).astype(BF16), "rep", scatter_dimension=0, tiled=True
    ).astype(F32)
    d_kv = lax.psum_scatter(d_kv, "rep", scatter_dimension=0, tiled=False)
    d_kv = absolute(exchange_four([d_kv[j] for j in range(4)], core, yy), g)
    d_keys = jnp.concatenate([piece[:, :HD] for piece in d_kv], axis=1)
    d_values = jnp.concatenate([piece[:, HD:] for piece in d_kv], axis=1)
    d_wq = t_dot(h_group, d_query).astype(BF16).reshape(4, reps, out_rows, share)
    d_wq = lax.psum_scatter(jnp.swapaxes(d_wq, 0, 1), "rep", scatter_dimension=0, tiled=False)
    d_wq = absolute(exchange_four([pick(d_wq, g ^ j, 0) for j in range(4)], core, yy), g)
    d_wquery = jnp.concatenate(d_wq, axis=1).astype(F32)

    d_gain_one = jnp.sum(d_h_one * normed_one, axis=0)
    scaled_one = d_h_one * gain_attn
    d_tokens = (
        d_resid
        + inv_one
        * (scaled_one - normed_one * jnp.mean(scaled_one * normed_one, axis=1, keepdims=True))
    ).astype(BF16)
    gains = jnp.stack(
        [d_gain_one.reshape(4 * reps, out_rows), d_gain_two.reshape(4 * reps, out_rows)], axis=1
    )
    gains = lax.psum_scatter(gains, BOTH, scatter_dimension=0, tiled=False)
    return (
        output,
        d_tokens,
        gains[0],
        gains[1],
        d_wquery,
        d_wout,
        d_wgate,
        d_wup,
        d_wdown,
        d_keys,
        d_values,
    )


def solution(mesh):
    spread = P(BOTH, None)
    member = P("grp", None)
    in_specs = (
        spread,
        spread,
        P(),
        P(),
        member,
        member,
        member,
        member,
        member,
        spread,
        spread,
        P(),
    )
    out_specs = (
        spread,
        spread,
        P(BOTH),
        P(BOTH),
        spread,
        spread,
        spread,
        spread,
        spread,
        spread,
        spread,
    )
    return jax.shard_map(
        on_device, mesh=mesh, in_specs=in_specs, out_specs=out_specs, check_vma=False
    )
```

```python
import functools

import jax
import jax.numpy as jnp
from jax import lax
from jax.experimental import pallas as pl
from jax.experimental.pallas import tpu as pltpu
from jax.sharding import PartitionSpec as P

HD = 128
EPSILON = 1e-06
NEGATIVE = -1e30
F32 = jnp.float32
BF16 = jnp.bfloat16
BOTH = ("grp", "rep")
BRIEF = pl.CostEstimate(flops=1, transcendentals=0, bytes_accessed=1)


def swap(value, mask):
    count = lax.axis_size(BOTH)
    return lax.ppermute(value, BOTH, [(i, i ^ mask) for i in range(count)])


def after(value, *earlier):
    return lax.optimization_barrier((value,) + earlier)[0]


def together(*values):
    return lax.optimization_barrier(values)


def dot(a, b):
    return jnp.dot(a, b, preferred_element_type=F32)


def dot_t(a, b):
    return lax.dot_general(a, b, (((1,), (1,)), ((), ())), preferred_element_type=F32)


def t_dot(a, b):
    return lax.dot_general(a, b, (((0,), (0,)), ((), ())), preferred_element_type=F32)


def pick(value, index, axis):
    return lax.dynamic_index_in_dim(value, index, axis, keepdims=False)


def scatter_four_core(parts, core):
    parts = parts.reshape((2, 2) + parts.shape[1:])
    got = swap(parts[:, 1].astype(BF16), core)
    return parts[:, 0] + got.astype(F32)


def corner_step(parts, yy, zz):
    half = parts.shape[1] // 2
    corner = parts[3].astype(BF16)
    return swap(corner[:half], yy), swap(corner[half:], zz)


def side_step(parts, to_z, to_y, yy, zz):
    half = parts.shape[1] // 2
    for_z = jnp.concatenate([parts[2, :half] + to_z.astype(F32), parts[2, half:]])
    for_y = jnp.concatenate([parts[1, :half], parts[1, half:] + to_y.astype(F32)])
    return swap(for_z.astype(BF16), zz), swap(for_y.astype(BF16), yy)


def exchange_four(pieces, core, yy):
    from_y = swap(jnp.stack([pieces[2], pieces[3]]), yy)
    from_c = swap(pieces[1], core)
    return [pieces[0], from_c, from_y[0], swap(from_y[1], core)]


def absolute(pieces, g):
    odd, upper = (g & 1) == 1, (g >> 1) == 1
    a = jnp.where(odd, pieces[1], pieces[0])
    b = jnp.where(odd, pieces[0], pieces[1])
    c = jnp.where(odd, pieces[3], pieces[2])
    d = jnp.where(odd, pieces[2], pieces[3])
    return [
        jnp.where(upper, c, a),
        jnp.where(upper, d, b),
        jnp.where(upper, a, c),
        jnp.where(upper, b, d),
    ]


def halve(value, bit, mask, axis, hold=None):
    got = swap(pick(value, 1 - bit, axis).astype(BF16), mask)
    if hold is not None:
        got = after(got, hold)
    return pick(value, bit, axis).astype(F32) + got.astype(F32)


def scatter_high(value, r, high, axis, hold=None):
    for mask in reversed(high):
        shape = value.shape
        value = value.reshape(shape[:axis] + (2, shape[axis] // 2) + shape[axis + 1 :])
        value = halve(value, (r & mask) // mask, mask, axis, hold)
    return jnp.squeeze(value, axis)


def scatter_rep(value, r, high, hold=None):
    reps = value.shape[0]
    rest = value.shape[1:]
    value = halve(value.reshape((reps // 4, 2, 2) + rest), r & 1, 1, 2, hold)
    value = halve(value, (r >> 1) & 1, 2, 1)
    return scatter_high(value, r, high, 0)


def ring_of(reps):
    ring = (0, 1, 3, 2)
    pairs = []
    for member in range(4):
        for k in range(4):
            for x in range(2):
                base = member * reps + x
                pairs.append((base + 2 * ring[k], base + 2 * ring[(k + 1) % 4]))
    return pairs


def ring_slots(r, reps):
    order = jnp.array((0, 1, 3, 2), jnp.int32)
    other = jnp.arange(reps, dtype=jnp.int32)
    steps = (order[r >> 1] - order[other >> 1]) & 3
    return 2 * steps + ((other ^ r) & 1)


def pack_kernel(
    outer, chunk, wide, info_ref, gate_ref, up_ref, stay_ref, core_ref, y_ref, relay_ref, held
):
    step = pl.program_id(0)
    g, bit, x = info_ref[0], (info_ref[1] >> 1) & 1, info_ref[1] & 1
    rows = gate_ref.shape[0]
    quarter = outer * 4 * chunk
    fill = jnp.zeros((rows, wide - chunk), BF16)

    for b in range(2):

        @pl.when(bit == b)
        def _():
            for which, ref in enumerate((gate_ref, up_ref)):
                block = ref[...]
                for member in range(4):
                    parts = []
                    for xd in range(2):
                        for o in range(outer):
                            at = member * quarter + (o * 4 + b * 2 + xd) * chunk
                            parts += [block[:, at : at + chunk], fill]
                    span = 2 * outer * wide
                    held[member ^ g, :, which * span : (which + 1) * span] = jnp.concatenate(
                        parts, axis=1
                    )

    stay_ref[...] = held[0]
    core_ref[...] = held[1]

    @pl.when(step // (pl.num_programs(0) // 2) == x)
    def _():
        y_ref[...] = held[2]
        relay_ref[...] = held[3]


def pack(info, w_gate, w_up, outer, chunk, wide):
    rows, width = w_gate.shape
    span = 4 * outer * wide
    steps = 8
    part = rows // steps

    def lower(i, info):
        return jnp.clip(i - (info[1] & 1) * (steps // 2), 0, steps // 2 - 1), 0

    def plain(i, info):
        return i, 0

    shape = jax.ShapeDtypeStruct((rows, span), BF16)
    small = jax.ShapeDtypeStruct((rows // 2, span), BF16)
    return pl.pallas_call(
        functools.partial(pack_kernel, outer, chunk, wide),
        grid_spec=pltpu.PrefetchScalarGridSpec(
            num_scalar_prefetch=1,
            grid=(steps,),
            in_specs=[pl.BlockSpec((part, width), plain), pl.BlockSpec((part, width), plain)],
            out_specs=[
                pl.BlockSpec((part, span), plain),
                pl.BlockSpec((part, span), plain),
                pl.BlockSpec((part, span), lower),
                pl.BlockSpec((part, span), lower),
            ],
            scratch_shapes=[pltpu.VMEM((4, part, span), BF16)],
        ),
        out_shape=[shape, shape, small, small],
        compiler_params=pltpu.CompilerParams(vmem_limit_bytes=32 << 20),
        cost_estimate=BRIEF,
        name="pack",
    )(info, w_gate, w_up)


def pack_down_kernel(outer, chunk, wide, info_ref, down_ref, out_ref):
    bit = (info_ref[1] >> 1) & 1
    block = down_ref[...]
    fill = jnp.zeros((wide - chunk, block.shape[1]), BF16)
    for b in range(2):

        @pl.when(bit == b)
        def _():
            for xd in range(2):
                for o in range(outer):
                    at = (o * 4 + b * 2 + xd) * chunk
                    piece = jnp.concatenate([block[at : at + chunk], fill], axis=0)
                    to = (xd * outer + o) * wide
                    out_ref[to : to + wide] = piece


def pack_down(info, w_down, outer, chunk, wide):
    rows, width = w_down.shape
    steps = 4
    part = width // steps
    mine = 2 * outer * wide
    return pl.pallas_call(
        functools.partial(pack_down_kernel, outer, chunk, wide),
        grid=(steps,),
        in_specs=[
            pl.BlockSpec(memory_space=pltpu.SMEM),
            pl.BlockSpec((rows, part), lambda i: (0, i)),
        ],
        out_specs=pl.BlockSpec((mine, part), lambda i: (0, i)),
        out_shape=jax.ShapeDtypeStruct((mine, width), BF16),
        compiler_params=pltpu.CompilerParams(vmem_limit_bytes=32 << 20),
        cost_estimate=BRIEF,
        name="pack_down",
    )(info, w_down)


def columns_grad_kernel(rows, mine, info_ref, ha, hb, da, db, send_g, send_u, keep_g, keep_u):
    odd = (info_ref[1] & 1) == 1
    grad = t_dot(ha[...], da[...]) + t_dot(hb[...], db[...])
    count, width = grad.shape
    grad = grad.reshape(count // (2 * rows), 2, rows, width)
    low, upp = grad[:, 0], grad[:, 1]
    send = jnp.where(odd, low, upp).astype(BF16).reshape(count // 2, width)
    keep = jnp.where(odd, upp, low).reshape(count // 2, width)
    send_g[...] = send[:, :mine]
    send_u[...] = send[:, mine:]
    keep_g[...] = keep[:, :mine]
    keep_u[...] = keep[:, mine:]


def columns_grad(info, ha, hb, da, db, rows):
    tokens, width = ha.shape
    mine = da.shape[1] // 2
    part = min(512, width)
    half = pl.BlockSpec((part // 2, mine), lambda i: (i, 0))
    lhs = pl.BlockSpec((tokens, part), lambda i: (0, i))
    rhs = pl.BlockSpec(da.shape, lambda i: (0, 0))
    return pl.pallas_call(
        functools.partial(columns_grad_kernel, rows, mine),
        grid=(width // part,),
        in_specs=[pl.BlockSpec(memory_space=pltpu.SMEM), lhs, lhs, rhs, rhs],
        out_specs=[half] * 4,
        out_shape=[jax.ShapeDtypeStruct((width // 2, mine), BF16)] * 2
        + [jax.ShapeDtypeStruct((width // 2, mine), F32)] * 2,
        compiler_params=pltpu.CompilerParams(vmem_limit_bytes=56 << 20),
        cost_estimate=BRIEF,
        name="columns_grad",
    )(info, ha, hb, da, db)


def rows_grad_kernel(info_ref, ha, hb, da, db, send_ref, keep_ref):
    odd = (info_ref[1] & 1) == 1
    grad = t_dot(ha[...], da[...]) + t_dot(hb[...], db[...])
    half = grad.shape[0] // 2
    low, upp = grad[:half], grad[half:]
    send_ref[...] = jnp.where(odd, low, upp).astype(BF16)
    keep_ref[...] = jnp.where(odd, upp, low)


def rows_grad(info, ha, hb, da, db):
    tokens, mine = ha.shape
    width = da.shape[1]
    part = min(512, width)
    half = pl.BlockSpec((mine // 2, part), lambda i: (0, i))
    lhs = pl.BlockSpec(ha.shape, lambda i: (0, 0))
    rhs = pl.BlockSpec((tokens, part), lambda i: (0, i))
    return pl.pallas_call(
        rows_grad_kernel,
        grid=(width // part,),
        in_specs=[pl.BlockSpec(memory_space=pltpu.SMEM), lhs, lhs, rhs, rhs],
        out_specs=[half] * 2,
        out_shape=[
            jax.ShapeDtypeStruct((mine // 2, width), BF16),
            jax.ShapeDtypeStruct((mine // 2, width), F32),
        ],
        compiler_params=pltpu.CompilerParams(vmem_limit_bytes=48 << 20),
        cost_estimate=BRIEF,
        name="rows_grad",
    )(info, ha, hb, da, db)


def unpack_kernel(
    outer, chunk, wide, info_ref, got_g, got_u, w_gate, w_up, gain, gate_ref, up_ref, dg_ref
):
    g, bit = info_ref[0], (info_ref[1] >> 1) & 1
    total = 0.0
    for got, ref, weight in ((got_g, gate_ref, w_gate), (got_u, up_ref, w_up)):
        parts = []
        for member in range(4):
            pieces = [got[member ^ g, b ^ bit] for b in range(2)]
            for o in range(outer):
                for b in range(2):
                    for xd in range(2):
                        at = (xd * outer + o) * wide
                        parts.append(pieces[b][:, at : at + chunk])
        grad = jnp.concatenate(parts, axis=1).astype(F32)
        ref[...] = grad
        total = total + jnp.sum(grad * weight[...].astype(F32), axis=1, keepdims=True)
    dg_ref[...] = total / gain[...]


def unpack(info, got_g, got_u, w_gate, w_up, gain, outer, chunk, wide):
    rows = got_g.shape[2]
    shape = jax.ShapeDtypeStruct((rows, 16 * outer * chunk), F32)
    vmem = pl.BlockSpec(memory_space=pltpu.VMEM)
    return pl.pallas_call(
        functools.partial(unpack_kernel, outer, chunk, wide),
        in_specs=[pl.BlockSpec(memory_space=pltpu.SMEM)] + [vmem] * 5,
        out_specs=[vmem] * 3,
        out_shape=[shape, shape, jax.ShapeDtypeStruct((rows, 1), F32)],
        compiler_params=pltpu.CompilerParams(vmem_limit_bytes=32 << 20),
        cost_estimate=BRIEF,
        name="unpack",
    )(info, got_g, got_u, w_gate, w_up, gain)


def block_bounds(info_ref, starts_ref, j, reps):
    place = ((info_ref[0] ^ j) * reps + info_ref[1]) * HD
    docs = starts_ref.shape[0]
    first = jnp.int32(0)
    for d in range(docs):
        first = jnp.maximum(first, jnp.where(starts_ref[d] <= place, starts_ref[d], 0))
    position = place + lax.broadcasted_iota(jnp.int32, (4, HD, 1), 1).reshape(4 * HD, 1)
    lowest = jnp.zeros_like(position)
    for d in range(docs):
        lowest = jnp.maximum(lowest, jnp.where(starts_ref[d] <= position, starts_ref[d], 0))
    return place, first, position, lowest


def key_tile(info_ref, slots_ref, kv_ref, tile, reps):
    per = reps // 4
    member = (tile // per) ^ info_ref[0]
    base = 4 * (tile % per)
    piece = jnp.concatenate([kv_ref[slots_ref[base + k], member] for k in range(4)], axis=0)
    return piece[:, :HD], piece[:, HD:]


def head_rows(ref):
    return jnp.concatenate([ref[0, :, h * HD : (h + 1) * HD] for h in range(4)], axis=0)


def attend_kernel(reps, info_ref, slots_ref, starts_ref, q_ref, kv_ref, o_ref, lse_ref):
    j = pl.program_id(0)
    place, first, position, lowest = block_bounds(info_ref, starts_ref, j, reps)
    query = head_rows(q_ref)
    rows = 4 * HD
    scale = HD ** (-0.5)

    def step(tile, carry):
        best, total, accum = carry
        key, value = key_tile(info_ref, slots_ref, kv_ref, tile, reps)
        scores = dot_t(query, key) * scale
        at = tile * 512 + lax.broadcasted_iota(jnp.int32, (1, 512), 1)
        scores = jnp.where((at >= lowest) & (at <= position), scores, NEGATIVE)
        new_best = jnp.maximum(best, jnp.max(scores, axis=1, keepdims=True))
        weights = jnp.exp(scores - new_best)
        factor = jnp.exp(best - new_best)
        total = total * factor + jnp.sum(weights, axis=1, keepdims=True)
        accum = accum * factor + dot(weights.astype(BF16), value)
        return new_best, total, accum

    init = (
        jnp.full((rows, 1), NEGATIVE, F32),
        jnp.zeros((rows, 1), F32),
        jnp.zeros((rows, HD), F32),
    )
    best, total, accum = lax.fori_loop(first // 512, place // 512 + 1, step, init)
    out = accum / total
    for h in range(4):
        o_ref[0, :, h * HD : (h + 1) * HD] = out[h * HD : (h + 1) * HD].astype(BF16)
    lse_ref[0] = best + jnp.log(total)


def attend(info, slots, starts, query, kv):
    reps = kv.shape[0]
    return pl.pallas_call(
        functools.partial(attend_kernel, reps),
        grid=(4,),
        in_specs=[
            pl.BlockSpec(memory_space=pltpu.SMEM),
            pl.BlockSpec(memory_space=pltpu.SMEM),
            pl.BlockSpec(memory_space=pltpu.SMEM),
            pl.BlockSpec((1, HD, 4 * HD), lambda j: (j, 0, 0)),
            pl.BlockSpec(kv.shape, lambda j: (0, 0, 0, 0)),
        ],
        out_specs=[
            pl.BlockSpec((1, HD, 4 * HD), lambda j: (j, 0, 0)),
            pl.BlockSpec((1, 4 * HD, 1), lambda j: (j, 0, 0)),
        ],
        out_shape=[
            jax.ShapeDtypeStruct((4, HD, 4 * HD), BF16),
            jax.ShapeDtypeStruct((4, 4 * HD, 1), F32),
        ],
        compiler_params=pltpu.CompilerParams(vmem_limit_bytes=48 << 20),
        cost_estimate=BRIEF,
        name="attend",
    )(info, slots, starts, query, kv)


def attend_back_kernel(
    reps,
    info_ref,
    slots_ref,
    starts_ref,
    q_ref,
    do_ref,
    o_ref,
    lse_ref,
    kv_ref,
    dq_ref,
    dkv_ref,
    sums,
):
    j = pl.program_id(0)

    @pl.when(j == 0)
    def _():
        sums[...] = jnp.zeros_like(sums)

    place, first, position, lowest = block_bounds(info_ref, starts_ref, j, reps)
    query = head_rows(q_ref)
    d_out = head_rows(do_ref)
    out = head_rows(o_ref)
    lse = lse_ref[0]
    delta = jnp.sum(d_out.astype(F32) * out.astype(F32), axis=1, keepdims=True)
    scale = HD ** (-0.5)
    per = reps // 4

    def step(tile, d_query):
        key, value = key_tile(info_ref, slots_ref, kv_ref, tile, reps)
        scores = dot_t(query, key) * scale
        at = tile * 512 + lax.broadcasted_iota(jnp.int32, (1, 512), 1)
        probs = jnp.where((at >= lowest) & (at <= position), jnp.exp(scores - lse), 0.0)
        d_probs = dot_t(d_out, value)
        d_scores = (probs * (d_probs - delta)).astype(BF16)
        d_query = d_query + dot(d_scores, key)
        d_key = t_dot(d_scores, query) * scale
        d_value = t_dot(probs.astype(BF16), d_out)
        member = (tile // per) ^ info_ref[0]
        both = jnp.concatenate([d_key, d_value], axis=1)
        for k in range(4):
            slot = (4 * (tile % per) + k) ^ info_ref[1]
            sums[slot, member] = sums[slot, member] + both[k * HD : (k + 1) * HD]
        return d_query

    d_query = lax.fori_loop(
        first // 512, place // 512 + 1, step, jnp.zeros((4 * HD, HD), F32)
    )
    d_query = (d_query * scale).astype(BF16)
    for h in range(4):
        dq_ref[0, :, h * HD : (h + 1) * HD] = d_query[h * HD : (h + 1) * HD]

    @pl.when(j == 3)
    def _():
        dkv_ref[...] = sums[...].astype(BF16)


def attend_back(info, slots, starts, query, d_out, out, lse, kv):
    reps = kv.shape[0]
    rows = pl.BlockSpec((1, HD, 4 * HD), lambda j: (j, 0, 0))
    whole = pl.BlockSpec(kv.shape, lambda j: (0, 0, 0, 0))
    return pl.pallas_call(
        functools.partial(attend_back_kernel, reps),
        grid=(4,),
        in_specs=[
            pl.BlockSpec(memory_space=pltpu.SMEM),
            pl.BlockSpec(memory_space=pltpu.SMEM),
            pl.BlockSpec(memory_space=pltpu.SMEM),
            rows,
            rows,
            rows,
            pl.BlockSpec((1, 4 * HD, 1), lambda j: (j, 0, 0)),
            whole,
        ],
        out_specs=[rows, whole],
        out_shape=[
            jax.ShapeDtypeStruct((4, HD, 4 * HD), BF16),
            jax.ShapeDtypeStruct(kv.shape, BF16),
        ],
        scratch_shapes=[pltpu.VMEM(kv.shape, F32)],
        compiler_params=pltpu.CompilerParams(vmem_limit_bytes=60 << 20),
        cost_estimate=BRIEF,
        name="attend_back",
    )(info, slots, starts, query, d_out, out, lse, kv)


def on_device(
    tokens,
    cotangent,
    gain_attn,
    gain_ffn,
    w_query,
    w_out,
    w_gate,
    w_up,
    w_down,
    keys,
    values,
    starts,
):
    reps = lax.axis_size("rep")
    rows, width = tokens.shape
    hidden_all = w_gate.shape[1]
    g = lax.axis_index("grp")
    r = lax.axis_index("rep")
    core, yy, xx, zz = reps, 2 * reps, 1, 2
    high = [1 << k for k in range(2, 16) if (1 << k) < reps]
    outer = reps // 4
    x_bit, z_bit = r & 1, (r >> 1) & 1
    share = width // 4
    out_rows = width // (4 * reps)
    chunk = hidden_all // (4 * reps)
    wide = -(-(2 * outer * chunk) // 256) * 256 // (2 * outer)
    mine = 2 * outer * wide
    info = jnp.stack([g, r]).astype(jnp.int32)

    kv_parts = [
        jnp.concatenate(
            [
                lax.dynamic_slice_in_dim(keys, (g ^ j) * HD, HD, 1),
                lax.dynamic_slice_in_dim(values, (g ^ j) * HD, HD, 1),
            ],
            axis=1,
        )
        for j in range(4)
    ]
    kv_own = jnp.stack(exchange_four(kv_parts, core, yy))

    x_full = tokens.astype(F32)
    inv_one = lax.rsqrt(jnp.mean(x_full * x_full, axis=1, keepdims=True) + EPSILON)
    normed_one = x_full * inv_one
    h_one = (normed_one * gain_attn).astype(BF16)

    h_y = swap(h_one, yy)
    wq_half = share // 2
    wq_y = jnp.stack(
        [
            lax.dynamic_slice(w_query, (x_bit * wq_half, (g ^ j) * share), (wq_half, share))
            for j in (2, 3)
        ]
    )
    stay, to_core, to_y, relay = pack(info, w_gate, w_up, outer, chunk, wide)
    wd = pack_down(info, w_down, outer, chunk, wide)
    dy_y = cotangent
    if reps == 8:
        pairs = ring_of(reps)
        wq_y = swap(after(wq_y, kv_own), yy)
        one = lax.ppermute(kv_own, BOTH, pairs)
        one, h_y = together(one, h_y)
        two = lax.ppermute(one, BOTH, pairs)
        two, wq_y, stay, wd = together(two, wq_y, stay, wd)
        wq_x = swap(wq_y, xx)
        dy_y = swap(after(dy_y, two), yy)
        three = lax.ppermute(two, BOTH, pairs)
        three, wq_x, dy_y = together(three, wq_x, dy_y)
        relay = swap(after(relay, two), yy)
        kv = jnp.stack([part for v in (kv_own, one, two, three) for part in (v, swap(v, xx))])
        slots = ring_slots(r, reps)
        kv, relay = together(kv, relay)
    else:
        wq_y, dy_y, relay = swap(wq_y, yy), swap(dy_y, yy), swap(relay, yy)
        wq_x = swap(wq_y, xx)
        kv = lax.all_gather(kv_own, "rep", axis=0, tiled=False)
        slots = jnp.arange(reps, dtype=jnp.int32)

    h_group = jnp.stack([h_one, swap(h_one, core), h_y, swap(h_y, core)])
    h_group = h_group.reshape(4 * rows, width)
    upper_half = x_bit == 1
    wq_y = jnp.concatenate(
        [jnp.where(upper_half, wq_x, wq_y), jnp.where(upper_half, wq_y, wq_x)], axis=1
    )
    wq_parts = [
        lax.dynamic_slice_in_dim(w_query, g * share, share, 1),
        swap(lax.dynamic_slice_in_dim(w_query, (g ^ 1) * share, share, 1), core),
        wq_y[0],
        swap(wq_y[1], core),
    ]
    wq_cols = jnp.concatenate(absolute(wq_parts, g), axis=0)
    query = dot(h_group, wq_cols).astype(BF16).reshape(4, rows, share)

    from_y = swap(after(to_y, relay), yy)
    relay_x = swap(relay, xx)
    attn, lse = attend(info, slots, starts, query, kv)
    attn, lse, from_y = together(attn, lse, from_y)
    attn_rows = attn.reshape(4 * rows, share)
    branch = scatter_four_core(dot(attn_rows, w_out).reshape(4, rows, width), core)
    from_branch = swap(branch[1].astype(BF16), yy)
    from_branch, relay_x = together(from_branch, relay_x)
    from_y_x = swap(from_y, xx)
    dy_near = jnp.stack([cotangent, dy_y])
    dy_far = swap(after(dy_near, attn), zz)
    resid = x_full + branch[0] + from_branch.astype(F32)
    inv_two = lax.rsqrt(jnp.mean(resid * resid, axis=1, keepdims=True) + EPSILON)
    normed_two = resid * inv_two
    h_two = (normed_two * gain_ffn).astype(BF16)

    h_y, h_z = swap(h_two, yy), swap(h_two, zz)
    h_y, h_z, dy_far = together(h_y, h_z, dy_far)
    low, upp = swap(h_y[: rows // 2], zz), swap(h_z[rows // 2 :], yy)
    low, upp, from_y_x = together(low, upp, from_y_x)
    h_a = jnp.concatenate([h_two, h_y, h_z, low, upp])
    h_b = swap(h_a, core)
    dy_a = jnp.stack([dy_near, dy_far]).reshape(4 * rows, width)
    dy_b = swap(dy_a, core)
    diagonal, diagonal_x = swap(relay, core), swap(relay_x, core)
    w_gu = jnp.concatenate(
        absolute(
            [
                stay,
                swap(to_core, core),
                jnp.concatenate(
                    [
                        jnp.where(upper_half, from_y_x, from_y),
                        jnp.where(upper_half, from_y, from_y_x),
                    ]
                ),
                jnp.concatenate(
                    [
                        jnp.where(upper_half, diagonal_x, diagonal),
                        jnp.where(upper_half, diagonal, diagonal_x),
                    ]
                ),
            ],
            g,
        ),
        axis=0,
    )

    def feed_forward(h, dy):
        both = dot(h, w_gu)
        gate, upper = both[:, :mine], both[:, mine:]
        d_hidden = dot_t(dy, wd)
        sigma = jax.nn.sigmoid(gate)
        swish = gate * sigma
        hidden = (swish * upper).astype(BF16)
        d_gate = (d_hidden * upper * sigma * (1.0 + gate * (1.0 - sigma))).astype(BF16)
        d_upper = (d_hidden * swish).astype(BF16)
        return hidden, jnp.concatenate([d_gate, d_upper], axis=1)

    hidden_a, d_both_a = feed_forward(h_a, dy_a)
    hidden_b, d_both_b = feed_forward(h_b, dy_b)
    from_core = swap(dot_t(d_both_b, w_gu).astype(BF16), core)
    d_h_parts = dot_t(d_both_a, w_gu) + from_core.astype(F32)
    d_h_parts = d_h_parts.reshape(4, rows, width)

    send_d, keep_d = rows_grad(info, hidden_a, hidden_b, dy_a, dy_b)
    send_g, send_u, keep_g, keep_u = columns_grad(info, h_a, h_b, d_both_a, d_both_b, out_rows)
    got_d = swap(send_d, xx)
    to_z, to_y = corner_step(d_h_parts, yy, zz)
    to_z, to_y, send_d, keep_d = together(to_z, to_y, send_d, keep_d)
    from_z, from_y = side_step(d_h_parts, to_z, to_y, yy, zz)
    from_z, from_y, send_g, send_u, got_d = together(from_z, from_y, send_g, send_u, got_d)
    got_g = swap(send_g, xx)
    d_h_two = d_h_parts[0] + from_z.astype(F32) + from_y.astype(F32)
    scaled_two = d_h_two * gain_ffn
    d_resid = cotangent.astype(F32) + inv_two * (
        scaled_two - normed_two * jnp.mean(scaled_two * normed_two, axis=1, keepdims=True)
    )
    da_own = d_resid.astype(BF16)
    da_y, da_c = swap(da_own, yy), swap(da_own, core)
    out_core = swap(dot(hidden_b, wd).astype(BF16), core)
    da_y, da_c, out_core = together(da_y, da_c, out_core)
    d_group = jnp.stack([da_own, da_c, da_y, swap(da_y, core)]).reshape(4 * rows, width)
    d_group, got_g = together(d_group, got_g)
    got_u = swap(send_u, xx)
    out_parts = (dot(hidden_a, wd) + out_core.astype(F32)).reshape(4, rows, width)
    out_z, out_y = corner_step(after(out_parts, d_group), yy, zz)

    d_attn = dot_t(d_group, w_out).astype(BF16).reshape(4, rows, share)
    grad_d = (keep_d + got_d.astype(F32)).reshape(outer, wide, width)
    d_query, d_kv = attend_back(info, slots, starts, query, d_attn, attn, lse, kv)
    d_query, d_kv, got_u, out_z, out_y = together(d_query, d_kv, got_u, out_z, out_y)
    d_query = d_query.reshape(4 * rows, share)
    out_z, out_y = side_step(out_parts, out_z, out_y, yy, zz)
    grad_d = scatter_high(grad_d, r, high, 0)

    d_h_one = scatter_four_core(dot_t(d_query, wq_cols).reshape(4, rows, width), core)
    from_h = swap(d_h_one[1].astype(BF16), yy)
    from_h, out_z, out_y, grad_d = together(from_h, out_z, out_y, grad_d)
    d_wdown = grad_d[:chunk]
    output = (resid + out_parts[0] + out_z.astype(F32) + out_y.astype(F32)).astype(BF16)
    d_h_one = d_h_one[0] + from_h.astype(F32)
    scaled_one = d_h_one * gain_attn
    d_tokens = (
        d_resid
        + inv_one
        * (scaled_one - normed_one * jnp.mean(scaled_one * normed_one, axis=1, keepdims=True))
    ).astype(BF16)

    def on(got, keep):
        grad = (keep + got.astype(F32)).reshape(4, outer, 2, out_rows, mine)
        grad = scatter_high(grad, r, high, 1).astype(BF16)
        other = swap(pick(grad, 1 - z_bit, 1), zz)
        grad = jnp.stack([pick(grad, z_bit, 1), other])
        return jnp.stack(exchange_four([pick(grad, g ^ j, 1) for j in range(4)], core, yy))

    grad_g = on(got_g, keep_g)
    grad_u = on(got_u, keep_u)
    gate_rows = lax.dynamic_slice_in_dim(w_gate, r * out_rows, out_rows, 0)
    up_rows = lax.dynamic_slice_in_dim(w_up, r * out_rows, out_rows, 0)
    gain_at = (g * reps + r) * out_rows
    gain_rows = lax.dynamic_slice_in_dim(gain_ffn, gain_at, out_rows, 0)
    d_wgate, d_wup, d_gain_two = unpack(
        info, grad_g, grad_u, gate_rows, up_rows, gain_rows[:, None], outer, chunk, wide
    )

    d_wout = t_dot(attn_rows, d_group).reshape(reps, out_rows, width)
    d_wout = scatter_rep(d_wout, r, high)
    d_kv = d_kv.reshape((outer, 2, 2) + d_kv.shape[1:])
    d_kv = d_kv[:, 0].astype(F32) + swap(d_kv[:, 1], zz).astype(F32)
    d_kv = d_kv[:, 0] + swap(d_kv[:, 1].astype(BF16), xx).astype(F32)
    for mask in reversed(high):
        d_kv = d_kv.reshape((2, d_kv.shape[0] // 2) + d_kv.shape[1:])
        d_kv = d_kv[0] + swap(d_kv[1].astype(BF16), mask).astype(F32)
    d_kv = d_kv[0].astype(BF16)
    d_kv = absolute(exchange_four([d_kv[j] for j in range(4)], core, yy), g)
    d_keys = jnp.concatenate([piece[:, :HD] for piece in d_kv], axis=1)
    d_values = jnp.concatenate([piece[:, HD:] for piece in d_kv], axis=1)
    d_wq = t_dot(h_group, d_query).reshape(4, reps, out_rows, share)
    d_wq = scatter_rep(jnp.swapaxes(d_wq, 0, 1), r, high).astype(BF16)
    d_wq = absolute(exchange_four([pick(d_wq, g ^ j, 0) for j in range(4)], core, yy), g)
    d_wquery = jnp.concatenate(d_wq, axis=1).astype(F32)
    query_rows = lax.dynamic_slice_in_dim(w_query, r * out_rows, out_rows, 0)
    gain_rows = lax.dynamic_slice_in_dim(gain_attn, gain_at, out_rows, 0)
    d_gain_one = jnp.sum(d_wquery * query_rows.astype(F32), axis=1) / gain_rows
    return (
        output,
        d_tokens,
        d_gain_one,
        d_gain_two[:, 0],
        d_wquery,
        d_wout,
        d_wgate,
        d_wup,
        d_wdown,
        d_keys,
        d_values,
    )


def solution(mesh):
    spread = P(BOTH, None)
    member = P("grp", None)
    in_specs = (
        spread,
        spread,
        P(),
        P(),
        member,
        member,
        member,
        member,
        member,
        spread,
        spread,
        P(),
    )
    out_specs = (
        spread,
        spread,
        P(BOTH),
        P(BOTH),
        spread,
        spread,
        spread,
        spread,
        spread,
        spread,
        spread,
    )
    return jax.shard_map(
        on_device, mesh=mesh, in_specs=in_specs, out_specs=out_specs, check_vma=False
    )
```

```python
import functools

import jax
import jax.numpy as jnp
from jax import lax
from jax.experimental import pallas as pl
from jax.experimental.pallas import tpu as pltpu
from jax.sharding import PartitionSpec as P

HD = 128
EPSILON = 1e-06
NEGATIVE = -1e30
F32 = jnp.float32
BF16 = jnp.bfloat16
BOTH = ("grp", "rep")
BRIEF = pl.CostEstimate(flops=1, transcendentals=0, bytes_accessed=1)


def swap(value, mask):
    count = lax.axis_size(BOTH)
    return lax.ppermute(value, BOTH, [(i, i ^ mask) for i in range(count)])


def after(value, *earlier):
    return lax.optimization_barrier((value,) + earlier)[0]


def together(*values):
    return lax.optimization_barrier(values)


def dot(a, b):
    return jnp.dot(a, b, preferred_element_type=F32)


def dot_t(a, b):
    return lax.dot_general(a, b, (((1,), (1,)), ((), ())), preferred_element_type=F32)


def t_dot(a, b):
    return lax.dot_general(a, b, (((0,), (0,)), ((), ())), preferred_element_type=F32)


def pick(value, index, axis):
    return lax.dynamic_index_in_dim(value, index, axis, keepdims=False)


def scatter_four_core(parts, core):
    parts = parts.reshape((2, 2) + parts.shape[1:])
    got = swap(parts[:, 1].astype(BF16), core)
    return parts[:, 0] + got.astype(F32)


def side_step(parts, to_z, to_y, rows, yy, zz):
    half = rows // 2
    for_z = [parts[2 * rows : 2 * rows + half] + to_z.astype(F32), parts[2 * rows + half :]]
    for_y = [parts[rows : rows + half], parts[rows + half : 2 * rows] + to_y.astype(F32)]
    for_z, for_y = jnp.concatenate(for_z), jnp.concatenate(for_y)
    return swap(for_z.astype(BF16), zz), swap(for_y.astype(BF16), yy)


def exchange_four(pieces, core, yy):
    from_y = swap(jnp.stack([pieces[2], pieces[3]]), yy)
    from_c = swap(pieces[1], core)
    return [pieces[0], from_c, from_y[0], swap(from_y[1], core)]


def absolute(pieces, g):
    odd, upper = (g & 1) == 1, (g >> 1) == 1
    a = jnp.where(odd, pieces[1], pieces[0])
    b = jnp.where(odd, pieces[0], pieces[1])
    c = jnp.where(odd, pieces[3], pieces[2])
    d = jnp.where(odd, pieces[2], pieces[3])
    return [
        jnp.where(upper, c, a),
        jnp.where(upper, d, b),
        jnp.where(upper, a, c),
        jnp.where(upper, b, d),
    ]


def part(value, bit, mask, axis):
    return pick(value, bit, axis).astype(F32), swap(pick(value, 1 - bit, axis).astype(BF16), mask)


def high_part(value, r, mask, axis):
    shape = value.shape
    value = value.reshape(shape[:axis] + (2, shape[axis] // 2) + shape[axis + 1 :])
    return part(value, (r & mask) // mask, mask, axis)


def high_rest(kept, got, r, high, axis):
    value = kept + got.astype(F32)
    for mask in reversed(high[:-1]):
        kept, got = high_part(value, r, mask, axis)
        value = kept + got.astype(F32)
    return jnp.squeeze(value, axis)


def ring_of(reps):
    ring = (0, 1, 3, 2)
    pairs = []
    for member in range(4):
        for k in range(4):
            for x in range(2):
                base = member * reps + x
                pairs.append((base + 2 * ring[k], base + 2 * ring[(k + 1) % 4]))
    return pairs


def ring_slots(r, reps):
    order = jnp.array((0, 1, 3, 2), jnp.int32)
    other = jnp.arange(reps, dtype=jnp.int32)
    steps = (order[r >> 1] - order[other >> 1]) & 3
    return 2 * steps + ((other ^ r) & 1)


def pack_kernel(
    outer, chunk, wide, info_ref, gate_ref, up_ref, stay_ref, core_ref, y_ref, relay_ref, held
):
    step = pl.program_id(0)
    g, bit, x = info_ref[0], (info_ref[1] >> 1) & 1, info_ref[1] & 1
    rows = gate_ref.shape[0]
    quarter = outer * 4 * chunk
    fill = jnp.zeros((rows, wide - chunk), BF16)

    for b in range(2):

        @pl.when(bit == b)
        def _():
            for which, ref in enumerate((gate_ref, up_ref)):
                block = ref[...]
                for member in range(4):
                    parts = []
                    for xd in range(2):
                        for o in range(outer):
                            at = member * quarter + (o * 4 + b * 2 + xd) * chunk
                            parts += [block[:, at : at + chunk], fill]
                    span = 2 * outer * wide
                    held[member ^ g, :, which * span : (which + 1) * span] = jnp.concatenate(
                        parts, axis=1
                    )

    stay_ref[...] = held[0]
    core_ref[...] = held[1]

    @pl.when(step // (pl.num_programs(0) // 2) == x)
    def _():
        y_ref[...] = held[2]
        relay_ref[...] = held[3]


def pack(info, w_gate, w_up, outer, chunk, wide):
    rows, width = w_gate.shape
    span = 4 * outer * wide
    steps = 8
    part = rows // steps

    def lower(i, info):
        return jnp.clip(i - (info[1] & 1) * (steps // 2), 0, steps // 2 - 1), 0

    def plain(i, info):
        return i, 0

    shape = jax.ShapeDtypeStruct((rows, span), BF16)
    small = jax.ShapeDtypeStruct((rows // 2, span), BF16)
    return pl.pallas_call(
        functools.partial(pack_kernel, outer, chunk, wide),
        grid_spec=pltpu.PrefetchScalarGridSpec(
            num_scalar_prefetch=1,
            grid=(steps,),
            in_specs=[pl.BlockSpec((part, width), plain), pl.BlockSpec((part, width), plain)],
            out_specs=[
                pl.BlockSpec((part, span), plain),
                pl.BlockSpec((part, span), plain),
                pl.BlockSpec((part, span), lower),
                pl.BlockSpec((part, span), lower),
            ],
            scratch_shapes=[pltpu.VMEM((4, part, span), BF16)],
        ),
        out_shape=[shape, shape, small, small],
        compiler_params=pltpu.CompilerParams(vmem_limit_bytes=32 << 20),
        cost_estimate=BRIEF,
        name="pack",
    )(info, w_gate, w_up)


def pack_down_kernel(outer, chunk, wide, info_ref, down_ref, out_ref):
    bit = (info_ref[1] >> 1) & 1
    block = down_ref[...]
    fill = jnp.zeros((wide - chunk, block.shape[1]), BF16)
    for b in range(2):

        @pl.when(bit == b)
        def _():
            for xd in range(2):
                for o in range(outer):
                    at = (o * 4 + b * 2 + xd) * chunk
                    piece = jnp.concatenate([block[at : at + chunk], fill], axis=0)
                    to = (xd * outer + o) * wide
                    out_ref[to : to + wide] = piece


def pack_down(info, w_down, outer, chunk, wide):
    rows, width = w_down.shape
    steps = 4
    part = width // steps
    mine = 2 * outer * wide
    return pl.pallas_call(
        functools.partial(pack_down_kernel, outer, chunk, wide),
        grid=(steps,),
        in_specs=[
            pl.BlockSpec(memory_space=pltpu.SMEM),
            pl.BlockSpec((rows, part), lambda i: (0, i)),
        ],
        out_specs=pl.BlockSpec((mine, part), lambda i: (0, i)),
        out_shape=jax.ShapeDtypeStruct((mine, width), BF16),
        compiler_params=pltpu.CompilerParams(vmem_limit_bytes=32 << 20),
        cost_estimate=BRIEF,
        name="pack_down",
    )(info, w_down)


def feed_forward_kernel(h_ref, dy_ref, gate_ref, up_ref, down_ref, hid_ref, d_gate_ref, d_up_ref):
    h = h_ref[...]
    gate = dot(h, gate_ref[...])
    upper = dot(h, up_ref[...])
    d_hidden = dot_t(dy_ref[...], down_ref[...])
    sigma = 1.0 / (1.0 + jnp.exp(-gate))
    swish = gate * sigma
    hid_ref[...] = (swish * upper).astype(BF16)
    d_up_ref[...] = (d_hidden * swish).astype(BF16)
    d_gate_ref[...] = (d_hidden * upper * (sigma + swish * (1.0 - sigma))).astype(BF16)


def feed_forward(h, dy, w_gu, wd):
    tokens, width = h.shape
    mine = wd.shape[0]
    piece = 256
    steps = mine // piece
    whole = pl.BlockSpec((tokens, width), lambda j: (0, 0))
    out = pl.BlockSpec((tokens, piece), lambda j: (0, j))
    return pl.pallas_call(
        feed_forward_kernel,
        grid=(steps,),
        in_specs=[
            whole,
            whole,
            pl.BlockSpec((width, piece), lambda j: (0, j)),
            pl.BlockSpec((width, piece), lambda j: (0, j + steps)),
            pl.BlockSpec((piece, width), lambda j: (j, 0)),
        ],
        out_specs=[out] * 3,
        out_shape=[jax.ShapeDtypeStruct((tokens, mine), BF16)] * 3,
        compiler_params=pltpu.CompilerParams(vmem_limit_bytes=48 << 20),
        name="feed_forward",
    )(h, dy, w_gu, w_gu, wd)


def inputs_grad_kernel(mine, d_gate_ref, d_up_ref, w_ref, out_ref):
    w = w_ref[...]
    out = dot_t(d_gate_ref[...], w[:, :mine]) + dot_t(d_up_ref[...], w[:, mine:])
    out_ref[...] = out.astype(BF16)


def inputs_grad_sum_kernel(
    mine, rows, d_gate_ref, d_up_ref, w_ref, other_ref, parts_ref, low_ref, upp_ref
):
    w = w_ref[...]
    out = dot_t(d_gate_ref[...], w[:, :mine]) + dot_t(d_up_ref[...], w[:, mine:])
    out = out + other_ref[...].astype(F32)
    parts_ref[...] = out[: 3 * rows]
    low_ref[...] = out[3 * rows : 3 * rows + rows // 2].astype(BF16)
    upp_ref[...] = out[3 * rows + rows // 2 :].astype(BF16)


def inputs_grad(d_gate, d_up, w_gu, other=None):
    tokens, mine = d_gate.shape
    width = w_gu.shape[0]
    piece = min(512, width)
    rows = tokens // 4
    lhs = pl.BlockSpec((tokens, mine), lambda j: (0, 0))
    in_specs = [lhs, lhs, pl.BlockSpec((piece, 2 * mine), lambda j: (j, 0))]
    out = pl.BlockSpec((tokens, piece), lambda j: (0, j))
    params = pltpu.CompilerParams(vmem_limit_bytes=48 << 20)
    if other is None:
        return pl.pallas_call(
            functools.partial(inputs_grad_kernel, mine),
            grid=(width // piece,),
            in_specs=in_specs,
            out_specs=out,
            out_shape=jax.ShapeDtypeStruct((tokens, width), BF16),
            compiler_params=params,
            name="inputs_grad",
        )(d_gate, d_up, w_gu)
    half = pl.BlockSpec((rows // 2, piece), lambda j: (0, j))
    return pl.pallas_call(
        functools.partial(inputs_grad_sum_kernel, mine, rows),
        grid=(width // piece,),
        in_specs=in_specs + [out],
        out_specs=[pl.BlockSpec((3 * rows, piece), lambda j: (0, j)), half, half],
        out_shape=[jax.ShapeDtypeStruct((3 * rows, width), F32)]
        + [jax.ShapeDtypeStruct((rows // 2, width), BF16)] * 2,
        compiler_params=params,
        name="inputs_grad_sum",
    )(d_gate, d_up, w_gu, other)


def columns_grad_kernel(
    rows, info_ref, ha, hb, ga, gb, ua, ub, send_g, send_u, keep_g, keep_u
):
    odd = (info_ref[1] & 1) == 1
    for da, db, send, keep in ((ga, gb, send_g, keep_g), (ua, ub, send_u, keep_u)):
        grad = t_dot(ha[...], da[...]) + t_dot(hb[...], db[...])
        count, width = grad.shape
        grad = grad.reshape(count // (2 * rows), 2, rows, width)
        low, upp = grad[:, 0], grad[:, 1]
        send[...] = jnp.where(odd, low, upp).astype(BF16).reshape(count // 2, width)
        keep[...] = jnp.where(odd, upp, low).reshape(count // 2, width)


def columns_grad(info, ha, hb, ga, gb, ua, ub, rows):
    tokens, width = ha.shape
    mine = ga.shape[1]
    part = min(512, width)
    half = pl.BlockSpec((part // 2, mine), lambda i: (i, 0))
    lhs = pl.BlockSpec((tokens, part), lambda i: (0, i))
    rhs = pl.BlockSpec(ga.shape, lambda i: (0, 0))
    return pl.pallas_call(
        functools.partial(columns_grad_kernel, rows),
        grid=(width // part,),
        in_specs=[pl.BlockSpec(memory_space=pltpu.SMEM), lhs, lhs, rhs, rhs, rhs, rhs],
        out_specs=[half] * 4,
        out_shape=[jax.ShapeDtypeStruct((width // 2, mine), BF16)] * 2
        + [jax.ShapeDtypeStruct((width // 2, mine), F32)] * 2,
        compiler_params=pltpu.CompilerParams(vmem_limit_bytes=56 << 20),
        name="columns_grad",
    )(info, ha, hb, ga, gb, ua, ub)


def rows_grad_kernel(info_ref, ha, hb, da, db, send_ref, keep_ref):
    odd = (info_ref[1] & 1) == 1
    grad = t_dot(ha[...], da[...]) + t_dot(hb[...], db[...])
    half = grad.shape[0] // 2
    low, upp = grad[:half], grad[half:]
    send_ref[...] = jnp.where(odd, low, upp).astype(BF16)
    keep_ref[...] = jnp.where(odd, upp, low)


def rows_grad(info, ha, hb, da, db):
    tokens, mine = ha.shape
    width = da.shape[1]
    part = min(512, width)
    half = pl.BlockSpec((mine // 2, part), lambda i: (0, i))
    lhs = pl.BlockSpec(ha.shape, lambda i: (0, 0))
    rhs = pl.BlockSpec((tokens, part), lambda i: (0, i))
    return pl.pallas_call(
        rows_grad_kernel,
        grid=(width // part,),
        in_specs=[pl.BlockSpec(memory_space=pltpu.SMEM), lhs, lhs, rhs, rhs],
        out_specs=[half] * 2,
        out_shape=[
            jax.ShapeDtypeStruct((mine // 2, width), BF16),
            jax.ShapeDtypeStruct((mine // 2, width), F32),
        ],
        compiler_params=pltpu.CompilerParams(vmem_limit_bytes=48 << 20),
        cost_estimate=BRIEF,
        name="rows_grad",
    )(info, ha, hb, da, db)


def unpack_kernel(
    outer, chunk, wide, info_ref, got_g, got_u, w_gate, w_up, gain, gate_ref, up_ref, dg_ref
):
    g, bit = info_ref[0], (info_ref[1] >> 1) & 1
    total = 0.0
    for got, ref, weight in ((got_g, gate_ref, w_gate), (got_u, up_ref, w_up)):
        parts = []
        for member in range(4):
            pieces = [got[member ^ g, b ^ bit] for b in range(2)]
            for o in range(outer):
                for b in range(2):
                    for xd in range(2):
                        at = (xd * outer + o) * wide
                        parts.append(pieces[b][:, at : at + chunk])
        grad = jnp.concatenate(parts, axis=1).astype(F32)
        ref[...] = grad
        total = total + jnp.sum(grad * weight[...].astype(F32), axis=1, keepdims=True)
    dg_ref[...] = total / gain[...]


def unpack(info, got_g, got_u, w_gate, w_up, gain, outer, chunk, wide):
    rows = got_g.shape[2]
    shape = jax.ShapeDtypeStruct((rows, 16 * outer * chunk), F32)
    vmem = pl.BlockSpec(memory_space=pltpu.VMEM)
    return pl.pallas_call(
        functools.partial(unpack_kernel, outer, chunk, wide),
        in_specs=[pl.BlockSpec(memory_space=pltpu.SMEM)] + [vmem] * 5,
        out_specs=[vmem] * 3,
        out_shape=[shape, shape, jax.ShapeDtypeStruct((rows, 1), F32)],
        compiler_params=pltpu.CompilerParams(vmem_limit_bytes=32 << 20),
        cost_estimate=BRIEF,
        name="unpack",
    )(info, got_g, got_u, w_gate, w_up, gain)


def block_bounds(info_ref, starts_ref, j, reps):
    place = ((info_ref[0] ^ j) * reps + info_ref[1]) * HD
    docs = starts_ref.shape[0]
    first = jnp.int32(0)
    for d in range(docs):
        first = jnp.maximum(first, jnp.where(starts_ref[d] <= place, starts_ref[d], 0))
    position = place + lax.broadcasted_iota(jnp.int32, (4, HD, 1), 1).reshape(4 * HD, 1)
    lowest = jnp.zeros_like(position)
    for d in range(docs):
        lowest = jnp.maximum(lowest, jnp.where(starts_ref[d] <= position, starts_ref[d], 0))
    return place, first, position, lowest


def key_tile(info_ref, slots_ref, kv_ref, tile, reps):
    per = reps // 4
    member = (tile // per) ^ info_ref[0]
    base = 4 * (tile % per)
    piece = jnp.concatenate([kv_ref[slots_ref[base + k], member] for k in range(4)], axis=0)
    return piece[:, :HD], piece[:, HD:]


def head_rows(ref):
    return jnp.concatenate([ref[0, :, h * HD : (h + 1) * HD] for h in range(4)], axis=0)


def attend_kernel(reps, info_ref, slots_ref, starts_ref, q_ref, kv_ref, o_ref, lse_ref):
    j = pl.program_id(0)
    place, first, position, lowest = block_bounds(info_ref, starts_ref, j, reps)
    query = head_rows(q_ref)
    rows = 4 * HD
    scale = HD ** (-0.5)

    def step(tile, carry):
        best, total, accum = carry
        key, value = key_tile(info_ref, slots_ref, kv_ref, tile, reps)
        scores = dot_t(query, key) * scale
        at = tile * 512 + lax.broadcasted_iota(jnp.int32, (1, 512), 1)
        scores = jnp.where((at >= lowest) & (at <= position), scores, NEGATIVE)
        new_best = jnp.maximum(best, jnp.max(scores, axis=1, keepdims=True))
        weights = jnp.exp(scores - new_best)
        factor = jnp.exp(best - new_best)
        total = total * factor + jnp.sum(weights, axis=1, keepdims=True)
        accum = accum * factor + dot(weights.astype(BF16), value)
        return new_best, total, accum

    init = (
        jnp.full((rows, 1), NEGATIVE, F32),
        jnp.zeros((rows, 1), F32),
        jnp.zeros((rows, HD), F32),
    )
    best, total, accum = lax.fori_loop(first // 512, place // 512 + 1, step, init)
    out = accum / total
    for h in range(4):
        o_ref[0, :, h * HD : (h + 1) * HD] = out[h * HD : (h + 1) * HD].astype(BF16)
    lse_ref[0] = best + jnp.log(total)


def attend(info, slots, starts, query, kv):
    reps = kv.shape[0]
    return pl.pallas_call(
        functools.partial(attend_kernel, reps),
        grid=(4,),
        in_specs=[
            pl.BlockSpec(memory_space=pltpu.SMEM),
            pl.BlockSpec(memory_space=pltpu.SMEM),
            pl.BlockSpec(memory_space=pltpu.SMEM),
            pl.BlockSpec((1, HD, 4 * HD), lambda j: (j, 0, 0)),
            pl.BlockSpec(kv.shape, lambda j: (0, 0, 0, 0)),
        ],
        out_specs=[
            pl.BlockSpec((1, HD, 4 * HD), lambda j: (j, 0, 0)),
            pl.BlockSpec((1, 4 * HD, 1), lambda j: (j, 0, 0)),
        ],
        out_shape=[
            jax.ShapeDtypeStruct((4, HD, 4 * HD), BF16),
            jax.ShapeDtypeStruct((4, 4 * HD, 1), F32),
        ],
        compiler_params=pltpu.CompilerParams(vmem_limit_bytes=48 << 20),
        cost_estimate=BRIEF,
        name="attend",
    )(info, slots, starts, query, kv)


def attend_back_kernel(
    reps,
    info_ref,
    slots_ref,
    starts_ref,
    q_ref,
    do_ref,
    o_ref,
    lse_ref,
    kv_ref,
    dq_ref,
    keep_ref,
    send_ref,
    sums,
):
    j = pl.program_id(0)

    @pl.when(j == 0)
    def _():
        sums[...] = jnp.zeros_like(sums)

    place, first, position, lowest = block_bounds(info_ref, starts_ref, j, reps)
    query = head_rows(q_ref)
    d_out = head_rows(do_ref)
    out = head_rows(o_ref)
    lse = lse_ref[0]
    delta = jnp.sum(d_out.astype(F32) * out.astype(F32), axis=1, keepdims=True)
    scale = HD ** (-0.5)
    per = reps // 4

    def step(tile, d_query):
        key, value = key_tile(info_ref, slots_ref, kv_ref, tile, reps)
        scores = dot_t(query, key) * scale
        at = tile * 512 + lax.broadcasted_iota(jnp.int32, (1, 512), 1)
        probs = jnp.where((at >= lowest) & (at <= position), jnp.exp(scores - lse), 0.0)
        d_probs = dot_t(d_out, value)
        d_scores = (probs * (d_probs - delta)).astype(BF16)
        d_query = d_query + dot(d_scores, key)
        d_key = t_dot(d_scores, query) * scale
        d_value = t_dot(probs.astype(BF16), d_out)
        member = (tile // per) ^ info_ref[0]
        both = jnp.concatenate([d_key, d_value], axis=1)
        for k in range(4):
            slot = (4 * (tile % per) + k) ^ info_ref[1]
            sums[slot, member] = sums[slot, member] + both[k * HD : (k + 1) * HD]
        return d_query

    d_query = lax.fori_loop(
        first // 512, place // 512 + 1, step, jnp.zeros((4 * HD, HD), F32)
    )
    d_query = (d_query * scale).astype(BF16)
    for h in range(4):
        dq_ref[0, :, h * HD : (h + 1) * HD] = d_query[h * HD : (h + 1) * HD]

    @pl.when(j == 3)
    def _():
        for slot in range(reps // 2):
            keep_ref[slot] = sums[2 * slot].astype(BF16)
            send_ref[slot] = sums[2 * slot + 1].astype(BF16)


def attend_back(info, slots, starts, query, d_out, out, lse, kv):
    reps = kv.shape[0]
    rows = pl.BlockSpec((1, HD, 4 * HD), lambda j: (j, 0, 0))
    whole = pl.BlockSpec(kv.shape, lambda j: (0, 0, 0, 0))
    half = pl.BlockSpec((reps // 2,) + kv.shape[1:], lambda j: (0, 0, 0, 0))
    return pl.pallas_call(
        functools.partial(attend_back_kernel, reps),
        grid=(4,),
        in_specs=[
            pl.BlockSpec(memory_space=pltpu.SMEM),
            pl.BlockSpec(memory_space=pltpu.SMEM),
            pl.BlockSpec(memory_space=pltpu.SMEM),
            rows,
            rows,
            rows,
            pl.BlockSpec((1, 4 * HD, 1), lambda j: (j, 0, 0)),
            whole,
        ],
        out_specs=[rows, half, half],
        out_shape=[jax.ShapeDtypeStruct((4, HD, 4 * HD), BF16)]
        + [jax.ShapeDtypeStruct((reps // 2,) + kv.shape[1:], BF16)] * 2,
        scratch_shapes=[pltpu.VMEM(kv.shape, F32)],
        compiler_params=pltpu.CompilerParams(vmem_limit_bytes=60 << 20),
        cost_estimate=BRIEF,
        name="attend_back",
    )(info, slots, starts, query, d_out, out, lse, kv)


def on_device(
    tokens,
    cotangent,
    gain_attn,
    gain_ffn,
    w_query,
    w_out,
    w_gate,
    w_up,
    w_down,
    keys,
    values,
    starts,
):
    reps = lax.axis_size("rep")
    rows, width = tokens.shape
    hidden_all = w_gate.shape[1]
    g = lax.axis_index("grp")
    r = lax.axis_index("rep")
    core, yy, xx, zz = reps, 2 * reps, 1, 2
    high = [1 << k for k in range(2, 16) if (1 << k) < reps]
    outer = reps // 4
    x_bit, z_bit = r & 1, (r >> 1) & 1
    share = width // 4
    out_rows = width // (4 * reps)
    chunk = hidden_all // (4 * reps)
    wide = -(-(2 * outer * chunk) // 256) * 256 // (2 * outer)
    mine = 2 * outer * wide
    info = jnp.stack([g, r]).astype(jnp.int32)

    kv_parts = [
        jnp.concatenate(
            [
                lax.dynamic_slice_in_dim(keys, (g ^ j) * HD, HD, 1),
                lax.dynamic_slice_in_dim(values, (g ^ j) * HD, HD, 1),
            ],
            axis=1,
        )
        for j in range(4)
    ]
    kv_y = swap(jnp.stack([kv_parts[2], kv_parts[3]]), yy)
    kv_own = jnp.stack([kv_parts[0], swap(kv_parts[1], core), kv_y[0], swap(kv_y[1], core)])

    x_full = tokens.astype(F32)
    inv_one = lax.rsqrt(jnp.mean(x_full * x_full, axis=1, keepdims=True) + EPSILON)
    normed_one = x_full * inv_one
    h_one = (normed_one * gain_attn).astype(BF16)

    h_y = swap(after(h_one, kv_y), yy)
    wq_half = share // 2
    wq_y = jnp.stack(
        [
            lax.dynamic_slice(w_query, (x_bit * wq_half, (g ^ j) * share), (wq_half, share))
            for j in (2, 3)
        ]
    )
    wd = pack_down(info, w_down, outer, chunk, wide)
    if reps == 8:
        pairs = ring_of(reps)
        one = lax.ppermute(kv_own, BOTH, pairs)
        zero_x = swap(kv_own, xx)
        wq_y = swap(after(wq_y, kv_own), yy)
        one, h_y, wd, zero_x = together(one, h_y, wd, zero_x)
        stay, to_core, to_y, relay = pack(after(info, one), w_gate, w_up, outer, chunk, wide)
        two = lax.ppermute(one, BOTH, pairs)
        one_x = swap(one, xx)
        two, wq_y, stay, one_x = together(two, wq_y, stay, one_x)
        three = lax.ppermute(two, BOTH, pairs)
        wq_x = swap(wq_y, xx)
        two_x = swap(two, xx)
        dy_y = swap(after(cotangent, two), yy)
        three, two_x = together(three, two_x)
        three_x = swap(three, xx)
        three_x, wq_x, dy_y = together(three_x, wq_x, dy_y)
        kv = jnp.stack([kv_own, zero_x, one, one_x, two, two_x, three, three_x])
        slots = ring_slots(r, reps)
        relay = swap(after(relay, wq_y), yy)
    else:
        stay, to_core, to_y, relay = pack(info, w_gate, w_up, outer, chunk, wide)
        wq_y, dy_y, relay = swap(wq_y, yy), swap(cotangent, yy), swap(relay, yy)
        wq_x = swap(wq_y, xx)
        kv = lax.all_gather(kv_own, "rep", axis=0, tiled=False)
        slots = jnp.arange(reps, dtype=jnp.int32)

    h_group = jnp.stack([h_one, swap(h_one, core), h_y, swap(h_y, core)])
    h_group = h_group.reshape(4 * rows, width)
    upper_half = x_bit == 1
    wq_y = jnp.concatenate(
        [jnp.where(upper_half, wq_x, wq_y), jnp.where(upper_half, wq_y, wq_x)], axis=1
    )
    wq_parts = [
        lax.dynamic_slice_in_dim(w_query, g * share, share, 1),
        swap(lax.dynamic_slice_in_dim(w_query, (g ^ 1) * share, share, 1), core),
        wq_y[0],
        swap(wq_y[1], core),
    ]
    wq_cols = jnp.concatenate(absolute(wq_parts, g), axis=0)
    query = dot(h_group, wq_cols).astype(BF16).reshape(4, rows, share)

    dy_near = jnp.stack([cotangent, dy_y])
    dy_far = swap(dy_near, zz)
    attn, lse = attend(info, slots, starts, query, kv)
    attn, lse, relay = together(attn, lse, relay)
    from_y = swap(after(to_y, relay), yy)
    relay_x = swap(relay, xx)
    attn_rows = attn.reshape(4 * rows, share)
    branch = scatter_four_core(dot(attn_rows, w_out).reshape(4, rows, width), core)
    from_branch = swap(branch[1].astype(BF16), yy)
    from_branch, from_y = together(from_branch, from_y)
    resid = x_full + branch[0] + from_branch.astype(F32)
    inv_two = lax.rsqrt(jnp.mean(resid * resid, axis=1, keepdims=True) + EPSILON)
    normed_two = resid * inv_two
    h_two = (normed_two * gain_ffn).astype(BF16)

    h_y, h_z = swap(h_two, yy), swap(h_two, zz)
    from_y_x = swap(from_y, xx)
    h_y, h_z, relay_x = together(h_y, h_z, relay_x)
    low, upp = swap(h_y[: rows // 2], zz), swap(h_z[rows // 2 :], yy)
    low, upp, from_y_x, dy_far = together(low, upp, from_y_x, dy_far)
    h_a = jnp.concatenate([h_two, h_y, h_z, low, upp])
    h_b = swap(h_a, core)
    dy_a = jnp.stack([dy_near, dy_far]).reshape(4 * rows, width)
    dy_b = swap(dy_a, core)
    diagonal, diagonal_x = swap(relay, core), swap(relay_x, core)
    w_gu = jnp.concatenate(
        absolute(
            [
                stay,
                swap(to_core, core),
                jnp.concatenate(
                    [
                        jnp.where(upper_half, from_y_x, from_y),
                        jnp.where(upper_half, from_y, from_y_x),
                    ]
                ),
                jnp.concatenate(
                    [
                        jnp.where(upper_half, diagonal_x, diagonal),
                        jnp.where(upper_half, diagonal, diagonal_x),
                    ]
                ),
            ],
            g,
        ),
        axis=0,
    )

    hidden_b, d_gate_b, d_up_b = feed_forward(h_b, dy_b, w_gu, wd)
    from_core = swap(inputs_grad(d_gate_b, d_up_b, w_gu), core)
    hidden_a, d_gate_a, d_up_a = feed_forward(h_a, after(dy_a, d_up_b), w_gu, wd)
    d_h_parts, corner_low, corner_upp = inputs_grad(d_gate_a, d_up_a, w_gu, from_core)

    to_z, to_y = swap(corner_low, yy), swap(corner_upp, zz)
    send_g, send_u, keep_g, keep_u = columns_grad(
        after(info, d_h_parts), h_a, h_b, d_gate_a, d_gate_b, d_up_a, d_up_b, out_rows
    )
    to_z, to_y, send_g = together(to_z, to_y, send_g)
    got_g = swap(send_g, xx)
    from_z, from_y = side_step(d_h_parts, to_z, to_y, rows, yy, zz)
    out_core = swap(dot(after(hidden_b, to_z), wd).astype(BF16), core)
    send_d, keep_d = rows_grad(after(info, to_z), hidden_a, hidden_b, dy_a, dy_b)
    out_parts = dot(after(hidden_a, to_z), wd)
    from_z, from_y, out_core, send_d, out_parts = together(
        from_z, from_y, out_core, send_d, out_parts
    )
    d_h_two = d_h_parts[:rows] + from_z.astype(F32) + from_y.astype(F32)
    scaled_two = d_h_two * gain_ffn
    d_resid = cotangent.astype(F32) + inv_two * (
        scaled_two - normed_two * jnp.mean(scaled_two * normed_two, axis=1, keepdims=True)
    )
    da_own = d_resid.astype(BF16)
    da_y, da_c = swap(da_own, yy), swap(da_own, core)
    out_parts = (out_parts + out_core.astype(F32)).reshape(4, rows, width)
    out_z = swap(out_parts[2:].astype(BF16), zz)
    da_y, da_c = together(da_y, da_c)
    d_group = jnp.stack([da_own, da_c, da_y, swap(da_y, core)]).reshape(4 * rows, width)
    d_group, got_g, out_z = together(d_group, got_g, out_z)

    got_u = swap(after(send_u, got_g), xx)
    grad_g = (keep_g + got_g.astype(F32)).reshape(4, outer, 2, out_rows, mine)
    keep_g, got_g = high_part(grad_g, r, high[-1], 1)
    d_attn = dot_t(d_group, w_out).astype(BF16).reshape(4, rows, share)
    grad_o = t_dot(attn_rows, d_group).reshape(outer, 2, 2, out_rows, width)
    keep_o, got_o = part(grad_o, z_bit, zz, 1)
    d_query, keep_kv, send_kv = attend_back(info, slots, starts, query, d_attn, attn, lse, kv)
    d_query, send_kv, got_u, out_z = together(d_query, send_kv, got_u, out_z)
    out_parts = out_parts[:2] + out_z.astype(F32)

    got_d = swap(after(send_d, got_u), xx)
    grad_u = (keep_u + got_u.astype(F32)).reshape(4, outer, 2, out_rows, mine)
    keep_u, got_u = high_part(grad_u, r, high[-1], 1)
    d_query = d_query.reshape(4 * rows, share)
    d_h_one = dot_t(d_query, wq_cols).reshape(2, 2, rows, width)
    got_h = swap(d_h_one[:, 1].astype(BF16), core)
    d_wq = t_dot(h_group, d_query).reshape(4, outer, 2, 2, out_rows, share)
    got_h, got_g, got_o, d_wq = together(got_h, got_g, got_o, d_wq)

    d_h_one = d_h_one[:, 0] + got_h.astype(F32)
    from_h = swap(d_h_one[1].astype(BF16), yy)
    grad_g = high_rest(keep_g, got_g, r, high, 1).astype(BF16)
    near_g, far_g = pick(grad_g, z_bit, 1), swap(pick(grad_g, 1 - z_bit, 1), zz)
    from_h, far_g, got_d, send_kv, d_wq = together(from_h, far_g, got_d, send_kv, d_wq)

    got_kv = swap(send_kv, xx)
    grad_d = (keep_d + got_d.astype(F32)).reshape(outer, wide, width)
    keep_d, got_d = high_part(grad_d, r, high[-1], 0)
    d_h_one = d_h_one[0] + from_h.astype(F32)
    scaled_one = d_h_one * gain_attn
    d_tokens = (
        d_resid
        + inv_one
        * (scaled_one - normed_one * jnp.mean(scaled_one * normed_one, axis=1, keepdims=True))
    ).astype(BF16)
    grad_g = jnp.stack([near_g, far_g])
    grad_g = [pick(grad_g, g ^ j, 1) for j in range(4)]
    y_g = swap(jnp.stack([grad_g[2], grad_g[3]]), yy)
    got_u, y_g, got_o = together(got_u, y_g, got_o)

    grad_u = high_rest(keep_u, got_u, r, high, 1).astype(BF16)
    near_u, far_u = pick(grad_u, z_bit, 1), swap(pick(grad_u, 1 - z_bit, 1), zz)
    grad_g = jnp.stack(
        [grad_g[0], swap(after(grad_g[1], y_g), core), y_g[0], swap(y_g[1], core)]
    )
    far_u, grad_g, got_kv, got_o, d_wq = together(far_u, grad_g, got_kv, got_o, d_wq)

    keep_q, got_q = part(d_wq, x_bit, xx, 3)
    grad_kv = keep_kv.astype(F32) + got_kv.astype(F32)
    grad_kv = grad_kv.reshape((outer, 2) + grad_kv.shape[1:])
    keep_kv, got_kv = grad_kv[:, 0], swap(grad_kv[:, 1].astype(BF16), zz)
    grad_u = jnp.stack([near_u, far_u])
    grad_u = [pick(grad_u, g ^ j, 1) for j in range(4)]
    y_u = swap(jnp.stack([grad_u[2], grad_u[3]]), yy)
    got_kv, y_u, got_d = together(got_kv, y_u, got_d)

    d_wdown = high_rest(keep_d, got_d, r, high, 0)[:chunk]
    grad_kv = keep_kv + got_kv.astype(F32)
    for mask in reversed(high):
        grad_kv = grad_kv.reshape((2, grad_kv.shape[0] // 2) + grad_kv.shape[1:])
        grad_kv = grad_kv[0] + swap(grad_kv[1].astype(BF16), mask).astype(F32)
    grad_u = jnp.stack(
        [grad_u[0], swap(after(grad_u[1], y_u), core), y_u[0], swap(y_u[1], core)]
    )
    out_y = swap(after(out_parts[1], y_u).astype(BF16), yy)
    got_q, grad_u, keep_o = together(got_q, grad_u, keep_o)
    keep_q, got_q = part(keep_q + got_q.astype(F32), z_bit, zz, 2)
    keep_o, got_o = part(keep_o + got_o.astype(F32), x_bit, xx, 1)
    got_q, got_o, out_y, grad_kv = together(got_q, got_o, out_y, grad_kv)

    output = (resid + out_parts[0] + out_y.astype(F32)).astype(BF16)
    keep_q, got_q = high_part(keep_q + got_q.astype(F32), r, high[-1], 1)
    keep_o, got_o = high_part(keep_o + got_o.astype(F32), r, high[-1], 0)
    grad_kv = grad_kv[0].astype(BF16)
    grad_kv = absolute(exchange_four([grad_kv[j] for j in range(4)], core, yy), g)
    d_keys = jnp.concatenate([piece[:, :HD] for piece in grad_kv], axis=1)
    d_values = jnp.concatenate([piece[:, HD:] for piece in grad_kv], axis=1)
    d_wq = high_rest(keep_q, got_q, r, high, 1).astype(BF16)
    d_wq = absolute(exchange_four([pick(d_wq, g ^ j, 0) for j in range(4)], core, yy), g)
    d_wquery = jnp.concatenate(d_wq, axis=1).astype(F32)
    d_wout = high_rest(keep_o, got_o, r, high, 0)

    def own_rows(value):
        return lax.dynamic_slice_in_dim(value, r * out_rows, out_rows, 0)

    gain_at = (g * reps + r) * out_rows
    gain_rows = lax.dynamic_slice_in_dim(gain_ffn, gain_at, out_rows, 0)[:, None]
    d_wgate, d_wup, d_gain_two = unpack(
        info, grad_g, grad_u, own_rows(w_gate), own_rows(w_up), gain_rows, outer, chunk, wide
    )
    gain_rows = lax.dynamic_slice_in_dim(gain_attn, gain_at, out_rows, 0)
    d_gain_one = jnp.sum(d_wquery * own_rows(w_query).astype(F32), axis=1) / gain_rows
    return (
        output,
        d_tokens,
        d_gain_one,
        d_gain_two[:, 0],
        d_wquery,
        d_wout,
        d_wgate,
        d_wup,
        d_wdown,
        d_keys,
        d_values,
    )


def solution(mesh):
    spread = P(BOTH, None)
    member = P("grp", None)
    in_specs = (
        spread,
        spread,
        P(),
        P(),
        member,
        member,
        member,
        member,
        member,
        spread,
        spread,
        P(),
    )
    out_specs = (
        spread,
        spread,
        P(BOTH),
        P(BOTH),
        spread,
        spread,
        spread,
        spread,
        spread,
        spread,
        spread,
    )
    return jax.shard_map(
        on_device, mesh=mesh, in_specs=in_specs, out_specs=out_specs, check_vma=False
    )
```

```python
import functools

import jax
import jax.numpy as jnp
from jax import lax
from jax.experimental import pallas as pl
from jax.experimental.pallas import tpu as pltpu
from jax.sharding import PartitionSpec as P

HD = 128
EPSILON = 1e-06
NEGATIVE = -1e30
F32 = jnp.float32
BF16 = jnp.bfloat16
BOTH = ("grp", "rep")
BRIEF = pl.CostEstimate(flops=1, transcendentals=0, bytes_accessed=1)


def swap(value, mask):
    count = lax.axis_size(BOTH)
    return lax.ppermute(value, BOTH, [(i, i ^ mask) for i in range(count)])


def after(value, *earlier):
    return lax.optimization_barrier((value,) + earlier)[0]


def together(*values):
    return lax.optimization_barrier(values)


def dot(a, b):
    return jnp.dot(a, b, preferred_element_type=F32)


def dot_t(a, b):
    return lax.dot_general(a, b, (((1,), (1,)), ((), ())), preferred_element_type=F32)


def t_dot(a, b):
    return lax.dot_general(a, b, (((0,), (0,)), ((), ())), preferred_element_type=F32)


def pick(value, index, axis):
    return lax.dynamic_index_in_dim(value, index, axis, keepdims=False)


def scatter_four_core(parts, core):
    parts = parts.reshape((2, 2) + parts.shape[1:])
    got = swap(parts[:, 1].astype(BF16), core)
    return parts[:, 0] + got.astype(F32)


def side_step(parts, to_z, to_y, rows, yy, zz):
    half = rows // 2
    for_z = [parts[2 * rows : 2 * rows + half] + to_z.astype(F32), parts[2 * rows + half :]]
    for_y = [parts[rows : rows + half], parts[rows + half : 2 * rows] + to_y.astype(F32)]
    for_z, for_y = jnp.concatenate(for_z), jnp.concatenate(for_y)
    return swap(for_z.astype(BF16), zz), swap(for_y.astype(BF16), yy)


def exchange_four(pieces, core, yy):
    from_y = swap(jnp.stack([pieces[2], pieces[3]]), yy)
    from_c = swap(pieces[1], core)
    return [pieces[0], from_c, from_y[0], swap(from_y[1], core)]


def absolute(pieces, g):
    odd, upper = (g & 1) == 1, (g >> 1) == 1
    a = jnp.where(odd, pieces[1], pieces[0])
    b = jnp.where(odd, pieces[0], pieces[1])
    c = jnp.where(odd, pieces[3], pieces[2])
    d = jnp.where(odd, pieces[2], pieces[3])
    return [
        jnp.where(upper, c, a),
        jnp.where(upper, d, b),
        jnp.where(upper, a, c),
        jnp.where(upper, b, d),
    ]


def part(value, bit, mask, axis):
    return pick(value, bit, axis).astype(F32), swap(pick(value, 1 - bit, axis).astype(BF16), mask)


def high_part(value, r, mask, axis):
    shape = value.shape
    value = value.reshape(shape[:axis] + (2, shape[axis] // 2) + shape[axis + 1 :])
    return part(value, (r & mask) // mask, mask, axis)


def high_rest(kept, got, r, high, axis):
    value = kept + got.astype(F32)
    for mask in reversed(high[:-1]):
        kept, got = high_part(value, r, mask, axis)
        value = kept + got.astype(F32)
    return jnp.squeeze(value, axis)


def ring_of(reps):
    ring = (0, 1, 3, 2)
    pairs = []
    for member in range(4):
        for k in range(4):
            for x in range(2):
                base = member * reps + x
                pairs.append((base + 2 * ring[k], base + 2 * ring[(k + 1) % 4]))
    return pairs


def ring_slots(r, reps):
    order = jnp.array((0, 1, 3, 2), jnp.int32)
    other = jnp.arange(reps, dtype=jnp.int32)
    steps = (order[r >> 1] - order[other >> 1]) & 3
    return 2 * steps + ((other ^ r) & 1)


def pack_kernel(
    outer, chunk, wide, info_ref, gate_ref, up_ref, stay_ref, core_ref, y_ref, relay_ref, held
):
    step = pl.program_id(0)
    g, bit, x = info_ref[0], (info_ref[1] >> 1) & 1, info_ref[1] & 1
    rows = gate_ref.shape[0]
    quarter = outer * 4 * chunk
    fill = jnp.zeros((rows, wide - chunk), BF16)

    for b in range(2):

        @pl.when(bit == b)
        def _():
            for which, ref in enumerate((gate_ref, up_ref)):
                block = ref[...]
                for member in range(4):
                    parts = []
                    for xd in range(2):
                        for o in range(outer):
                            at = member * quarter + (o * 4 + b * 2 + xd) * chunk
                            parts += [block[:, at : at + chunk], fill]
                    span = 2 * outer * wide
                    held[member ^ g, :, which * span : (which + 1) * span] = jnp.concatenate(
                        parts, axis=1
                    )

    stay_ref[...] = held[0]
    core_ref[...] = held[1]

    @pl.when(step // (pl.num_programs(0) // 2) == x)
    def _():
        y_ref[...] = held[2]
        relay_ref[...] = held[3]


def pack(info, w_gate, w_up, outer, chunk, wide):
    rows, width = w_gate.shape
    span = 4 * outer * wide
    steps = 8
    part = rows // steps

    def lower(i, info):
        return jnp.clip(i - (info[1] & 1) * (steps // 2), 0, steps // 2 - 1), 0

    def plain(i, info):
        return i, 0

    shape = jax.ShapeDtypeStruct((rows, span), BF16)
    small = jax.ShapeDtypeStruct((rows // 2, span), BF16)
    return pl.pallas_call(
        functools.partial(pack_kernel, outer, chunk, wide),
        grid_spec=pltpu.PrefetchScalarGridSpec(
            num_scalar_prefetch=1,
            grid=(steps,),
            in_specs=[pl.BlockSpec((part, width), plain), pl.BlockSpec((part, width), plain)],
            out_specs=[
                pl.BlockSpec((part, span), plain),
                pl.BlockSpec((part, span), plain),
                pl.BlockSpec((part, span), lower),
                pl.BlockSpec((part, span), lower),
            ],
            scratch_shapes=[pltpu.VMEM((4, part, span), BF16)],
        ),
        out_shape=[shape, shape, small, small],
        compiler_params=pltpu.CompilerParams(vmem_limit_bytes=32 << 20),
        cost_estimate=BRIEF,
        name="pack",
    )(info, w_gate, w_up)


def pack_down_kernel(outer, chunk, wide, info_ref, down_ref, out_ref):
    bit = (info_ref[1] >> 1) & 1
    block = down_ref[...]
    fill = jnp.zeros((wide - chunk, block.shape[1]), BF16)
    for b in range(2):

        @pl.when(bit == b)
        def _():
            for xd in range(2):
                for o in range(outer):
                    at = (o * 4 + b * 2 + xd) * chunk
                    piece = jnp.concatenate([block[at : at + chunk], fill], axis=0)
                    to = (xd * outer + o) * wide
                    out_ref[to : to + wide] = piece


def pack_down(info, w_down, outer, chunk, wide):
    rows, width = w_down.shape
    steps = 4
    part = width // steps
    mine = 2 * outer * wide
    return pl.pallas_call(
        functools.partial(pack_down_kernel, outer, chunk, wide),
        grid=(steps,),
        in_specs=[
            pl.BlockSpec(memory_space=pltpu.SMEM),
            pl.BlockSpec((rows, part), lambda i: (0, i)),
        ],
        out_specs=pl.BlockSpec((mine, part), lambda i: (0, i)),
        out_shape=jax.ShapeDtypeStruct((mine, width), BF16),
        compiler_params=pltpu.CompilerParams(vmem_limit_bytes=32 << 20),
        cost_estimate=BRIEF,
        name="pack_down",
    )(info, w_down)


def feed_forward_kernel(h_ref, dy_ref, gate_ref, up_ref, down_ref, hid_ref, d_gate_ref, d_up_ref):
    h = h_ref[...]
    gate = dot(h, gate_ref[...])
    upper = dot(h, up_ref[...])
    d_hidden = dot_t(dy_ref[...], down_ref[...])
    sigma = 1.0 / (1.0 + jnp.exp(-gate))
    swish = gate * sigma
    hid_ref[...] = (swish * upper).astype(BF16)
    d_up_ref[...] = (d_hidden * swish).astype(BF16)
    d_gate_ref[...] = (d_hidden * upper * (sigma + swish * (1.0 - sigma))).astype(BF16)


def feed_forward(h, dy, w_gu, wd):
    tokens, width = h.shape
    mine = wd.shape[0]
    piece = 256
    steps = mine // piece
    whole = pl.BlockSpec((tokens, width), lambda j: (0, 0))
    out = pl.BlockSpec((tokens, piece), lambda j: (0, j))
    return pl.pallas_call(
        feed_forward_kernel,
        grid=(steps,),
        in_specs=[
            whole,
            whole,
            pl.BlockSpec((width, piece), lambda j: (0, j)),
            pl.BlockSpec((width, piece), lambda j: (0, j + steps)),
            pl.BlockSpec((piece, width), lambda j: (j, 0)),
        ],
        out_specs=[out] * 3,
        out_shape=[jax.ShapeDtypeStruct((tokens, mine), BF16)] * 3,
        compiler_params=pltpu.CompilerParams(vmem_limit_bytes=48 << 20),
        name="feed_forward",
    )(h, dy, w_gu, w_gu, wd)


def inputs_grad_kernel(mine, d_gate_ref, d_up_ref, w_ref, out_ref):
    w = w_ref[...]
    out = dot_t(d_gate_ref[...], w[:, :mine]) + dot_t(d_up_ref[...], w[:, mine:])
    out_ref[...] = out.astype(BF16)


def inputs_grad_sum_kernel(
    mine, rows, d_gate_ref, d_up_ref, w_ref, other_ref, parts_ref, low_ref, upp_ref
):
    w = w_ref[...]
    out = dot_t(d_gate_ref[...], w[:, :mine]) + dot_t(d_up_ref[...], w[:, mine:])
    out = out + other_ref[...].astype(F32)
    parts_ref[...] = out[: 3 * rows]
    low_ref[...] = out[3 * rows : 3 * rows + rows // 2].astype(BF16)
    upp_ref[...] = out[3 * rows + rows // 2 :].astype(BF16)


def inputs_grad(d_gate, d_up, w_gu, other=None):
    tokens, mine = d_gate.shape
    width = w_gu.shape[0]
    piece = min(512, width)
    rows = tokens // 4
    lhs = pl.BlockSpec((tokens, mine), lambda j: (0, 0))
    in_specs = [lhs, lhs, pl.BlockSpec((piece, 2 * mine), lambda j: (j, 0))]
    out = pl.BlockSpec((tokens, piece), lambda j: (0, j))
    params = pltpu.CompilerParams(vmem_limit_bytes=48 << 20)
    if other is None:
        return pl.pallas_call(
            functools.partial(inputs_grad_kernel, mine),
            grid=(width // piece,),
            in_specs=in_specs,
            out_specs=out,
            out_shape=jax.ShapeDtypeStruct((tokens, width), BF16),
            compiler_params=params,
            name="inputs_grad",
        )(d_gate, d_up, w_gu)
    half = pl.BlockSpec((rows // 2, piece), lambda j: (0, j))
    return pl.pallas_call(
        functools.partial(inputs_grad_sum_kernel, mine, rows),
        grid=(width // piece,),
        in_specs=in_specs + [out],
        out_specs=[pl.BlockSpec((3 * rows, piece), lambda j: (0, j)), half, half],
        out_shape=[jax.ShapeDtypeStruct((3 * rows, width), F32)]
        + [jax.ShapeDtypeStruct((rows // 2, width), BF16)] * 2,
        compiler_params=params,
        name="inputs_grad_sum",
    )(d_gate, d_up, w_gu, other)


def columns_grad_kernel(
    rows, info_ref, ha, hb, ga, gb, ua, ub, send_g, send_u, keep_g, keep_u
):
    odd = (info_ref[1] & 1) == 1
    for da, db, send, keep in ((ga, gb, send_g, keep_g), (ua, ub, send_u, keep_u)):
        grad = t_dot(ha[...], da[...]) + t_dot(hb[...], db[...])
        count, width = grad.shape
        grad = grad.reshape(count // (2 * rows), 2, rows, width)
        low, upp = grad[:, 0], grad[:, 1]
        send[...] = jnp.where(odd, low, upp).astype(BF16).reshape(count // 2, width)
        keep[...] = jnp.where(odd, upp, low).reshape(count // 2, width)


def columns_grad(info, ha, hb, ga, gb, ua, ub, rows):
    tokens, width = ha.shape
    mine = ga.shape[1]
    part = min(512, width)
    half = pl.BlockSpec((part // 2, mine), lambda i: (i, 0))
    lhs = pl.BlockSpec((tokens, part), lambda i: (0, i))
    rhs = pl.BlockSpec(ga.shape, lambda i: (0, 0))
    return pl.pallas_call(
        functools.partial(columns_grad_kernel, rows),
        grid=(width // part,),
        in_specs=[pl.BlockSpec(memory_space=pltpu.SMEM), lhs, lhs, rhs, rhs, rhs, rhs],
        out_specs=[half] * 4,
        out_shape=[jax.ShapeDtypeStruct((width // 2, mine), BF16)] * 2
        + [jax.ShapeDtypeStruct((width // 2, mine), F32)] * 2,
        compiler_params=pltpu.CompilerParams(vmem_limit_bytes=56 << 20),
        name="columns_grad",
    )(info, ha, hb, ga, gb, ua, ub)


def rows_grad_kernel(info_ref, ha, hb, da, db, send_one, send_two, keep_one, keep_two):
    odd = (info_ref[1] & 1) == 1
    step = pl.program_id(0)
    first = step < pl.num_programs(0) // 2
    grad = t_dot(ha[...], da[...]) + t_dot(hb[...], db[...])
    half = grad.shape[0] // 2
    low, upp = grad[:half], grad[half:]
    send = jnp.where(odd, low, upp).astype(BF16)
    keep = jnp.where(odd, upp, low)

    @pl.when(first)
    def _():
        send_one[...] = send
        keep_one[...] = keep

    @pl.when(jnp.logical_not(first))
    def _():
        send_two[...] = send
        keep_two[...] = keep


def rows_grad(info, ha, hb, da, db):
    tokens, mine = ha.shape
    width = da.shape[1]
    part = min(512, width // 2)
    steps = width // part
    one = pl.BlockSpec((mine // 2, part), lambda i: (0, jnp.minimum(i, steps // 2 - 1)))
    two = pl.BlockSpec((mine // 2, part), lambda i: (0, jnp.maximum(i - steps // 2, 0)))
    lhs = pl.BlockSpec(ha.shape, lambda i: (0, 0))
    rhs = pl.BlockSpec((tokens, part), lambda i: (0, i))
    return pl.pallas_call(
        rows_grad_kernel,
        grid=(steps,),
        in_specs=[pl.BlockSpec(memory_space=pltpu.SMEM), lhs, lhs, rhs, rhs],
        out_specs=[one, two, one, two],
        out_shape=[jax.ShapeDtypeStruct((mine // 2, width // 2), BF16)] * 2
        + [jax.ShapeDtypeStruct((mine // 2, width // 2), F32)] * 2,
        compiler_params=pltpu.CompilerParams(vmem_limit_bytes=48 << 20),
        name="rows_grad",
    )(info, ha, hb, da, db)


def query_back_kernel(rows, d_ref, w_ref, keep_ref, send_ref):
    out = dot_t(d_ref[...], w_ref[...])
    for k in range(2):
        keep_ref[k] = out[2 * k * rows : (2 * k + 1) * rows]
        send_ref[k] = out[(2 * k + 1) * rows : (2 * k + 2) * rows].astype(BF16)


def query_back(d_query, wq, rows):
    width, share = wq.shape
    part = min(512, width)
    out = pl.BlockSpec((2, rows, part), lambda j: (0, 0, j))
    return pl.pallas_call(
        functools.partial(query_back_kernel, rows),
        grid=(width // part,),
        in_specs=[
            pl.BlockSpec(d_query.shape, lambda j: (0, 0)),
            pl.BlockSpec((part, share), lambda j: (j, 0)),
        ],
        out_specs=[out, out],
        out_shape=[
            jax.ShapeDtypeStruct((2, rows, width), F32),
            jax.ShapeDtypeStruct((2, rows, width), BF16),
        ],
        compiler_params=pltpu.CompilerParams(vmem_limit_bytes=32 << 20),
        name="query_back",
    )(d_query, wq)


def unpack_kernel(
    outer, chunk, wide, info_ref, got_g, got_u, w_gate, w_up, gain, gate_ref, up_ref, dg_ref
):
    g, bit = info_ref[0], (info_ref[1] >> 1) & 1
    total = 0.0
    for got, ref, weight in ((got_g, gate_ref, w_gate), (got_u, up_ref, w_up)):
        parts = []
        for member in range(4):
            pieces = [got[member ^ g, b ^ bit] for b in range(2)]
            for o in range(outer):
                for b in range(2):
                    for xd in range(2):
                        at = (xd * outer + o) * wide
                        parts.append(pieces[b][:, at : at + chunk])
        grad = jnp.concatenate(parts, axis=1).astype(F32)
        ref[...] = grad
        total = total + jnp.sum(grad * weight[...].astype(F32), axis=1, keepdims=True)
    dg_ref[...] = total / gain[...]


def unpack(info, got_g, got_u, w_gate, w_up, gain, outer, chunk, wide):
    rows = got_g.shape[2]
    weight = pl.BlockSpec((rows, w_gate.shape[1]), lambda i, info: (info[1], 0))
    shape = jax.ShapeDtypeStruct((rows, 16 * outer * chunk), F32)
    def whole(value):
        return pl.BlockSpec(value.shape, lambda i, info: (0,) * len(value.shape))

    outs = [shape, shape, jax.ShapeDtypeStruct((rows, 1), F32)]
    return pl.pallas_call(
        functools.partial(unpack_kernel, outer, chunk, wide),
        grid_spec=pltpu.PrefetchScalarGridSpec(
            num_scalar_prefetch=1,
            grid=(1,),
            in_specs=[whole(got_g), whole(got_u), weight, weight, whole(gain)],
            out_specs=[whole(out) for out in outs],
        ),
        out_shape=outs,
        compiler_params=pltpu.CompilerParams(vmem_limit_bytes=32 << 20),
        name="unpack",
    )(info, got_g, got_u, w_gate, w_up, gain)


def block_bounds(info_ref, starts_ref, j, reps):
    place = ((info_ref[0] ^ j) * reps + info_ref[1]) * HD
    docs = starts_ref.shape[0]
    first = jnp.int32(0)
    for d in range(docs):
        first = jnp.maximum(first, jnp.where(starts_ref[d] <= place, starts_ref[d], 0))
    position = place + lax.broadcasted_iota(jnp.int32, (4, HD, 1), 1).reshape(4 * HD, 1)
    lowest = jnp.zeros_like(position)
    for d in range(docs):
        lowest = jnp.maximum(lowest, jnp.where(starts_ref[d] <= position, starts_ref[d], 0))
    return place, first, position, lowest


def key_tile(info_ref, slots_ref, kv_ref, tile, reps):
    per = reps // 4
    member = (tile // per) ^ info_ref[0]
    base = 4 * (tile % per)
    piece = jnp.concatenate([kv_ref[slots_ref[base + k], member] for k in range(4)], axis=0)
    return piece[:, :HD], piece[:, HD:]


def head_rows(ref):
    return jnp.concatenate([ref[0, :, h * HD : (h + 1) * HD] for h in range(4)], axis=0)


def attend_kernel(reps, info_ref, slots_ref, starts_ref, q_ref, kv_ref, o_ref, lse_ref):
    j = pl.program_id(0)
    place, first, position, lowest = block_bounds(info_ref, starts_ref, j, reps)
    query = head_rows(q_ref)
    rows = 4 * HD
    scale = HD ** (-0.5)

    def step(tile, carry):
        best, total, accum = carry
        key, value = key_tile(info_ref, slots_ref, kv_ref, tile, reps)
        scores = dot_t(query, key) * scale
        at = tile * 512 + lax.broadcasted_iota(jnp.int32, (1, 512), 1)
        scores = jnp.where((at >= lowest) & (at <= position), scores, NEGATIVE)
        new_best = jnp.maximum(best, jnp.max(scores, axis=1, keepdims=True))
        weights = jnp.exp(scores - new_best)
        factor = jnp.exp(best - new_best)
        total = total * factor + jnp.sum(weights, axis=1, keepdims=True)
        accum = accum * factor + dot(weights.astype(BF16), value)
        return new_best, total, accum

    init = (
        jnp.full((rows, 1), NEGATIVE, F32),
        jnp.zeros((rows, 1), F32),
        jnp.zeros((rows, HD), F32),
    )
    best, total, accum = lax.fori_loop(first // 512, place // 512 + 1, step, init)
    out = accum / total
    for h in range(4):
        o_ref[0, :, h * HD : (h + 1) * HD] = out[h * HD : (h + 1) * HD].astype(BF16)
    lse_ref[0] = best + jnp.log(total)


def attend(info, slots, starts, query, kv):
    reps = kv.shape[0]
    return pl.pallas_call(
        functools.partial(attend_kernel, reps),
        grid=(4,),
        in_specs=[
            pl.BlockSpec(memory_space=pltpu.SMEM),
            pl.BlockSpec(memory_space=pltpu.SMEM),
            pl.BlockSpec(memory_space=pltpu.SMEM),
            pl.BlockSpec((1, HD, 4 * HD), lambda j: (j, 0, 0)),
            pl.BlockSpec(kv.shape, lambda j: (0, 0, 0, 0)),
        ],
        out_specs=[
            pl.BlockSpec((1, HD, 4 * HD), lambda j: (j, 0, 0)),
            pl.BlockSpec((1, 4 * HD, 1), lambda j: (j, 0, 0)),
        ],
        out_shape=[
            jax.ShapeDtypeStruct((4, HD, 4 * HD), BF16),
            jax.ShapeDtypeStruct((4, 4 * HD, 1), F32),
        ],
        compiler_params=pltpu.CompilerParams(vmem_limit_bytes=48 << 20),
        cost_estimate=BRIEF,
        name="attend",
    )(info, slots, starts, query, kv)


def attend_back_kernel(
    reps,
    info_ref,
    slots_ref,
    starts_ref,
    q_ref,
    do_ref,
    o_ref,
    lse_ref,
    kv_ref,
    dq_ref,
    keep_ref,
    send_ref,
    sums,
):
    j = pl.program_id(0)

    @pl.when(j == 0)
    def _():
        sums[...] = jnp.zeros_like(sums)

    place, first, position, lowest = block_bounds(info_ref, starts_ref, j, reps)
    query = head_rows(q_ref)
    d_out = head_rows(do_ref)
    out = head_rows(o_ref)
    lse = lse_ref[0]
    delta = jnp.sum(d_out.astype(F32) * out.astype(F32), axis=1, keepdims=True)
    scale = HD ** (-0.5)
    per = reps // 4

    def step(tile, d_query):
        key, value = key_tile(info_ref, slots_ref, kv_ref, tile, reps)
        scores = dot_t(query, key) * scale
        at = tile * 512 + lax.broadcasted_iota(jnp.int32, (1, 512), 1)
        probs = jnp.where((at >= lowest) & (at <= position), jnp.exp(scores - lse), 0.0)
        d_probs = dot_t(d_out, value)
        d_scores = (probs * (d_probs - delta)).astype(BF16)
        d_query = d_query + dot(d_scores, key)
        d_key = t_dot(d_scores, query) * scale
        d_value = t_dot(probs.astype(BF16), d_out)
        member = (tile // per) ^ info_ref[0]
        both = jnp.concatenate([d_key, d_value], axis=1)
        for k in range(4):
            slot = (4 * (tile % per) + k) ^ info_ref[1]
            sums[slot, member] = sums[slot, member] + both[k * HD : (k + 1) * HD]
        return d_query

    d_query = lax.fori_loop(
        first // 512, place // 512 + 1, step, jnp.zeros((4 * HD, HD), F32)
    )
    d_query = (d_query * scale).astype(BF16)
    for h in range(4):
        dq_ref[0, :, h * HD : (h + 1) * HD] = d_query[h * HD : (h + 1) * HD]

    @pl.when(j == 3)
    def _():
        for slot in range(reps // 2):
            keep_ref[slot] = sums[2 * slot].astype(BF16)
            send_ref[slot] = sums[2 * slot + 1].astype(BF16)


def attend_back(info, slots, starts, query, d_out, out, lse, kv):
    reps = kv.shape[0]
    rows = pl.BlockSpec((1, HD, 4 * HD), lambda j: (j, 0, 0))
    whole = pl.BlockSpec(kv.shape, lambda j: (0, 0, 0, 0))
    half = pl.BlockSpec((reps // 2,) + kv.shape[1:], lambda j: (0, 0, 0, 0))
    return pl.pallas_call(
        functools.partial(attend_back_kernel, reps),
        grid=(4,),
        in_specs=[
            pl.BlockSpec(memory_space=pltpu.SMEM),
            pl.BlockSpec(memory_space=pltpu.SMEM),
            pl.BlockSpec(memory_space=pltpu.SMEM),
            rows,
            rows,
            rows,
            pl.BlockSpec((1, 4 * HD, 1), lambda j: (j, 0, 0)),
            whole,
        ],
        out_specs=[rows, half, half],
        out_shape=[jax.ShapeDtypeStruct((4, HD, 4 * HD), BF16)]
        + [jax.ShapeDtypeStruct((reps // 2,) + kv.shape[1:], BF16)] * 2,
        scratch_shapes=[pltpu.VMEM(kv.shape, F32)],
        compiler_params=pltpu.CompilerParams(vmem_limit_bytes=60 << 20),
        cost_estimate=BRIEF,
        name="attend_back",
    )(info, slots, starts, query, d_out, out, lse, kv)


def on_device(
    tokens,
    cotangent,
    gain_attn,
    gain_ffn,
    w_query,
    w_out,
    w_gate,
    w_up,
    w_down,
    keys,
    values,
    starts,
):
    reps = lax.axis_size("rep")
    rows, width = tokens.shape
    hidden_all = w_gate.shape[1]
    g = lax.axis_index("grp")
    r = lax.axis_index("rep")
    core, yy, xx, zz = reps, 2 * reps, 1, 2
    high = [1 << k for k in range(2, 16) if (1 << k) < reps]
    outer = reps // 4
    x_bit, z_bit = r & 1, (r >> 1) & 1
    share = width // 4
    out_rows = width // (4 * reps)
    chunk = hidden_all // (4 * reps)
    wide = -(-(2 * outer * chunk) // 256) * 256 // (2 * outer)
    mine = 2 * outer * wide
    info = jnp.stack([g, r]).astype(jnp.int32)

    kv_parts = [
        jnp.concatenate(
            [
                lax.dynamic_slice_in_dim(keys, (g ^ j) * HD, HD, 1),
                lax.dynamic_slice_in_dim(values, (g ^ j) * HD, HD, 1),
            ],
            axis=1,
        )
        for j in range(4)
    ]
    kv_y = swap(jnp.stack([kv_parts[2], kv_parts[3]]), yy)
    kv_own = jnp.stack([kv_parts[0], swap(kv_parts[1], core), kv_y[0], swap(kv_y[1], core)])

    x_full = tokens.astype(F32)
    inv_one = lax.rsqrt(jnp.mean(x_full * x_full, axis=1, keepdims=True) + EPSILON)
    normed_one = x_full * inv_one
    h_one = (normed_one * gain_attn).astype(BF16)

    h_y = swap(after(h_one, kv_y), yy)
    wq_half = share // 2
    wq_y = jnp.stack(
        [
            lax.dynamic_slice(w_query, (x_bit * wq_half, (g ^ j) * share), (wq_half, share))
            for j in (2, 3)
        ]
    )
    wd = pack_down(info, w_down, outer, chunk, wide)
    if reps == 8:
        pairs = ring_of(reps)
        one = lax.ppermute(kv_own, BOTH, pairs)
        zero_x = swap(kv_own, xx)
        wq_y = swap(after(wq_y, kv_own), yy)
        one, h_y, wd, zero_x = together(one, h_y, wd, zero_x)
        stay, to_core, to_y, relay = pack(after(info, one), w_gate, w_up, outer, chunk, wide)
        two = lax.ppermute(one, BOTH, pairs)
        one_x = swap(one, xx)
        two, wq_y, stay, one_x = together(two, wq_y, stay, one_x)
        three = lax.ppermute(two, BOTH, pairs)
        wq_x = swap(wq_y, xx)
        two_x = swap(two, xx)
        dy_y = swap(after(cotangent, two), yy)
        three, two_x = together(three, two_x)
        three_x = swap(three, xx)
        three_x, wq_x, dy_y = together(three_x, wq_x, dy_y)
        kv = jnp.stack([kv_own, zero_x, one, one_x, two, two_x, three, three_x])
        slots = ring_slots(r, reps)
        relay = swap(after(relay, wq_y), yy)
    else:
        stay, to_core, to_y, relay = pack(info, w_gate, w_up, outer, chunk, wide)
        wq_y, dy_y, relay = swap(wq_y, yy), swap(cotangent, yy), swap(relay, yy)
        wq_x = swap(wq_y, xx)
        kv = lax.all_gather(kv_own, "rep", axis=0, tiled=False)
        slots = jnp.arange(reps, dtype=jnp.int32)

    h_group = jnp.stack([h_one, swap(h_one, core), h_y, swap(h_y, core)])
    h_group = h_group.reshape(4 * rows, width)
    upper_half = x_bit == 1
    wq_y = jnp.concatenate(
        [jnp.where(upper_half, wq_x, wq_y), jnp.where(upper_half, wq_y, wq_x)], axis=1
    )
    wq_parts = [
        lax.dynamic_slice_in_dim(w_query, g * share, share, 1),
        swap(lax.dynamic_slice_in_dim(w_query, (g ^ 1) * share, share, 1), core),
        wq_y[0],
        swap(wq_y[1], core),
    ]
    wq_cols = jnp.concatenate(absolute(wq_parts, g), axis=0)
    query = dot(h_group, wq_cols).astype(BF16).reshape(4, rows, share)

    dy_near = jnp.stack([cotangent, dy_y])
    dy_far = swap(dy_near, zz)
    attn, lse = attend(info, slots, starts, query, kv)
    attn, lse, relay = together(attn, lse, relay)
    from_y = swap(after(to_y, relay), yy)
    relay_x = swap(relay, xx)
    attn_rows = attn.reshape(4 * rows, share)
    branch = scatter_four_core(dot(attn_rows, w_out).reshape(4, rows, width), core)
    from_branch = swap(branch[1].astype(BF16), yy)
    from_branch, from_y = together(from_branch, from_y)
    resid = x_full + branch[0] + from_branch.astype(F32)
    inv_two = lax.rsqrt(jnp.mean(resid * resid, axis=1, keepdims=True) + EPSILON)
    normed_two = resid * inv_two
    h_two = (normed_two * gain_ffn).astype(BF16)

    h_y, h_z = swap(h_two, yy), swap(h_two, zz)
    from_y_x = swap(from_y, xx)
    h_y, h_z, relay_x = together(h_y, h_z, relay_x)
    low, upp = swap(h_y[: rows // 2], zz), swap(h_z[rows // 2 :], yy)
    low, upp, from_y_x, dy_far = together(low, upp, from_y_x, dy_far)
    h_a = jnp.concatenate([h_two, h_y, h_z, low, upp])
    h_b = swap(h_a, core)
    dy_a = jnp.stack([dy_near, dy_far]).reshape(4 * rows, width)
    dy_b = swap(dy_a, core)
    diagonal, diagonal_x = swap(relay, core), swap(relay_x, core)
    w_gu = jnp.concatenate(
        absolute(
            [
                stay,
                swap(to_core, core),
                jnp.concatenate(
                    [
                        jnp.where(upper_half, from_y_x, from_y),
                        jnp.where(upper_half, from_y, from_y_x),
                    ]
                ),
                jnp.concatenate(
                    [
                        jnp.where(upper_half, diagonal_x, diagonal),
                        jnp.where(upper_half, diagonal, diagonal_x),
                    ]
                ),
            ],
            g,
        ),
        axis=0,
    )

    hidden_b, d_gate_b, d_up_b = feed_forward(h_b, dy_b, w_gu, wd)
    from_core = swap(inputs_grad(d_gate_b, d_up_b, w_gu), core)
    hidden_a, d_gate_a, d_up_a = feed_forward(h_a, after(dy_a, d_up_b), w_gu, wd)
    d_h_parts, corner_low, corner_upp = inputs_grad(d_gate_a, d_up_a, w_gu, from_core)

    to_z, to_y = swap(corner_low, yy), swap(corner_upp, zz)
    send_g, send_u, keep_g, keep_u = columns_grad(
        after(info, d_h_parts), h_a, h_b, d_gate_a, d_gate_b, d_up_a, d_up_b, out_rows
    )
    to_z, to_y, send_g = together(to_z, to_y, send_g)
    got_g = swap(send_g, xx)
    from_z, from_y = side_step(d_h_parts, to_z, to_y, rows, yy, zz)
    out_core = swap(dot(after(hidden_b, to_z), wd).astype(BF16), core)
    send_d, send_e, keep_d, keep_e = rows_grad(
        after(info, to_z), hidden_a, hidden_b, dy_a, dy_b
    )
    out_parts = dot(after(hidden_a, to_z), wd)
    from_z, from_y, out_core, send_d, out_parts = together(
        from_z, from_y, out_core, send_d, out_parts
    )
    d_h_two = d_h_parts[:rows] + from_z.astype(F32) + from_y.astype(F32)
    scaled_two = d_h_two * gain_ffn
    d_resid = cotangent.astype(F32) + inv_two * (
        scaled_two - normed_two * jnp.mean(scaled_two * normed_two, axis=1, keepdims=True)
    )
    da_own = d_resid.astype(BF16)
    da_y, da_c = swap(da_own, yy), swap(da_own, core)
    out_parts = (out_parts + out_core.astype(F32)).reshape(2, 2, rows, width)
    da_y, da_c = together(da_y, da_c)
    d_group = jnp.stack([da_own, da_c, da_y, swap(da_y, core)]).reshape(4 * rows, width)
    d_group, got_g = together(d_group, got_g)

    got_u = swap(after(send_u, got_g), xx)
    grad_g = (keep_g + got_g.astype(F32)).reshape(4, outer, 2, out_rows, mine)
    keep_g, got_g = high_part(grad_g, r, high[-1], 1)
    d_attn = dot_t(d_group, w_out).astype(BF16).reshape(4, rows, share)
    grad_o = t_dot(attn_rows, d_group).reshape(outer, 2, 2, out_rows, width)
    keep_o, got_o = part(grad_o, z_bit, zz, 1)
    out_y = swap(after(out_parts, d_group)[:, 1].astype(BF16), yy)
    d_query, keep_kv, send_kv = attend_back(info, slots, starts, query, d_attn, attn, lse, kv)
    d_query, send_kv, got_u, out_y = together(d_query, send_kv, got_u, out_y)

    got_kv = swap(send_kv, xx)
    grad_u = (keep_u + got_u.astype(F32)).reshape(4, outer, 2, out_rows, mine)
    keep_u, got_u = high_part(grad_u, r, high[-1], 1)
    d_query = d_query.reshape(4 * rows, share)
    d_h_one, send_h = query_back(d_query, wq_cols, rows)
    got_h = swap(send_h, core)
    d_wq = t_dot(h_group, d_query).reshape(4, outer, 2, 2, out_rows, share)
    out_parts = out_parts[:, 0] + out_y.astype(F32)
    got_h, got_g, d_wq = together(got_h, got_g, d_wq)

    d_h_one = d_h_one + got_h.astype(F32)
    from_h = swap(d_h_one[1].astype(BF16), yy)
    grad_g = high_rest(keep_g, got_g, r, high, 1).astype(BF16)
    near_g, far_g = pick(grad_g, z_bit, 1), swap(pick(grad_g, 1 - z_bit, 1), zz)
    got_kv, d_wq = together(got_kv, d_wq)

    keep_q, got_q = part(d_wq, x_bit, xx, 3)
    grad_kv = keep_kv.astype(F32) + got_kv.astype(F32)
    grad_kv = grad_kv.reshape((outer, 2) + grad_kv.shape[1:])
    keep_kv, got_kv = grad_kv[:, 0], swap(grad_kv[:, 1].astype(BF16), zz)
    from_h, far_g, got_u, got_o = together(from_h, far_g, got_u, got_o)

    d_h_one = d_h_one[0] + from_h.astype(F32)
    scaled_one = d_h_one * gain_attn
    d_tokens = (
        d_resid
        + inv_one
        * (scaled_one - normed_one * jnp.mean(scaled_one * normed_one, axis=1, keepdims=True))
    ).astype(BF16)
    grad_g = jnp.stack([near_g, far_g])
    grad_g = [pick(grad_g, g ^ j, 1) for j in range(4)]
    y_g = swap(jnp.stack([grad_g[2], grad_g[3]]), yy)
    grad_u = high_rest(keep_u, got_u, r, high, 1).astype(BF16)
    near_u, far_u = pick(grad_u, z_bit, 1), swap(pick(grad_u, 1 - z_bit, 1), zz)
    y_g, got_kv, got_q, send_d, send_e = together(y_g, got_kv, got_q, send_d, send_e)

    got_d = swap(send_d, xx)
    keep_q, got_q = part(keep_q + got_q.astype(F32), z_bit, zz, 2)
    grad_kv = keep_kv + got_kv.astype(F32)
    for mask in reversed(high):
        grad_kv = grad_kv.reshape((2, grad_kv.shape[0] // 2) + grad_kv.shape[1:])
        grad_kv = grad_kv[0] + swap(grad_kv[1].astype(BF16), mask).astype(F32)
    grad_g = jnp.stack(
        [grad_g[0], swap(after(grad_g[1], y_g), core), y_g[0], swap(y_g[1], core)]
    )
    far_u, got_d, got_q, send_e, out_parts = together(far_u, got_d, got_q, send_e, out_parts)
    out_z = swap(out_parts[1].astype(BF16), zz)

    got_e = swap(send_e, xx)
    keep_q, got_q = high_part(keep_q + got_q.astype(F32), r, high[-1], 1)
    grad_d = (keep_d + got_d.astype(F32)).reshape(outer, wide, width // 2)
    keep_d, got_d = high_part(grad_d, r, high[-1], 0)
    grad_u = jnp.stack([near_u, far_u])
    grad_u = [pick(grad_u, g ^ j, 1) for j in range(4)]
    y_u = swap(jnp.stack([grad_u[2], grad_u[3]]), yy)
    y_u, got_e, got_q, grad_g, grad_kv, keep_o = together(
        y_u, got_e, got_q, grad_g, grad_kv, keep_o
    )

    grad_e = (keep_e + got_e.astype(F32)).reshape(outer, wide, width // 2)
    keep_e, got_e = high_part(grad_e, r, high[-1], 0)
    keep_o, got_o = part(keep_o + got_o.astype(F32), x_bit, xx, 1)
    grad_kv = grad_kv[0].astype(BF16)
    y_kv = swap(jnp.stack([grad_kv[2], grad_kv[3]]), yy)
    grad_u = jnp.stack(
        [grad_u[0], swap(after(grad_u[1], y_u), core), y_u[0], swap(y_u[1], core)]
    )
    d_wq = high_rest(keep_q, got_q, r, high, 1).astype(BF16)
    d_wq = [pick(d_wq, g ^ j, 0) for j in range(4)]
    y_q = swap(jnp.stack([d_wq[2], d_wq[3]]), yy)
    y_q, y_kv, grad_u, got_o, got_d, got_e, out_z = together(
        y_q, y_kv, grad_u, got_o, got_d, got_e, out_z
    )

    keep_o, got_o = high_part(keep_o + got_o.astype(F32), r, high[-1], 0)
    c_q, cy_q = swap(after(d_wq[1], y_q), core), swap(y_q[1], core)
    d_wq = absolute([d_wq[0], c_q, y_q[0], cy_q], g)
    d_wquery = jnp.concatenate(d_wq, axis=1).astype(F32)
    grad_kv = [grad_kv[0], swap(after(grad_kv[1], y_kv), core), y_kv[0], swap(y_kv[1], core)]
    grad_kv = absolute(grad_kv, g)
    d_keys = jnp.concatenate([piece[:, :HD] for piece in grad_kv], axis=1)
    d_values = jnp.concatenate([piece[:, HD:] for piece in grad_kv], axis=1)
    output = (resid + out_parts[0] + out_z.astype(F32)).astype(BF16)
    d_wout = high_rest(keep_o, got_o, r, high, 0)
    d_wdown = jnp.concatenate(
        [high_rest(keep_d, got_d, r, high, 0), high_rest(keep_e, got_e, r, high, 0)], axis=1
    )[:chunk]

    def own_rows(value):
        return lax.dynamic_slice_in_dim(value, r * out_rows, out_rows, 0)

    gain_at = (g * reps + r) * out_rows
    gain_rows = lax.dynamic_slice_in_dim(gain_ffn, gain_at, out_rows, 0)[:, None]
    d_wgate, d_wup, d_gain_two = unpack(
        info, grad_g, grad_u, w_gate, w_up, gain_rows, outer, chunk, wide
    )
    gain_rows = lax.dynamic_slice_in_dim(gain_attn, gain_at, out_rows, 0)
    d_gain_one = jnp.sum(d_wquery * own_rows(w_query).astype(F32), axis=1) / gain_rows
    return (
        output,
        d_tokens,
        d_gain_one,
        d_gain_two[:, 0],
        d_wquery,
        d_wout,
        d_wgate,
        d_wup,
        d_wdown,
        d_keys,
        d_values,
    )


def solution(mesh):
    spread = P(BOTH, None)
    member = P("grp", None)
    in_specs = (
        spread,
        spread,
        P(),
        P(),
        member,
        member,
        member,
        member,
        member,
        spread,
        spread,
        P(),
    )
    out_specs = (
        spread,
        spread,
        P(BOTH),
        P(BOTH),
        spread,
        spread,
        spread,
        spread,
        spread,
        spread,
        spread,
    )
    return jax.shard_map(
        on_device, mesh=mesh, in_specs=in_specs, out_specs=out_specs, check_vma=False
    )
```

```python
import functools

import jax
import jax.numpy as jnp
from jax import lax
from jax.experimental import pallas as pl
from jax.experimental.pallas import tpu as pltpu
from jax.sharding import PartitionSpec as P

HD = 128
EPSILON = 1e-06
NEGATIVE = -1e30
F32 = jnp.float32
BF16 = jnp.bfloat16
BOTH = ("grp", "rep")
BRIEF = pl.CostEstimate(flops=1, transcendentals=0, bytes_accessed=1)


def swap(value, mask):
    count = lax.axis_size(BOTH)
    return lax.ppermute(value, BOTH, [(i, i ^ mask) for i in range(count)])


def after(value, *earlier):
    return lax.optimization_barrier((value,) + earlier)[0]


def together(*values):
    return lax.optimization_barrier(values)


def dot(a, b):
    return jnp.dot(a, b, preferred_element_type=F32)


def dot_t(a, b):
    return lax.dot_general(a, b, (((1,), (1,)), ((), ())), preferred_element_type=F32)


def t_dot(a, b):
    return lax.dot_general(a, b, (((0,), (0,)), ((), ())), preferred_element_type=F32)


def pick(value, index, axis):
    return lax.dynamic_index_in_dim(value, index, axis, keepdims=False)


def scatter_four_core(parts, core):
    parts = parts.reshape((2, 2) + parts.shape[1:])
    got = swap(parts[:, 1].astype(BF16), core)
    return parts[:, 0] + got.astype(F32)


def side_step(parts, to_z, to_y, rows, yy, zz):
    half = rows // 2
    for_z = [parts[2 * rows : 2 * rows + half] + to_z.astype(F32), parts[2 * rows + half :]]
    for_y = [parts[rows : rows + half], parts[rows + half : 2 * rows] + to_y.astype(F32)]
    for_z, for_y = jnp.concatenate(for_z), jnp.concatenate(for_y)
    return swap(for_z.astype(BF16), zz), swap(for_y.astype(BF16), yy)


def exchange_four(pieces, core, yy):
    from_y = swap(jnp.stack([pieces[2], pieces[3]]), yy)
    from_c = swap(pieces[1], core)
    return [pieces[0], from_c, from_y[0], swap(from_y[1], core)]


def absolute(pieces, g):
    odd, upper = (g & 1) == 1, (g >> 1) == 1
    a = jnp.where(odd, pieces[1], pieces[0])
    b = jnp.where(odd, pieces[0], pieces[1])
    c = jnp.where(odd, pieces[3], pieces[2])
    d = jnp.where(odd, pieces[2], pieces[3])
    return [
        jnp.where(upper, c, a),
        jnp.where(upper, d, b),
        jnp.where(upper, a, c),
        jnp.where(upper, b, d),
    ]


def part(value, bit, mask, axis):
    return pick(value, bit, axis).astype(F32), swap(pick(value, 1 - bit, axis).astype(BF16), mask)


def high_part(value, r, mask, axis):
    shape = value.shape
    value = value.reshape(shape[:axis] + (2, shape[axis] // 2) + shape[axis + 1 :])
    return part(value, (r & mask) // mask, mask, axis)


def high_rest(kept, got, r, high, axis):
    value = kept + got.astype(F32)
    for mask in reversed(high[:-1]):
        kept, got = high_part(value, r, mask, axis)
        value = kept + got.astype(F32)
    return jnp.squeeze(value, axis)


def ring_of(reps):
    ring = (0, 1, 3, 2)
    pairs = []
    for member in range(4):
        for k in range(4):
            for x in range(2):
                base = member * reps + x
                pairs.append((base + 2 * ring[k], base + 2 * ring[(k + 1) % 4]))
    return pairs


def ring_slots(r, reps):
    order = jnp.array((0, 1, 3, 2), jnp.int32)
    other = jnp.arange(reps, dtype=jnp.int32)
    steps = (order[r >> 1] - order[other >> 1]) & 3
    return 2 * steps + ((other ^ r) & 1)


def pack_kernel(
    outer, chunk, wide, info_ref, gate_ref, up_ref, stay_ref, core_ref, y_ref, relay_ref, held
):
    step = pl.program_id(0)
    g, bit, x = info_ref[0], (info_ref[1] >> 1) & 1, info_ref[1] & 1
    rows = gate_ref.shape[0]
    quarter = outer * 4 * chunk
    fill = jnp.zeros((rows, wide - chunk), BF16)

    for b in range(2):

        @pl.when(bit == b)
        def _():
            for which, ref in enumerate((gate_ref, up_ref)):
                block = ref[...]
                for member in range(4):
                    parts = []
                    for xd in range(2):
                        for o in range(outer):
                            at = member * quarter + (o * 4 + b * 2 + xd) * chunk
                            parts += [block[:, at : at + chunk], fill]
                    span = 2 * outer * wide
                    held[member ^ g, :, which * span : (which + 1) * span] = jnp.concatenate(
                        parts, axis=1
                    )

    stay_ref[...] = held[0]
    core_ref[...] = held[1]

    @pl.when(step // (pl.num_programs(0) // 2) == x)
    def _():
        y_ref[...] = held[2]
        relay_ref[...] = held[3]


def pack(info, w_gate, w_up, outer, chunk, wide):
    rows, width = w_gate.shape
    span = 4 * outer * wide
    steps = 8
    part = rows // steps

    def lower(i, info):
        return jnp.clip(i - (info[1] & 1) * (steps // 2), 0, steps // 2 - 1), 0

    def plain(i, info):
        return i, 0

    shape = jax.ShapeDtypeStruct((rows, span), BF16)
    small = jax.ShapeDtypeStruct((rows // 2, span), BF16)
    return pl.pallas_call(
        functools.partial(pack_kernel, outer, chunk, wide),
        grid_spec=pltpu.PrefetchScalarGridSpec(
            num_scalar_prefetch=1,
            grid=(steps,),
            in_specs=[pl.BlockSpec((part, width), plain), pl.BlockSpec((part, width), plain)],
            out_specs=[
                pl.BlockSpec((part, span), plain),
                pl.BlockSpec((part, span), plain),
                pl.BlockSpec((part, span), lower),
                pl.BlockSpec((part, span), lower),
            ],
            scratch_shapes=[pltpu.VMEM((4, part, span), BF16)],
        ),
        out_shape=[shape, shape, small, small],
        compiler_params=pltpu.CompilerParams(vmem_limit_bytes=32 << 20),
        cost_estimate=BRIEF,
        name="pack",
    )(info, w_gate, w_up)


def pack_down_kernel(outer, chunk, wide, info_ref, down_ref, out_ref):
    bit = (info_ref[1] >> 1) & 1
    block = down_ref[...]
    fill = jnp.zeros((wide - chunk, block.shape[1]), BF16)
    for b in range(2):

        @pl.when(bit == b)
        def _():
            for xd in range(2):
                for o in range(outer):
                    at = (o * 4 + b * 2 + xd) * chunk
                    piece = jnp.concatenate([block[at : at + chunk], fill], axis=0)
                    to = (xd * outer + o) * wide
                    out_ref[to : to + wide] = piece


def pack_down(info, w_down, outer, chunk, wide):
    rows, width = w_down.shape
    steps = 4
    part = width // steps
    mine = 2 * outer * wide
    return pl.pallas_call(
        functools.partial(pack_down_kernel, outer, chunk, wide),
        grid=(steps,),
        in_specs=[
            pl.BlockSpec(memory_space=pltpu.SMEM),
            pl.BlockSpec((rows, part), lambda i: (0, i)),
        ],
        out_specs=pl.BlockSpec((mine, part), lambda i: (0, i)),
        out_shape=jax.ShapeDtypeStruct((mine, width), BF16),
        compiler_params=pltpu.CompilerParams(vmem_limit_bytes=32 << 20),
        cost_estimate=BRIEF,
        name="pack_down",
    )(info, w_down)


def feed_forward_kernel(h_ref, dy_ref, gate_ref, up_ref, down_ref, hid_ref, d_gate_ref, d_up_ref):
    h = h_ref[...]
    gate = dot(h, gate_ref[...])
    upper = dot(h, up_ref[...])
    d_hidden = dot_t(dy_ref[...], down_ref[...])
    sigma = jax.nn.sigmoid(gate)
    swish = gate * sigma
    hid_ref[...] = (swish * upper).astype(BF16)
    d_up_ref[...] = (d_hidden * swish).astype(BF16)
    d_gate_ref[...] = (d_hidden * upper * (sigma + swish * (1.0 - sigma))).astype(BF16)


def feed_forward(h, dy, w_gu, wd):
    tokens, width = h.shape
    mine = wd.shape[0]
    piece = 256
    steps = mine // piece
    whole = pl.BlockSpec((tokens, width), lambda j: (0, 0))
    out = pl.BlockSpec((tokens, piece), lambda j: (0, j))
    return pl.pallas_call(
        feed_forward_kernel,
        grid=(steps,),
        in_specs=[
            whole,
            whole,
            pl.BlockSpec((width, piece), lambda j: (0, j)),
            pl.BlockSpec((width, piece), lambda j: (0, j + steps)),
            pl.BlockSpec((piece, width), lambda j: (j, 0)),
        ],
        out_specs=[out] * 3,
        out_shape=[jax.ShapeDtypeStruct((tokens, mine), BF16)] * 3,
        compiler_params=pltpu.CompilerParams(vmem_limit_bytes=48 << 20),
        name="feed_forward",
    )(h, dy, w_gu, w_gu, wd)


def inputs_grad_kernel(mine, d_gate_ref, d_up_ref, w_ref, out_ref):
    w = w_ref[...]
    out = dot_t(d_gate_ref[...], w[:, :mine]) + dot_t(d_up_ref[...], w[:, mine:])
    out_ref[...] = out.astype(BF16)


def inputs_grad_sum_kernel(
    mine, rows, d_gate_ref, d_up_ref, w_ref, other_ref, parts_ref, low_ref, upp_ref
):
    w = w_ref[...]
    out = dot_t(d_gate_ref[...], w[:, :mine]) + dot_t(d_up_ref[...], w[:, mine:])
    out = out + other_ref[...].astype(F32)
    parts_ref[...] = out[: 3 * rows]
    low_ref[...] = out[3 * rows : 3 * rows + rows // 2].astype(BF16)
    upp_ref[...] = out[3 * rows + rows // 2 :].astype(BF16)


def inputs_grad(d_gate, d_up, w_gu, other=None):
    tokens, mine = d_gate.shape
    width = w_gu.shape[0]
    piece = min(512, width)
    rows = tokens // 4
    lhs = pl.BlockSpec((tokens, mine), lambda j: (0, 0))
    in_specs = [lhs, lhs, pl.BlockSpec((piece, 2 * mine), lambda j: (j, 0))]
    out = pl.BlockSpec((tokens, piece), lambda j: (0, j))
    params = pltpu.CompilerParams(vmem_limit_bytes=48 << 20)
    if other is None:
        return pl.pallas_call(
            functools.partial(inputs_grad_kernel, mine),
            grid=(width // piece,),
            in_specs=in_specs,
            out_specs=out,
            out_shape=jax.ShapeDtypeStruct((tokens, width), BF16),
            compiler_params=params,
            name="inputs_grad",
        )(d_gate, d_up, w_gu)
    half = pl.BlockSpec((rows // 2, piece), lambda j: (0, j))
    return pl.pallas_call(
        functools.partial(inputs_grad_sum_kernel, mine, rows),
        grid=(width // piece,),
        in_specs=in_specs + [out],
        out_specs=[pl.BlockSpec((3 * rows, piece), lambda j: (0, j)), half, half],
        out_shape=[jax.ShapeDtypeStruct((3 * rows, width), F32)]
        + [jax.ShapeDtypeStruct((rows // 2, width), BF16)] * 2,
        compiler_params=params,
        name="inputs_grad_sum",
    )(d_gate, d_up, w_gu, other)


def columns_grad_kernel(
    rows, info_ref, ha, hb, ga, gb, ua, ub, send_g, send_u, keep_g, keep_u
):
    odd = (info_ref[1] & 1) == 1
    for da, db, send, keep in ((ga, gb, send_g, keep_g), (ua, ub, send_u, keep_u)):
        grad = t_dot(ha[...], da[...]) + t_dot(hb[...], db[...])
        count, width = grad.shape
        grad = grad.reshape(count // (2 * rows), 2, rows, width)
        low, upp = grad[:, 0], grad[:, 1]
        send[...] = jnp.where(odd, low, upp).astype(BF16).reshape(count // 2, width)
        keep[...] = jnp.where(odd, upp, low).reshape(count // 2, width)


def columns_grad(info, ha, hb, ga, gb, ua, ub, rows):
    tokens, width = ha.shape
    mine = ga.shape[1]
    part = min(512, width)
    half = pl.BlockSpec((part // 2, mine), lambda i: (i, 0))
    lhs = pl.BlockSpec((tokens, part), lambda i: (0, i))
    rhs = pl.BlockSpec(ga.shape, lambda i: (0, 0))
    return pl.pallas_call(
        functools.partial(columns_grad_kernel, rows),
        grid=(width // part,),
        in_specs=[pl.BlockSpec(memory_space=pltpu.SMEM), lhs, lhs, rhs, rhs, rhs, rhs],
        out_specs=[half] * 4,
        out_shape=[jax.ShapeDtypeStruct((width // 2, mine), BF16)] * 2
        + [jax.ShapeDtypeStruct((width // 2, mine), F32)] * 2,
        compiler_params=pltpu.CompilerParams(vmem_limit_bytes=56 << 20),
        name="columns_grad",
    )(info, ha, hb, ga, gb, ua, ub)


def rows_grad_kernel(info_ref, ha, hb, da, db, send_one, send_two, keep_one, keep_two):
    odd = (info_ref[1] & 1) == 1
    step = pl.program_id(0)
    first = step < pl.num_programs(0) // 2
    grad = t_dot(ha[...], da[...]) + t_dot(hb[...], db[...])
    half = grad.shape[0] // 2
    low, upp = grad[:half], grad[half:]
    send = jnp.where(odd, low, upp).astype(BF16)
    keep = jnp.where(odd, upp, low)

    @pl.when(first)
    def _():
        send_one[...] = send
        keep_one[...] = keep

    @pl.when(jnp.logical_not(first))
    def _():
        send_two[...] = send
        keep_two[...] = keep


def rows_grad(info, ha, hb, da, db):
    tokens, mine = ha.shape
    width = da.shape[1]
    part = min(512, width // 2)
    steps = width // part
    one = pl.BlockSpec((mine // 2, part), lambda i: (0, jnp.minimum(i, steps // 2 - 1)))
    two = pl.BlockSpec((mine // 2, part), lambda i: (0, jnp.maximum(i - steps // 2, 0)))
    lhs = pl.BlockSpec(ha.shape, lambda i: (0, 0))
    rhs = pl.BlockSpec((tokens, part), lambda i: (0, i))
    return pl.pallas_call(
        rows_grad_kernel,
        grid=(steps,),
        in_specs=[pl.BlockSpec(memory_space=pltpu.SMEM), lhs, lhs, rhs, rhs],
        out_specs=[one, two, one, two],
        out_shape=[jax.ShapeDtypeStruct((mine // 2, width // 2), BF16)] * 2
        + [jax.ShapeDtypeStruct((mine // 2, width // 2), F32)] * 2,
        compiler_params=pltpu.CompilerParams(vmem_limit_bytes=48 << 20),
        name="rows_grad",
    )(info, ha, hb, da, db)


def query_back_kernel(rows, d_ref, w_ref, keep_ref, send_ref):
    out = dot_t(d_ref[...], w_ref[...])
    for k in range(2):
        keep_ref[k] = out[2 * k * rows : (2 * k + 1) * rows]
        send_ref[k] = out[(2 * k + 1) * rows : (2 * k + 2) * rows].astype(BF16)


def query_back(d_query, wq, rows):
    width, share = wq.shape
    part = min(512, width)
    out = pl.BlockSpec((2, rows, part), lambda j: (0, 0, j))
    return pl.pallas_call(
        functools.partial(query_back_kernel, rows),
        grid=(width // part,),
        in_specs=[
            pl.BlockSpec(d_query.shape, lambda j: (0, 0)),
            pl.BlockSpec((part, share), lambda j: (j, 0)),
        ],
        out_specs=[out, out],
        out_shape=[
            jax.ShapeDtypeStruct((2, rows, width), F32),
            jax.ShapeDtypeStruct((2, rows, width), BF16),
        ],
        compiler_params=pltpu.CompilerParams(vmem_limit_bytes=32 << 20),
        name="query_back",
    )(d_query, wq)


def unpack_kernel(
    outer, chunk, wide, info_ref, got_g, got_u, w_gate, w_up, gain, gate_ref, up_ref, dg_ref
):
    g, bit = info_ref[0], (info_ref[1] >> 1) & 1
    total = 0.0
    for got, ref, weight in ((got_g, gate_ref, w_gate), (got_u, up_ref, w_up)):
        parts = []
        for member in range(4):
            pieces = [got[member ^ g, b ^ bit] for b in range(2)]
            for o in range(outer):
                for b in range(2):
                    for xd in range(2):
                        at = (xd * outer + o) * wide
                        parts.append(pieces[b][:, at : at + chunk])
        grad = jnp.concatenate(parts, axis=1).astype(F32)
        ref[...] = grad
        total = total + jnp.sum(grad * weight[...].astype(F32), axis=1, keepdims=True)
    dg_ref[...] = total / gain[...]


def unpack(info, got_g, got_u, w_gate, w_up, gain, outer, chunk, wide):
    rows = got_g.shape[2]
    weight = pl.BlockSpec((rows, w_gate.shape[1]), lambda i, info: (info[1], 0))
    shape = jax.ShapeDtypeStruct((rows, 16 * outer * chunk), F32)
    def whole(value):
        return pl.BlockSpec(value.shape, lambda i, info: (0,) * len(value.shape))

    outs = [shape, shape, jax.ShapeDtypeStruct((rows, 1), F32)]
    return pl.pallas_call(
        functools.partial(unpack_kernel, outer, chunk, wide),
        grid_spec=pltpu.PrefetchScalarGridSpec(
            num_scalar_prefetch=1,
            grid=(1,),
            in_specs=[whole(got_g), whole(got_u), weight, weight, whole(gain)],
            out_specs=[whole(out) for out in outs],
        ),
        out_shape=outs,
        compiler_params=pltpu.CompilerParams(vmem_limit_bytes=32 << 20),
        name="unpack",
    )(info, got_g, got_u, w_gate, w_up, gain)


def block_bounds(info_ref, starts_ref, j, reps):
    place = ((info_ref[0] ^ j) * reps + info_ref[1]) * HD
    docs = starts_ref.shape[0]
    first = jnp.int32(0)
    for d in range(docs):
        first = jnp.maximum(first, jnp.where(starts_ref[d] <= place, starts_ref[d], 0))
    position = place + lax.broadcasted_iota(jnp.int32, (4, HD, 1), 1).reshape(4 * HD, 1)
    lowest = jnp.zeros_like(position)
    for d in range(docs):
        lowest = jnp.maximum(lowest, jnp.where(starts_ref[d] <= position, starts_ref[d], 0))
    return place, first, position, lowest


def key_tile(info_ref, slots_ref, kv_ref, tile, reps):
    per = reps // 4
    member = (tile // per) ^ info_ref[0]
    base = 4 * (tile % per)
    piece = jnp.concatenate([kv_ref[slots_ref[base + k], member] for k in range(4)], axis=0)
    return piece[:, :HD], piece[:, HD:]


def head_rows(ref):
    return jnp.concatenate([ref[0, :, h * HD : (h + 1) * HD] for h in range(4)], axis=0)


def attend_kernel(reps, info_ref, slots_ref, starts_ref, q_ref, kv_ref, o_ref, lse_ref):
    j = pl.program_id(0)
    place, first, position, lowest = block_bounds(info_ref, starts_ref, j, reps)
    query = head_rows(q_ref)
    rows = 4 * HD
    scale = HD ** (-0.5)

    def step(tile, carry):
        best, total, accum = carry
        key, value = key_tile(info_ref, slots_ref, kv_ref, tile, reps)
        scores = dot_t(query, key) * scale
        at = tile * 512 + lax.broadcasted_iota(jnp.int32, (1, 512), 1)
        scores = jnp.where((at >= lowest) & (at <= position), scores, NEGATIVE)
        new_best = jnp.maximum(best, jnp.max(scores, axis=1, keepdims=True))
        weights = jnp.exp(scores - new_best)
        factor = jnp.exp(best - new_best)
        total = total * factor + jnp.sum(weights, axis=1, keepdims=True)
        accum = accum * factor + dot(weights.astype(BF16), value)
        return new_best, total, accum

    init = (
        jnp.full((rows, 1), NEGATIVE, F32),
        jnp.zeros((rows, 1), F32),
        jnp.zeros((rows, HD), F32),
    )
    best, total, accum = lax.fori_loop(first // 512, place // 512 + 1, step, init)
    out = accum / total
    for h in range(4):
        o_ref[0, :, h * HD : (h + 1) * HD] = out[h * HD : (h + 1) * HD].astype(BF16)
    lse_ref[0] = best + jnp.log(total)


def attend(info, slots, starts, query, kv):
    reps = kv.shape[0]
    return pl.pallas_call(
        functools.partial(attend_kernel, reps),
        grid=(4,),
        in_specs=[
            pl.BlockSpec(memory_space=pltpu.SMEM),
            pl.BlockSpec(memory_space=pltpu.SMEM),
            pl.BlockSpec(memory_space=pltpu.SMEM),
            pl.BlockSpec((1, HD, 4 * HD), lambda j: (j, 0, 0)),
            pl.BlockSpec(kv.shape, lambda j: (0, 0, 0, 0)),
        ],
        out_specs=[
            pl.BlockSpec((1, HD, 4 * HD), lambda j: (j, 0, 0)),
            pl.BlockSpec((1, 4 * HD, 1), lambda j: (j, 0, 0)),
        ],
        out_shape=[
            jax.ShapeDtypeStruct((4, HD, 4 * HD), BF16),
            jax.ShapeDtypeStruct((4, 4 * HD, 1), F32),
        ],
        compiler_params=pltpu.CompilerParams(vmem_limit_bytes=48 << 20),
        cost_estimate=BRIEF,
        name="attend",
    )(info, slots, starts, query, kv)


def attend_back_kernel(
    reps,
    info_ref,
    slots_ref,
    starts_ref,
    q_ref,
    do_ref,
    o_ref,
    lse_ref,
    kv_ref,
    dq_ref,
    keep_ref,
    send_ref,
    sums,
):
    j = pl.program_id(0)

    @pl.when(j == 0)
    def _():
        sums[...] = jnp.zeros_like(sums)

    place, first, position, lowest = block_bounds(info_ref, starts_ref, j, reps)
    query = head_rows(q_ref)
    d_out = head_rows(do_ref)
    out = head_rows(o_ref)
    lse = lse_ref[0]
    delta = jnp.sum(d_out.astype(F32) * out.astype(F32), axis=1, keepdims=True)
    scale = HD ** (-0.5)
    per = reps // 4

    def step(tile, d_query):
        key, value = key_tile(info_ref, slots_ref, kv_ref, tile, reps)
        scores = dot_t(query, key) * scale
        at = tile * 512 + lax.broadcasted_iota(jnp.int32, (1, 512), 1)
        probs = jnp.where((at >= lowest) & (at <= position), jnp.exp(scores - lse), 0.0)
        d_probs = dot_t(d_out, value)
        d_scores = (probs * (d_probs - delta)).astype(BF16)
        d_query = d_query + dot(d_scores, key)
        d_key = t_dot(d_scores, query) * scale
        d_value = t_dot(probs.astype(BF16), d_out)
        member = (tile // per) ^ info_ref[0]
        both = jnp.concatenate([d_key, d_value], axis=1)
        for k in range(4):
            slot = (4 * (tile % per) + k) ^ info_ref[1]
            sums[slot, member] = sums[slot, member] + both[k * HD : (k + 1) * HD]
        return d_query

    d_query = lax.fori_loop(
        first // 512, place // 512 + 1, step, jnp.zeros((4 * HD, HD), F32)
    )
    d_query = (d_query * scale).astype(BF16)
    for h in range(4):
        dq_ref[0, :, h * HD : (h + 1) * HD] = d_query[h * HD : (h + 1) * HD]

    @pl.when(j == 3)
    def _():
        for slot in range(reps // 2):
            keep_ref[slot] = sums[2 * slot].astype(BF16)
            send_ref[slot] = sums[2 * slot + 1].astype(BF16)


def attend_back(info, slots, starts, query, d_out, out, lse, kv):
    reps = kv.shape[0]
    rows = pl.BlockSpec((1, HD, 4 * HD), lambda j: (j, 0, 0))
    whole = pl.BlockSpec(kv.shape, lambda j: (0, 0, 0, 0))
    half = pl.BlockSpec((reps // 2,) + kv.shape[1:], lambda j: (0, 0, 0, 0))
    return pl.pallas_call(
        functools.partial(attend_back_kernel, reps),
        grid=(4,),
        in_specs=[
            pl.BlockSpec(memory_space=pltpu.SMEM),
            pl.BlockSpec(memory_space=pltpu.SMEM),
            pl.BlockSpec(memory_space=pltpu.SMEM),
            rows,
            rows,
            rows,
            pl.BlockSpec((1, 4 * HD, 1), lambda j: (j, 0, 0)),
            whole,
        ],
        out_specs=[rows, half, half],
        out_shape=[jax.ShapeDtypeStruct((4, HD, 4 * HD), BF16)]
        + [jax.ShapeDtypeStruct((reps // 2,) + kv.shape[1:], BF16)] * 2,
        scratch_shapes=[pltpu.VMEM(kv.shape, F32)],
        compiler_params=pltpu.CompilerParams(vmem_limit_bytes=60 << 20),
        cost_estimate=BRIEF,
        name="attend_back",
    )(info, slots, starts, query, d_out, out, lse, kv)


def on_device(
    tokens,
    cotangent,
    gain_attn,
    gain_ffn,
    w_query,
    w_out,
    w_gate,
    w_up,
    w_down,
    keys,
    values,
    starts,
):
    reps = lax.axis_size("rep")
    rows, width = tokens.shape
    hidden_all = w_gate.shape[1]
    g = lax.axis_index("grp")
    r = lax.axis_index("rep")
    core, yy, xx, zz = reps, 2 * reps, 1, 2
    high = [1 << k for k in range(2, 16) if (1 << k) < reps]
    outer = reps // 4
    x_bit, z_bit = r & 1, (r >> 1) & 1
    share = width // 4
    out_rows = width // (4 * reps)
    chunk = hidden_all // (4 * reps)
    wide = -(-(2 * outer * chunk) // 256) * 256 // (2 * outer)
    mine = 2 * outer * wide
    info = jnp.stack([g, r]).astype(jnp.int32)

    kv_parts = [
        jnp.concatenate(
            [
                lax.dynamic_slice_in_dim(keys, (g ^ j) * HD, HD, 1),
                lax.dynamic_slice_in_dim(values, (g ^ j) * HD, HD, 1),
            ],
            axis=1,
        )
        for j in range(4)
    ]
    kv_y = swap(jnp.stack([kv_parts[2], kv_parts[3]]), yy)
    kv_own = jnp.stack([kv_parts[0], swap(kv_parts[1], core), kv_y[0], swap(kv_y[1], core)])

    x_full = tokens.astype(F32)
    inv_one = lax.rsqrt(jnp.mean(x_full * x_full, axis=1, keepdims=True) + EPSILON)
    normed_one = x_full * inv_one
    h_one = (normed_one * gain_attn).astype(BF16)

    h_y = swap(after(h_one, kv_y), yy)
    wq_half = share // 2
    wq_y = jnp.stack(
        [
            lax.dynamic_slice(w_query, (x_bit * wq_half, (g ^ j) * share), (wq_half, share))
            for j in (2, 3)
        ]
    )
    wd = pack_down(info, w_down, outer, chunk, wide)
    if reps == 8:
        pairs = ring_of(reps)
        one = lax.ppermute(kv_own, BOTH, pairs)
        zero_x = swap(kv_own, xx)
        wq_y = swap(after(wq_y, kv_own), yy)
        one, h_y, wd, zero_x = together(one, h_y, wd, zero_x)
        stay, to_core, to_y, relay = pack(after(info, one), w_gate, w_up, outer, chunk, wide)
        two = lax.ppermute(one, BOTH, pairs)
        one_x = swap(one, xx)
        two, wq_y, stay, one_x = together(two, wq_y, stay, one_x)
        three = lax.ppermute(two, BOTH, pairs)
        wq_x = swap(wq_y, xx)
        two_x = swap(two, xx)
        dy_y = swap(after(cotangent, two), yy)
        three, two_x = together(three, two_x)
        three_x = swap(three, xx)
        three_x, wq_x, dy_y = together(three_x, wq_x, dy_y)
        kv = jnp.stack([kv_own, zero_x, one, one_x, two, two_x, three, three_x])
        slots = ring_slots(r, reps)
        relay = swap(after(relay, wq_y), yy)
    else:
        stay, to_core, to_y, relay = pack(info, w_gate, w_up, outer, chunk, wide)
        wq_y, dy_y, relay = swap(wq_y, yy), swap(cotangent, yy), swap(relay, yy)
        wq_x = swap(wq_y, xx)
        kv = lax.all_gather(kv_own, "rep", axis=0, tiled=False)
        slots = jnp.arange(reps, dtype=jnp.int32)

    h_group = jnp.stack([h_one, swap(h_one, core), h_y, swap(h_y, core)])
    h_group = h_group.reshape(4 * rows, width)
    upper_half = x_bit == 1
    wq_y = jnp.concatenate(
        [jnp.where(upper_half, wq_x, wq_y), jnp.where(upper_half, wq_y, wq_x)], axis=1
    )
    wq_parts = [
        lax.dynamic_slice_in_dim(w_query, g * share, share, 1),
        swap(lax.dynamic_slice_in_dim(w_query, (g ^ 1) * share, share, 1), core),
        wq_y[0],
        swap(wq_y[1], core),
    ]
    wq_cols = jnp.concatenate(absolute(wq_parts, g), axis=0)
    query = dot(h_group, wq_cols).astype(BF16).reshape(4, rows, share)

    dy_near = jnp.stack([cotangent, dy_y])
    dy_far = swap(dy_near, zz)
    attn, lse = attend(info, slots, starts, query, kv)
    attn, lse, relay = together(attn, lse, relay)
    from_y = swap(after(to_y, relay), yy)
    relay_x = swap(relay, xx)
    attn_rows = attn.reshape(4 * rows, share)
    branch = scatter_four_core(dot(attn_rows, w_out).reshape(4, rows, width), core)
    from_branch = swap(branch[1].astype(BF16), yy)
    from_branch, from_y = together(from_branch, from_y)
    resid = x_full + branch[0] + from_branch.astype(F32)
    inv_two = lax.rsqrt(jnp.mean(resid * resid, axis=1, keepdims=True) + EPSILON)
    normed_two = resid * inv_two
    h_two = (normed_two * gain_ffn).astype(BF16)

    h_y, h_z = swap(h_two, yy), swap(h_two, zz)
    from_y_x = swap(from_y, xx)
    h_y, h_z, relay_x = together(h_y, h_z, relay_x)
    low, upp = swap(h_y[: rows // 2], zz), swap(h_z[rows // 2 :], yy)
    low, upp, from_y_x, dy_far = together(low, upp, from_y_x, dy_far)
    h_a = jnp.concatenate([h_two, h_y, h_z, low, upp])
    h_b = swap(h_a, core)
    dy_a = jnp.stack([dy_near, dy_far]).reshape(4 * rows, width)
    dy_b = swap(dy_a, core)
    diagonal, diagonal_x = swap(relay, core), swap(relay_x, core)
    w_gu = jnp.concatenate(
        absolute(
            [
                stay,
                swap(to_core, core),
                jnp.concatenate(
                    [
                        jnp.where(upper_half, from_y_x, from_y),
                        jnp.where(upper_half, from_y, from_y_x),
                    ]
                ),
                jnp.concatenate(
                    [
                        jnp.where(upper_half, diagonal_x, diagonal),
                        jnp.where(upper_half, diagonal, diagonal_x),
                    ]
                ),
            ],
            g,
        ),
        axis=0,
    )

    hidden_b, d_gate_b, d_up_b = feed_forward(h_b, dy_b, w_gu, wd)
    from_core = swap(inputs_grad(d_gate_b, d_up_b, w_gu), core)
    hidden_a, d_gate_a, d_up_a = feed_forward(h_a, after(dy_a, d_up_b), w_gu, wd)
    d_h_parts, corner_low, corner_upp = inputs_grad(d_gate_a, d_up_a, w_gu, from_core)

    to_z, to_y = swap(corner_low, yy), swap(corner_upp, zz)
    send_g, send_u, keep_g, keep_u = columns_grad(
        after(info, d_h_parts), h_a, h_b, d_gate_a, d_gate_b, d_up_a, d_up_b, out_rows
    )
    to_z, to_y, send_g = together(to_z, to_y, send_g)
    got_g = swap(send_g, xx)
    from_z, from_y = side_step(d_h_parts, to_z, to_y, rows, yy, zz)
    out_core = swap(dot(after(hidden_b, to_z), wd).astype(BF16), core)
    send_d, send_e, keep_d, keep_e = rows_grad(
        after(info, to_z), hidden_a, hidden_b, dy_a, dy_b
    )
    out_parts = dot(after(hidden_a, to_z), wd)
    from_z, from_y, out_core, send_d, out_parts = together(
        from_z, from_y, out_core, send_d, out_parts
    )
    d_h_two = d_h_parts[:rows] + from_z.astype(F32) + from_y.astype(F32)
    scaled_two = d_h_two * gain_ffn
    d_resid = cotangent.astype(F32) + inv_two * (
        scaled_two - normed_two * jnp.mean(scaled_two * normed_two, axis=1, keepdims=True)
    )
    da_own = d_resid.astype(BF16)
    da_y, da_c = swap(da_own, yy), swap(da_own, core)
    out_parts = (out_parts + out_core.astype(F32)).reshape(2, 2, rows, width)
    da_y, da_c = together(da_y, da_c)
    d_group = jnp.stack([da_own, da_c, da_y, swap(da_y, core)]).reshape(4 * rows, width)
    d_group, got_g = together(d_group, got_g)

    got_u = swap(after(send_u, got_g), xx)
    grad_g = (keep_g + got_g.astype(F32)).reshape(4, outer, 2, out_rows, mine)
    keep_g, got_g = high_part(grad_g, r, high[-1], 1)
    d_attn = dot_t(d_group, w_out).astype(BF16).reshape(4, rows, share)
    grad_o = t_dot(attn_rows, d_group).reshape(outer, 2, 2, out_rows, width)
    keep_o, got_o = part(grad_o, z_bit, zz, 1)
    out_y = swap(after(out_parts, d_group)[:, 1].astype(BF16), yy)
    d_query, keep_kv, send_kv = attend_back(info, slots, starts, query, d_attn, attn, lse, kv)
    d_query, send_kv, got_u, out_y = together(d_query, send_kv, got_u, out_y)

    got_kv = swap(send_kv, xx)
    grad_u = (keep_u + got_u.astype(F32)).reshape(4, outer, 2, out_rows, mine)
    keep_u, got_u = high_part(grad_u, r, high[-1], 1)
    d_query = d_query.reshape(4 * rows, share)
    d_h_one, send_h = query_back(d_query, wq_cols, rows)
    got_h = swap(send_h, core)
    d_wq = t_dot(h_group, d_query).reshape(4, outer, 2, 2, out_rows, share)
    out_parts = out_parts[:, 0] + out_y.astype(F32)
    got_h, got_g, d_wq = together(got_h, got_g, d_wq)

    d_h_one = d_h_one + got_h.astype(F32)
    from_h = swap(d_h_one[1].astype(BF16), yy)
    grad_g = high_rest(keep_g, got_g, r, high, 1).astype(BF16)
    near_g, far_g = pick(grad_g, z_bit, 1), swap(pick(grad_g, 1 - z_bit, 1), zz)
    got_kv, d_wq = together(got_kv, d_wq)

    keep_q, got_q = part(d_wq, x_bit, xx, 3)
    grad_kv = keep_kv.astype(F32) + got_kv.astype(F32)
    grad_kv = grad_kv.reshape((outer, 2) + grad_kv.shape[1:])
    keep_kv, got_kv = grad_kv[:, 0], swap(grad_kv[:, 1].astype(BF16), zz)
    from_h, far_g, got_u, got_o = together(from_h, far_g, got_u, got_o)

    d_h_one = d_h_one[0] + from_h.astype(F32)
    scaled_one = d_h_one * gain_attn
    d_tokens = (
        d_resid
        + inv_one
        * (scaled_one - normed_one * jnp.mean(scaled_one * normed_one, axis=1, keepdims=True))
    ).astype(BF16)
    grad_g = jnp.stack([near_g, far_g])
    grad_g = [pick(grad_g, g ^ j, 1) for j in range(4)]
    y_g = swap(jnp.stack([grad_g[2], grad_g[3]]), yy)
    grad_u = high_rest(keep_u, got_u, r, high, 1).astype(BF16)
    near_u, far_u = pick(grad_u, z_bit, 1), swap(pick(grad_u, 1 - z_bit, 1), zz)
    y_g, got_kv, got_q, send_d, send_e = together(y_g, got_kv, got_q, send_d, send_e)

    got_d = swap(send_d, xx)
    keep_q, got_q = part(keep_q + got_q.astype(F32), z_bit, zz, 2)
    grad_kv = keep_kv + got_kv.astype(F32)
    for mask in reversed(high):
        grad_kv = grad_kv.reshape((2, grad_kv.shape[0] // 2) + grad_kv.shape[1:])
        grad_kv = grad_kv[0] + swap(grad_kv[1].astype(BF16), mask).astype(F32)
    grad_g = jnp.stack(
        [grad_g[0], swap(after(grad_g[1], y_g), core), y_g[0], swap(y_g[1], core)]
    )
    far_u, got_d, got_q, send_e, out_parts = together(far_u, got_d, got_q, send_e, out_parts)
    out_z = swap(out_parts[1].astype(BF16), zz)

    got_e = swap(send_e, xx)
    keep_q, got_q = high_part(keep_q + got_q.astype(F32), r, high[-1], 1)
    grad_d = (keep_d + got_d.astype(F32)).reshape(outer, wide, width // 2)
    keep_d, got_d = high_part(grad_d, r, high[-1], 0)
    grad_u = jnp.stack([near_u, far_u])
    grad_u = [pick(grad_u, g ^ j, 1) for j in range(4)]
    y_u = swap(jnp.stack([grad_u[2], grad_u[3]]), yy)
    y_u, got_e, got_q, grad_g, grad_kv, keep_o = together(
        y_u, got_e, got_q, grad_g, grad_kv, keep_o
    )

    grad_e = (keep_e + got_e.astype(F32)).reshape(outer, wide, width // 2)
    keep_e, got_e = high_part(grad_e, r, high[-1], 0)
    keep_o, got_o = part(keep_o + got_o.astype(F32), x_bit, xx, 1)
    grad_kv = grad_kv[0].astype(BF16)
    y_kv = swap(jnp.stack([grad_kv[2], grad_kv[3]]), yy)
    grad_u = jnp.stack(
        [grad_u[0], swap(after(grad_u[1], y_u), core), y_u[0], swap(y_u[1], core)]
    )
    d_wq = high_rest(keep_q, got_q, r, high, 1).astype(BF16)
    d_wq = [pick(d_wq, g ^ j, 0) for j in range(4)]
    y_q = swap(jnp.stack([d_wq[2], d_wq[3]]), yy)
    y_q, y_kv, grad_u, got_o, got_d, got_e, out_z = together(
        y_q, y_kv, grad_u, got_o, got_d, got_e, out_z
    )

    keep_o, got_o = high_part(keep_o + got_o.astype(F32), r, high[-1], 0)
    c_q, cy_q = swap(after(d_wq[1], y_q), core), swap(y_q[1], core)
    d_wq = absolute([d_wq[0], c_q, y_q[0], cy_q], g)
    d_wquery = jnp.concatenate(d_wq, axis=1).astype(F32)
    grad_kv = [grad_kv[0], swap(after(grad_kv[1], y_kv), core), y_kv[0], swap(y_kv[1], core)]
    grad_kv = absolute(grad_kv, g)
    d_keys = jnp.concatenate([piece[:, :HD] for piece in grad_kv], axis=1)
    d_values = jnp.concatenate([piece[:, HD:] for piece in grad_kv], axis=1)
    output = (resid + out_parts[0] + out_z.astype(F32)).astype(BF16)
    d_wout = high_rest(keep_o, got_o, r, high, 0)
    d_wdown = jnp.concatenate(
        [high_rest(keep_d, got_d, r, high, 0), high_rest(keep_e, got_e, r, high, 0)], axis=1
    )[:chunk]

    def own_rows(value):
        return lax.dynamic_slice_in_dim(value, r * out_rows, out_rows, 0)

    gain_at = (g * reps + r) * out_rows
    gain_rows = lax.dynamic_slice_in_dim(gain_ffn, gain_at, out_rows, 0)[:, None]
    d_wgate, d_wup, d_gain_two = unpack(
        info, grad_g, grad_u, w_gate, w_up, gain_rows, outer, chunk, wide
    )
    gain_rows = lax.dynamic_slice_in_dim(gain_attn, gain_at, out_rows, 0)
    d_gain_one = jnp.sum(d_wquery * own_rows(w_query).astype(F32), axis=1) / gain_rows
    return (
        output,
        d_tokens,
        d_gain_one,
        d_gain_two[:, 0],
        d_wquery,
        d_wout,
        d_wgate,
        d_wup,
        d_wdown,
        d_keys,
        d_values,
    )


def solution(mesh):
    spread = P(BOTH, None)
    member = P("grp", None)
    in_specs = (
        spread,
        spread,
        P(),
        P(),
        member,
        member,
        member,
        member,
        member,
        spread,
        spread,
        P(),
    )
    out_specs = (
        spread,
        spread,
        P(BOTH),
        P(BOTH),
        spread,
        spread,
        spread,
        spread,
        spread,
        spread,
        spread,
    )
    return jax.shard_map(
        on_device, mesh=mesh, in_specs=in_specs, out_specs=out_specs, check_vma=False
    )
```

```python
import functools

import jax
import jax.numpy as jnp
from jax import lax
from jax.experimental import pallas as pl
from jax.experimental.pallas import tpu as pltpu
from jax.sharding import PartitionSpec as P

HD = 128
EPSILON = 1e-06
NEGATIVE = -1e30
F32 = jnp.float32
BF16 = jnp.bfloat16
BOTH = ("grp", "rep")
TILE = 4


def swap(value, mask):
    count = lax.axis_size(BOTH)
    return lax.ppermute(value, BOTH, [(i, i ^ mask) for i in range(count)])


def after(value, *earlier):
    return lax.optimization_barrier((value,) + earlier)[0]


def together(*values):
    return lax.optimization_barrier(values)


def dot(a, b):
    return jnp.dot(a, b, preferred_element_type=F32)


def dot_t(a, b):
    return lax.dot_general(a, b, (((1,), (1,)), ((), ())), preferred_element_type=F32)


def t_dot(a, b):
    return lax.dot_general(a, b, (((0,), (0,)), ((), ())), preferred_element_type=F32)


def pick(value, index, axis):
    return lax.dynamic_index_in_dim(value, index, axis, keepdims=False)


def scatter_four_core(parts, core):
    parts = parts.reshape((2, 2) + parts.shape[1:])
    got = swap(parts[:, 1].astype(BF16), core)
    return parts[:, 0] + got.astype(F32)


def side_step(parts, to_z, to_y, rows, yy, zz):
    half = rows // 2
    for_z = [parts[2 * rows : 2 * rows + half] + to_z.astype(F32), parts[2 * rows + half :]]
    for_y = [parts[rows : rows + half], parts[rows + half : 2 * rows] + to_y.astype(F32)]
    for_z, for_y = jnp.concatenate(for_z), jnp.concatenate(for_y)
    return swap(for_z.astype(BF16), zz), swap(for_y.astype(BF16), yy)


def exchange_four(pieces, core, yy):
    from_y = swap(jnp.stack([pieces[2], pieces[3]]), yy)
    from_c = swap(pieces[1], core)
    return [pieces[0], from_c, from_y[0], swap(from_y[1], core)]


def absolute(pieces, g):
    odd, upper = (g & 1) == 1, (g >> 1) == 1
    a = jnp.where(odd, pieces[1], pieces[0])
    b = jnp.where(odd, pieces[0], pieces[1])
    c = jnp.where(odd, pieces[3], pieces[2])
    d = jnp.where(odd, pieces[2], pieces[3])
    return [
        jnp.where(upper, c, a),
        jnp.where(upper, d, b),
        jnp.where(upper, a, c),
        jnp.where(upper, b, d),
    ]


def part(value, bit, mask, axis):
    return pick(value, bit, axis).astype(F32), swap(pick(value, 1 - bit, axis).astype(BF16), mask)


def high_part(value, r, mask, axis):
    shape = value.shape
    value = value.reshape(shape[:axis] + (2, shape[axis] // 2) + shape[axis + 1 :])
    return part(value, (r & mask) // mask, mask, axis)


def high_rest(kept, got, r, high, axis):
    value = kept + got.astype(F32)
    for mask in reversed(high[:-1]):
        kept, got = high_part(value, r, mask, axis)
        value = kept + got.astype(F32)
    return jnp.squeeze(value, axis)


def ring_of(reps):
    ring = (0, 1, 3, 2)
    pairs = []
    for member in range(4):
        for k in range(4):
            for x in range(2):
                base = member * reps + x
                pairs.append((base + 2 * ring[k], base + 2 * ring[(k + 1) % 4]))
    return pairs


def ring_slots(r, reps):
    order = jnp.array((0, 1, 3, 2), jnp.int32)
    other = jnp.arange(reps, dtype=jnp.int32)
    steps = (order[r >> 1] - order[other >> 1]) & 3
    return 2 * steps + ((other ^ r) & 1)


def pack_kernel(
    outer, chunk, wide, info_ref, gate_ref, up_ref, stay_ref, core_ref, y_ref, relay_ref, held
):
    step = pl.program_id(0)
    g, bit, x = info_ref[0], (info_ref[1] >> 1) & 1, info_ref[1] & 1
    rows = gate_ref.shape[0]
    quarter = outer * 4 * chunk
    fill = jnp.zeros((rows, wide - chunk), BF16)

    for b in range(2):

        @pl.when(bit == b)
        def _():
            for which, ref in enumerate((gate_ref, up_ref)):
                block = ref[...]
                for member in range(4):
                    parts = []
                    for xd in range(2):
                        for o in range(outer):
                            at = member * quarter + (o * 4 + b * 2 + xd) * chunk
                            parts += [block[:, at : at + chunk], fill]
                    span = 2 * outer * wide
                    held[member ^ g, :, which * span : (which + 1) * span] = jnp.concatenate(
                        parts, axis=1
                    )

    stay_ref[...] = held[0]
    core_ref[...] = held[1]

    @pl.when(step // (pl.num_programs(0) // 2) == x)
    def _():
        y_ref[...] = held[2]
        relay_ref[...] = held[3]


def pack(info, w_gate, w_up, outer, chunk, wide):
    rows, width = w_gate.shape
    span = 4 * outer * wide
    steps = 8
    part = rows // steps

    def lower(i, info):
        return jnp.clip(i - (info[1] & 1) * (steps // 2), 0, steps // 2 - 1), 0

    def plain(i, info):
        return i, 0

    shape = jax.ShapeDtypeStruct((rows, span), BF16)
    small = jax.ShapeDtypeStruct((rows // 2, span), BF16)
    return pl.pallas_call(
        functools.partial(pack_kernel, outer, chunk, wide),
        grid_spec=pltpu.PrefetchScalarGridSpec(
            num_scalar_prefetch=1,
            grid=(steps,),
            in_specs=[pl.BlockSpec((part, width), plain), pl.BlockSpec((part, width), plain)],
            out_specs=[
                pl.BlockSpec((part, span), plain),
                pl.BlockSpec((part, span), plain),
                pl.BlockSpec((part, span), lower),
                pl.BlockSpec((part, span), lower),
            ],
            scratch_shapes=[pltpu.VMEM((4, part, span), BF16)],
        ),
        out_shape=[shape, shape, small, small],
        compiler_params=pltpu.CompilerParams(vmem_limit_bytes=32 << 20),
        name="pack",
    )(info, w_gate, w_up)


def pack_down_kernel(outer, chunk, wide, info_ref, down_ref, out_ref):
    bit = (info_ref[1] >> 1) & 1
    block = down_ref[...]
    fill = jnp.zeros((wide - chunk, block.shape[1]), BF16)
    for b in range(2):

        @pl.when(bit == b)
        def _():
            for xd in range(2):
                for o in range(outer):
                    at = (o * 4 + b * 2 + xd) * chunk
                    piece = jnp.concatenate([block[at : at + chunk], fill], axis=0)
                    to = (xd * outer + o) * wide
                    out_ref[to : to + wide] = piece


def pack_down(info, w_down, outer, chunk, wide):
    rows, width = w_down.shape
    steps = 4
    part = width // steps
    mine = 2 * outer * wide
    return pl.pallas_call(
        functools.partial(pack_down_kernel, outer, chunk, wide),
        grid=(steps,),
        in_specs=[
            pl.BlockSpec(memory_space=pltpu.SMEM),
            pl.BlockSpec((rows, part), lambda i: (0, i)),
        ],
        out_specs=pl.BlockSpec((mine, part), lambda i: (0, i)),
        out_shape=jax.ShapeDtypeStruct((mine, width), BF16),
        compiler_params=pltpu.CompilerParams(vmem_limit_bytes=32 << 20),
        name="pack_down",
    )(info, w_down)


def feed_forward_kernel(h_ref, dy_ref, gate_ref, up_ref, down_ref, hid_ref, d_gate_ref, d_up_ref):
    h = h_ref[...]
    gate = dot(h, gate_ref[...])
    upper = dot(h, up_ref[...])
    d_hidden = dot_t(dy_ref[...], down_ref[...])
    sigma = jax.nn.sigmoid(gate)
    swish = gate * sigma
    hid_ref[...] = (swish * upper).astype(BF16)
    d_up_ref[...] = (d_hidden * swish).astype(BF16)
    d_gate_ref[...] = (d_hidden * upper * (sigma + swish * (1.0 - sigma))).astype(BF16)


def feed_forward(h, dy, w_gu, wd):
    tokens, width = h.shape
    mine = wd.shape[0]
    piece = 256
    steps = mine // piece
    whole = pl.BlockSpec((tokens, width), lambda j: (0, 0))
    out = pl.BlockSpec((tokens, piece), lambda j: (0, j))
    return pl.pallas_call(
        feed_forward_kernel,
        grid=(steps,),
        in_specs=[
            whole,
            whole,
            pl.BlockSpec((width, piece), lambda j: (0, j)),
            pl.BlockSpec((width, piece), lambda j: (0, j + steps)),
            pl.BlockSpec((piece, width), lambda j: (j, 0)),
        ],
        out_specs=[out] * 3,
        out_shape=[jax.ShapeDtypeStruct((tokens, mine), BF16)] * 3,
        compiler_params=pltpu.CompilerParams(vmem_limit_bytes=48 << 20),
        name="feed_forward",
    )(h, dy, w_gu, w_gu, wd)


def inputs_grad_kernel(mine, d_gate_ref, d_up_ref, w_ref, out_ref):
    w = w_ref[...]
    out = dot_t(d_gate_ref[...], w[:, :mine]) + dot_t(d_up_ref[...], w[:, mine:])
    out_ref[...] = out.astype(BF16)


def inputs_grad_sum_kernel(
    mine, rows, d_gate_ref, d_up_ref, w_ref, other_ref, parts_ref, low_ref, upp_ref
):
    w = w_ref[...]
    out = dot_t(d_gate_ref[...], w[:, :mine]) + dot_t(d_up_ref[...], w[:, mine:])
    out = out + other_ref[...].astype(F32)
    parts_ref[...] = out[: 3 * rows]
    low_ref[...] = out[3 * rows : 3 * rows + rows // 2].astype(BF16)
    upp_ref[...] = out[3 * rows + rows // 2 :].astype(BF16)


def inputs_grad(d_gate, d_up, w_gu, other=None):
    tokens, mine = d_gate.shape
    width = w_gu.shape[0]
    piece = min(512, width)
    rows = tokens // 4
    lhs = pl.BlockSpec((tokens, mine), lambda j: (0, 0))
    in_specs = [lhs, lhs, pl.BlockSpec((piece, 2 * mine), lambda j: (j, 0))]
    out = pl.BlockSpec((tokens, piece), lambda j: (0, j))
    params = pltpu.CompilerParams(vmem_limit_bytes=48 << 20)
    if other is None:
        return pl.pallas_call(
            functools.partial(inputs_grad_kernel, mine),
            grid=(width // piece,),
            in_specs=in_specs,
            out_specs=out,
            out_shape=jax.ShapeDtypeStruct((tokens, width), BF16),
            compiler_params=params,
            name="inputs_grad",
        )(d_gate, d_up, w_gu)
    half = pl.BlockSpec((rows // 2, piece), lambda j: (0, j))
    return pl.pallas_call(
        functools.partial(inputs_grad_sum_kernel, mine, rows),
        grid=(width // piece,),
        in_specs=in_specs + [out],
        out_specs=[pl.BlockSpec((3 * rows, piece), lambda j: (0, j)), half, half],
        out_shape=[jax.ShapeDtypeStruct((3 * rows, width), F32)]
        + [jax.ShapeDtypeStruct((rows // 2, width), BF16)] * 2,
        compiler_params=params,
        name="inputs_grad_sum",
    )(d_gate, d_up, w_gu, other)


def columns_grad_kernel(
    rows, info_ref, ha, hb, ga, gb, ua, ub, send_g, send_u, keep_g, keep_u
):
    odd = (info_ref[1] & 1) == 1
    for da, db, send, keep in ((ga, gb, send_g, keep_g), (ua, ub, send_u, keep_u)):
        grad = t_dot(ha[...], da[...]) + t_dot(hb[...], db[...])
        count, width = grad.shape
        grad = grad.reshape(count // (2 * rows), 2, rows, width)
        low, upp = grad[:, 0], grad[:, 1]
        send[...] = jnp.where(odd, low, upp).astype(BF16).reshape(count // 2, width)
        keep[...] = jnp.where(odd, upp, low).reshape(count // 2, width)


def columns_grad(info, ha, hb, ga, gb, ua, ub, rows):
    tokens, width = ha.shape
    mine = ga.shape[1]
    part = min(512, width)
    half = pl.BlockSpec((part // 2, mine), lambda i: (i, 0))
    lhs = pl.BlockSpec((tokens, part), lambda i: (0, i))
    rhs = pl.BlockSpec(ga.shape, lambda i: (0, 0))
    return pl.pallas_call(
        functools.partial(columns_grad_kernel, rows),
        grid=(width // part,),
        in_specs=[pl.BlockSpec(memory_space=pltpu.SMEM), lhs, lhs, rhs, rhs, rhs, rhs],
        out_specs=[half] * 4,
        out_shape=[jax.ShapeDtypeStruct((width // 2, mine), BF16)] * 2
        + [jax.ShapeDtypeStruct((width // 2, mine), F32)] * 2,
        compiler_params=pltpu.CompilerParams(vmem_limit_bytes=56 << 20),
        name="columns_grad",
    )(info, ha, hb, ga, gb, ua, ub)


def rows_grad_kernel(
    outer, used, info_ref, ha, hb, da, db, send_one, send_two, keep_one, keep_two
):
    odd = (info_ref[1] & 1) == 1
    step = pl.program_id(0)
    first = step < pl.num_programs(0) // 2
    grad = t_dot(ha[...], da[...]) + t_dot(hb[...], db[...])
    wide = grad.shape[0] // (2 * outer)
    halves = []
    for x in range(2):
        at = [(x * outer + o) * wide for o in range(outer)]
        halves.append(jnp.concatenate([grad[a : a + used] for a in at], axis=0))
    send = jnp.where(odd, halves[0], halves[1]).astype(BF16)
    keep = jnp.where(odd, halves[1], halves[0])

    @pl.when(first)
    def _():
        send_one[...] = send
        keep_one[...] = keep

    @pl.when(jnp.logical_not(first))
    def _():
        send_two[...] = send
        keep_two[...] = keep


def rows_grad(info, ha, hb, da, db, outer, used):
    count = outer * used
    tokens, mine = ha.shape
    width = da.shape[1]
    part = min(512, width // 2)
    steps = width // part
    one = pl.BlockSpec((count, part), lambda i: (0, jnp.minimum(i, steps // 2 - 1)))
    two = pl.BlockSpec((count, part), lambda i: (0, jnp.maximum(i - steps // 2, 0)))
    lhs = pl.BlockSpec(ha.shape, lambda i: (0, 0))
    rhs = pl.BlockSpec((tokens, part), lambda i: (0, i))
    return pl.pallas_call(
        functools.partial(rows_grad_kernel, outer, used),
        grid=(steps,),
        in_specs=[pl.BlockSpec(memory_space=pltpu.SMEM), lhs, lhs, rhs, rhs],
        out_specs=[one, two, one, two],
        out_shape=[jax.ShapeDtypeStruct((count, width // 2), BF16)] * 2
        + [jax.ShapeDtypeStruct((count, width // 2), F32)] * 2,
        compiler_params=pltpu.CompilerParams(vmem_limit_bytes=48 << 20),
        name="rows_grad",
    )(info, ha, hb, da, db)


def product_kernel(a_ref, b_ref, out_ref):
    out_ref[...] = dot(a_ref[...], b_ref[...]).astype(out_ref.dtype)


def product(a, b, kind):
    count, depth = a.shape
    width = b.shape[1]
    part = min(512, width)
    return pl.pallas_call(
        product_kernel,
        grid=(width // part,),
        in_specs=[
            pl.BlockSpec((count, depth), lambda j: (0, 0)),
            pl.BlockSpec((depth, part), lambda j: (0, j)),
        ],
        out_specs=pl.BlockSpec((count, part), lambda j: (0, j)),
        out_shape=jax.ShapeDtypeStruct((count, width), kind),
        compiler_params=pltpu.CompilerParams(vmem_limit_bytes=32 << 20),
        name="product",
    )(a, b)


def query_back_kernel(rows, d_ref, w_ref, keep_ref, send_ref):
    out = dot_t(d_ref[...], w_ref[...])
    for k in range(2):
        keep_ref[k] = out[2 * k * rows : (2 * k + 1) * rows]
        send_ref[k] = out[(2 * k + 1) * rows : (2 * k + 2) * rows].astype(BF16)


def query_back(d_query, wq, rows):
    width, share = wq.shape
    part = min(512, width)
    out = pl.BlockSpec((2, rows, part), lambda j: (0, 0, j))
    return pl.pallas_call(
        functools.partial(query_back_kernel, rows),
        grid=(width // part,),
        in_specs=[
            pl.BlockSpec(d_query.shape, lambda j: (0, 0)),
            pl.BlockSpec((part, share), lambda j: (j, 0)),
        ],
        out_specs=[out, out],
        out_shape=[
            jax.ShapeDtypeStruct((2, rows, width), F32),
            jax.ShapeDtypeStruct((2, rows, width), BF16),
        ],
        compiler_params=pltpu.CompilerParams(vmem_limit_bytes=32 << 20),
        name="query_back",
    )(d_query, wq)


def unpack_kernel(
    outer, chunk, wide, info_ref, got_g, got_u, w_gate, w_up, gain, gate_ref, up_ref, dg_ref
):
    g, bit = info_ref[0], (info_ref[1] >> 1) & 1
    total = 0.0
    for got, ref, weight in ((got_g, gate_ref, w_gate), (got_u, up_ref, w_up)):
        parts = []
        for member in range(4):
            pieces = [got[member ^ g, b ^ bit] for b in range(2)]
            for o in range(outer):
                for b in range(2):
                    for xd in range(2):
                        at = (xd * outer + o) * wide
                        parts.append(pieces[b][:, at : at + chunk])
        grad = jnp.concatenate(parts, axis=1).astype(F32)
        ref[...] = grad
        total = total + jnp.sum(grad * weight[...].astype(F32), axis=1, keepdims=True)
    dg_ref[...] = total / gain[...]


def unpack(info, got_g, got_u, w_gate, w_up, gain, outer, chunk, wide):
    rows = got_g.shape[2]
    weight = pl.BlockSpec((rows, w_gate.shape[1]), lambda i, info: (info[1], 0))
    shape = jax.ShapeDtypeStruct((rows, 16 * outer * chunk), F32)
    def whole(value):
        return pl.BlockSpec(value.shape, lambda i, info: (0,) * len(value.shape))

    outs = [shape, shape, jax.ShapeDtypeStruct((rows, 1), F32)]
    return pl.pallas_call(
        functools.partial(unpack_kernel, outer, chunk, wide),
        grid_spec=pltpu.PrefetchScalarGridSpec(
            num_scalar_prefetch=1,
            grid=(1,),
            in_specs=[whole(got_g), whole(got_u), weight, weight, whole(gain)],
            out_specs=[whole(out) for out in outs],
        ),
        out_shape=outs,
        compiler_params=pltpu.CompilerParams(vmem_limit_bytes=32 << 20),
        name="unpack",
    )(info, got_g, got_u, w_gate, w_up, gain)


def block_bounds(info_ref, starts_ref, j, reps):
    place = ((info_ref[0] ^ j) * reps + info_ref[1]) * HD
    docs = starts_ref.shape[0]
    first = jnp.int32(0)
    for d in range(docs):
        first = jnp.maximum(first, jnp.where(starts_ref[d] <= place, starts_ref[d], 0))
    position = place + lax.broadcasted_iota(jnp.int32, (4, HD, 1), 1).reshape(4 * HD, 1)
    lowest = jnp.zeros_like(position)
    for d in range(docs):
        lowest = jnp.maximum(lowest, jnp.where(starts_ref[d] <= position, starts_ref[d], 0))
    return place, first, position, lowest


def key_tile(info_ref, slots_ref, kv_ref, tile, reps):
    per = reps // TILE
    member = (tile // per) ^ info_ref[0]
    base = TILE * (tile % per)
    piece = jnp.concatenate([kv_ref[slots_ref[base + k], member] for k in range(TILE)], axis=0)
    return piece[:, :HD], piece[:, HD:]


def head_rows(ref):
    return jnp.concatenate([ref[0, :, h * HD : (h + 1) * HD] for h in range(4)], axis=0)


def attend_kernel(reps, info_ref, slots_ref, starts_ref, q_ref, kv_ref, o_ref, lse_ref):
    j = pl.program_id(0)
    place, first, position, lowest = block_bounds(info_ref, starts_ref, j, reps)
    query = head_rows(q_ref)
    rows = 4 * HD
    scale = HD ** (-0.5)

    def step(tile, carry):
        best, total, accum = carry
        key, value = key_tile(info_ref, slots_ref, kv_ref, tile, reps)
        scores = dot_t(query, key) * scale
        at = tile * TILE * HD + lax.broadcasted_iota(jnp.int32, (1, TILE * HD), 1)
        scores = jnp.where((at >= lowest) & (at <= position), scores, NEGATIVE)
        new_best = jnp.maximum(best, jnp.max(scores, axis=1, keepdims=True))
        weights = jnp.exp(scores - new_best)
        factor = jnp.exp(best - new_best)
        total = total * factor + jnp.sum(weights, axis=1, keepdims=True)
        accum = accum * factor + dot(weights.astype(BF16), value)
        return new_best, total, accum

    init = (
        jnp.full((rows, 1), NEGATIVE, F32),
        jnp.zeros((rows, 1), F32),
        jnp.zeros((rows, HD), F32),
    )
    best, total, accum = lax.fori_loop(
        first // (TILE * HD), place // (TILE * HD) + 1, step, init
    )
    out = accum / total
    for h in range(4):
        o_ref[0, :, h * HD : (h + 1) * HD] = out[h * HD : (h + 1) * HD].astype(BF16)
    lse_ref[0] = best + jnp.log(total)


def attend(info, slots, starts, query, kv):
    reps = kv.shape[0]
    return pl.pallas_call(
        functools.partial(attend_kernel, reps),
        grid=(4,),
        in_specs=[
            pl.BlockSpec(memory_space=pltpu.SMEM),
            pl.BlockSpec(memory_space=pltpu.SMEM),
            pl.BlockSpec(memory_space=pltpu.SMEM),
            pl.BlockSpec((1, HD, 4 * HD), lambda j: (j, 0, 0)),
            pl.BlockSpec(kv.shape, lambda j: (0, 0, 0, 0)),
        ],
        out_specs=[
            pl.BlockSpec((1, HD, 4 * HD), lambda j: (j, 0, 0)),
            pl.BlockSpec((1, 4 * HD, 1), lambda j: (j, 0, 0)),
        ],
        out_shape=[
            jax.ShapeDtypeStruct((4, HD, 4 * HD), BF16),
            jax.ShapeDtypeStruct((4, 4 * HD, 1), F32),
        ],
        compiler_params=pltpu.CompilerParams(vmem_limit_bytes=48 << 20),
        name="attend",
    )(info, slots, starts, query, kv)


def attend_back_kernel(
    reps,
    info_ref,
    slots_ref,
    starts_ref,
    q_ref,
    do_ref,
    o_ref,
    lse_ref,
    kv_ref,
    dq_ref,
    keep_ref,
    send_ref,
    sums,
):
    j = pl.program_id(0)

    @pl.when(j == 0)
    def _():
        sums[...] = jnp.zeros_like(sums)

    place, first, position, lowest = block_bounds(info_ref, starts_ref, j, reps)
    query = head_rows(q_ref)
    d_out = head_rows(do_ref)
    out = head_rows(o_ref)
    lse = lse_ref[0]
    delta = jnp.sum(d_out.astype(F32) * out.astype(F32), axis=1, keepdims=True)
    scale = HD ** (-0.5)
    per = reps // TILE

    def step(tile, d_query):
        key, value = key_tile(info_ref, slots_ref, kv_ref, tile, reps)
        scores = dot_t(query, key) * scale
        at = tile * TILE * HD + lax.broadcasted_iota(jnp.int32, (1, TILE * HD), 1)
        probs = jnp.where((at >= lowest) & (at <= position), jnp.exp(scores - lse), 0.0)
        d_probs = dot_t(d_out, value)
        d_scores = (probs * (d_probs - delta)).astype(BF16)
        d_query = d_query + dot(d_scores, key)
        d_key = t_dot(d_scores, query) * scale
        d_value = t_dot(probs.astype(BF16), d_out)
        member = (tile // per) ^ info_ref[0]
        both = jnp.concatenate([d_key, d_value], axis=1)
        for k in range(TILE):
            slot = (TILE * (tile % per) + k) ^ info_ref[1]
            sums[slot, member] = sums[slot, member] + both[k * HD : (k + 1) * HD]
        return d_query

    d_query = lax.fori_loop(
        first // (TILE * HD),
        place // (TILE * HD) + 1,
        step,
        jnp.zeros((4 * HD, HD), F32),
    )
    d_query = (d_query * scale).astype(BF16)
    for h in range(4):
        dq_ref[0, :, h * HD : (h + 1) * HD] = d_query[h * HD : (h + 1) * HD]

    @pl.when(j == 3)
    def _():
        for slot in range(reps // 2):
            keep_ref[slot] = sums[2 * slot].astype(BF16)
            send_ref[slot] = sums[2 * slot + 1].astype(BF16)


def attend_back(info, slots, starts, query, d_out, out, lse, kv):
    reps = kv.shape[0]
    rows = pl.BlockSpec((1, HD, 4 * HD), lambda j: (j, 0, 0))
    whole = pl.BlockSpec(kv.shape, lambda j: (0, 0, 0, 0))
    half = pl.BlockSpec((reps // 2,) + kv.shape[1:], lambda j: (0, 0, 0, 0))
    return pl.pallas_call(
        functools.partial(attend_back_kernel, reps),
        grid=(4,),
        in_specs=[
            pl.BlockSpec(memory_space=pltpu.SMEM),
            pl.BlockSpec(memory_space=pltpu.SMEM),
            pl.BlockSpec(memory_space=pltpu.SMEM),
            rows,
            rows,
            rows,
            pl.BlockSpec((1, 4 * HD, 1), lambda j: (j, 0, 0)),
            whole,
        ],
        out_specs=[rows, half, half],
        out_shape=[jax.ShapeDtypeStruct((4, HD, 4 * HD), BF16)]
        + [jax.ShapeDtypeStruct((reps // 2,) + kv.shape[1:], BF16)] * 2,
        scratch_shapes=[pltpu.VMEM(kv.shape, F32)],
        compiler_params=pltpu.CompilerParams(vmem_limit_bytes=60 << 20),
        name="attend_back",
    )(info, slots, starts, query, d_out, out, lse, kv)


def on_device(
    tokens,
    cotangent,
    gain_attn,
    gain_ffn,
    w_query,
    w_out,
    w_gate,
    w_up,
    w_down,
    keys,
    values,
    starts,
):
    reps = lax.axis_size("rep")
    rows, width = tokens.shape
    hidden_all = w_gate.shape[1]
    g = lax.axis_index("grp")
    r = lax.axis_index("rep")
    core, yy, xx, zz = reps, 2 * reps, 1, 2
    high = [1 << k for k in range(2, 16) if (1 << k) < reps]
    outer = reps // 4
    x_bit, z_bit = r & 1, (r >> 1) & 1
    share = width // 4
    out_rows = width // (4 * reps)
    chunk = hidden_all // (4 * reps)
    wide = -(-(2 * outer * chunk) // 256) * 256 // (2 * outer)
    mine = 2 * outer * wide
    used = -(-chunk // 16) * 16
    info = jnp.stack([g, r]).astype(jnp.int32)

    kv_parts = [
        jnp.concatenate(
            [
                lax.dynamic_slice_in_dim(keys, (g ^ j) * HD, HD, 1),
                lax.dynamic_slice_in_dim(values, (g ^ j) * HD, HD, 1),
            ],
            axis=1,
        )
        for j in range(4)
    ]
    kv_y = swap(jnp.stack([kv_parts[2], kv_parts[3]]), yy)
    kv_own = jnp.stack([kv_parts[0], swap(kv_parts[1], core), kv_y[0], swap(kv_y[1], core)])

    x_full = tokens.astype(F32)
    inv_one = lax.rsqrt(jnp.mean(x_full * x_full, axis=1, keepdims=True) + EPSILON)
    normed_one = x_full * inv_one
    h_one = (normed_one * gain_attn).astype(BF16)

    h_y = swap(after(h_one, kv_y), yy)
    wq_half = share // 2
    wq_y = jnp.stack(
        [
            lax.dynamic_slice(w_query, (x_bit * wq_half, (g ^ j) * share), (wq_half, share))
            for j in (2, 3)
        ]
    )
    wd = pack_down(info, w_down, outer, chunk, wide)
    if reps == 8:
        pairs = ring_of(reps)
        one = lax.ppermute(kv_own, BOTH, pairs)
        zero_x = swap(kv_own, xx)
        wq_y = swap(after(wq_y, kv_own), yy)
        one, h_y, wd, zero_x = together(one, h_y, wd, zero_x)
        stay, to_core, to_y, relay = pack(after(info, one), w_gate, w_up, outer, chunk, wide)
        two = lax.ppermute(one, BOTH, pairs)
        one_x = swap(one, xx)
        two, wq_y, stay, one_x = together(two, wq_y, stay, one_x)
        three = lax.ppermute(two, BOTH, pairs)
        wq_x = swap(wq_y, xx)
        two_x = swap(two, xx)
        dy_y = swap(after(cotangent, two), yy)
        three, two_x = together(three, two_x)
        three_x = swap(three, xx)
        three_x, wq_x, dy_y = together(three_x, wq_x, dy_y)
        kv = jnp.stack([kv_own, zero_x, one, one_x, two, two_x, three, three_x])
        slots = ring_slots(r, reps)
        relay = swap(after(relay, wq_y), yy)
    else:
        stay, to_core, to_y, relay = pack(info, w_gate, w_up, outer, chunk, wide)
        wq_y, dy_y, relay = swap(wq_y, yy), swap(cotangent, yy), swap(relay, yy)
        wq_x = swap(wq_y, xx)
        kv = lax.all_gather(kv_own, "rep", axis=0, tiled=False)
        slots = jnp.arange(reps, dtype=jnp.int32)

    h_group = jnp.stack([h_one, swap(h_one, core), h_y, swap(h_y, core)])
    h_group = h_group.reshape(4 * rows, width)
    upper_half = x_bit == 1
    wq_y = jnp.concatenate(
        [jnp.where(upper_half, wq_x, wq_y), jnp.where(upper_half, wq_y, wq_x)], axis=1
    )
    wq_parts = [
        lax.dynamic_slice_in_dim(w_query, g * share, share, 1),
        swap(lax.dynamic_slice_in_dim(w_query, (g ^ 1) * share, share, 1), core),
        wq_y[0],
        swap(wq_y[1], core),
    ]
    wq_cols = jnp.concatenate(absolute(wq_parts, g), axis=0)
    query = dot(h_group, wq_cols).astype(BF16).reshape(4, rows, share)

    dy_near = jnp.stack([cotangent, dy_y])
    dy_far = swap(dy_near, zz)
    attn, lse = attend(info, slots, starts, query, kv)
    attn, lse, relay = together(attn, lse, relay)
    from_y = swap(after(to_y, relay), yy)
    relay_x = swap(relay, xx)
    attn_rows = attn.reshape(4 * rows, share)
    branch = scatter_four_core(dot(attn_rows, w_out).reshape(4, rows, width), core)
    from_branch = swap(branch[1].astype(BF16), yy)
    from_branch, from_y = together(from_branch, from_y)
    resid = x_full + branch[0] + from_branch.astype(F32)
    inv_two = lax.rsqrt(jnp.mean(resid * resid, axis=1, keepdims=True) + EPSILON)
    normed_two = resid * inv_two
    h_two = (normed_two * gain_ffn).astype(BF16)

    h_y, h_z = swap(h_two, yy), swap(h_two, zz)
    from_y_x = swap(from_y, xx)
    h_y, h_z, relay_x = together(h_y, h_z, relay_x)
    low, upp = swap(h_y[: rows // 2], zz), swap(h_z[rows // 2 :], yy)
    low, upp, from_y_x, dy_far = together(low, upp, from_y_x, dy_far)
    h_a = jnp.concatenate([h_two, h_y, h_z, low, upp])
    h_b = swap(h_a, core)
    dy_a = jnp.stack([dy_near, dy_far]).reshape(4 * rows, width)
    dy_b = swap(dy_a, core)
    diagonal, diagonal_x = swap(relay, core), swap(relay_x, core)
    w_gu = jnp.concatenate(
        absolute(
            [
                stay,
                swap(to_core, core),
                jnp.concatenate(
                    [
                        jnp.where(upper_half, from_y_x, from_y),
                        jnp.where(upper_half, from_y, from_y_x),
                    ]
                ),
                jnp.concatenate(
                    [
                        jnp.where(upper_half, diagonal_x, diagonal),
                        jnp.where(upper_half, diagonal, diagonal_x),
                    ]
                ),
            ],
            g,
        ),
        axis=0,
    )

    hidden_b, d_gate_b, d_up_b = feed_forward(h_b, dy_b, w_gu, wd)
    from_core = swap(inputs_grad(d_gate_b, d_up_b, w_gu), core)
    hidden_a, d_gate_a, d_up_a = feed_forward(h_a, after(dy_a, d_up_b), w_gu, wd)
    d_h_parts, corner_low, corner_upp = inputs_grad(d_gate_a, d_up_a, w_gu, from_core)

    to_z, to_y = swap(corner_low, yy), swap(corner_upp, zz)
    send_g, send_u, keep_g, keep_u = columns_grad(
        after(info, d_h_parts), h_a, h_b, d_gate_a, d_gate_b, d_up_a, d_up_b, out_rows
    )
    to_z, to_y, send_g = together(to_z, to_y, send_g)
    got_g = swap(send_g, xx)
    from_z, from_y = side_step(d_h_parts, to_z, to_y, rows, yy, zz)
    out_core = swap(product(after(hidden_b, to_z), wd, BF16), core)
    send_d, send_e, keep_d, keep_e = rows_grad(
        after(info, to_z), hidden_a, hidden_b, dy_a, dy_b, outer, used
    )
    out_parts = dot(after(hidden_a, to_z), wd)
    from_z, from_y, out_core, send_d, out_parts = together(
        from_z, from_y, out_core, send_d, out_parts
    )
    d_h_two = d_h_parts[:rows] + from_z.astype(F32) + from_y.astype(F32)
    scaled_two = d_h_two * gain_ffn
    d_resid = cotangent.astype(F32) + inv_two * (
        scaled_two - normed_two * jnp.mean(scaled_two * normed_two, axis=1, keepdims=True)
    )
    da_own = d_resid.astype(BF16)
    da_y, da_c = swap(da_own, yy), swap(da_own, core)
    out_parts = (out_parts + out_core.astype(F32)).reshape(2, 2, rows, width)
    da_y, da_c = together(da_y, da_c)
    d_group = jnp.stack([da_own, da_c, da_y, swap(da_y, core)]).reshape(4 * rows, width)
    d_group, got_g = together(d_group, got_g)

    got_u = swap(after(send_u, got_g), xx)
    grad_g = (keep_g + got_g.astype(F32)).reshape(4, outer, 2, out_rows, mine)
    keep_g, got_g = high_part(grad_g, r, high[-1], 1)
    d_attn = dot_t(d_group, w_out).astype(BF16).reshape(4, rows, share)
    grad_o = t_dot(attn_rows, d_group).reshape(outer, 2, 2, out_rows, width)
    keep_o, got_o = part(grad_o, z_bit, zz, 1)
    out_y = swap(after(out_parts, d_group)[:, 1].astype(BF16), yy)
    d_query, keep_kv, send_kv = attend_back(info, slots, starts, query, d_attn, attn, lse, kv)
    d_query, send_kv, got_u, out_y = together(d_query, send_kv, got_u, out_y)

    got_kv = swap(send_kv, xx)
    grad_u = (keep_u + got_u.astype(F32)).reshape(4, outer, 2, out_rows, mine)
    keep_u, got_u = high_part(grad_u, r, high[-1], 1)
    d_query = d_query.reshape(4 * rows, share)
    d_h_one, send_h = query_back(d_query, wq_cols, rows)
    got_h = swap(send_h, core)
    d_wq = t_dot(h_group, d_query).reshape(4, outer, 2, 2, out_rows, share)
    out_parts = out_parts[:, 0] + out_y.astype(F32)
    got_h, got_g, d_wq = together(got_h, got_g, d_wq)

    d_h_one = d_h_one + got_h.astype(F32)
    from_h = swap(d_h_one[1].astype(BF16), yy)
    grad_g = high_rest(keep_g, got_g, r, high, 1).astype(BF16)
    near_g, far_g = pick(grad_g, z_bit, 1), swap(pick(grad_g, 1 - z_bit, 1), zz)
    got_kv, d_wq = together(got_kv, d_wq)

    keep_q, got_q = part(d_wq, x_bit, xx, 3)
    grad_kv = keep_kv.astype(F32) + got_kv.astype(F32)
    grad_kv = grad_kv.reshape((outer, 2) + grad_kv.shape[1:])
    keep_kv, got_kv = grad_kv[:, 0], swap(grad_kv[:, 1].astype(BF16), zz)
    from_h, far_g, got_u, got_o = together(from_h, far_g, got_u, got_o)

    d_h_one = d_h_one[0] + from_h.astype(F32)
    scaled_one = d_h_one * gain_attn
    d_tokens = (
        d_resid
        + inv_one
        * (scaled_one - normed_one * jnp.mean(scaled_one * normed_one, axis=1, keepdims=True))
    ).astype(BF16)
    grad_g = jnp.stack([near_g, far_g])
    grad_g = [pick(grad_g, g ^ j, 1) for j in range(4)]
    y_g = swap(jnp.stack([grad_g[2], grad_g[3]]), yy)
    grad_u = high_rest(keep_u, got_u, r, high, 1).astype(BF16)
    near_u, far_u = pick(grad_u, z_bit, 1), swap(pick(grad_u, 1 - z_bit, 1), zz)
    y_g, got_kv, got_q, send_d, send_e = together(y_g, got_kv, got_q, send_d, send_e)

    got_d = swap(send_d, xx)
    keep_q, got_q = part(keep_q + got_q.astype(F32), z_bit, zz, 2)
    grad_kv = keep_kv + got_kv.astype(F32)
    for mask in reversed(high):
        grad_kv = grad_kv.reshape((2, grad_kv.shape[0] // 2) + grad_kv.shape[1:])
        grad_kv = grad_kv[0] + swap(grad_kv[1].astype(BF16), mask).astype(F32)
    grad_g = jnp.stack(
        [grad_g[0], swap(after(grad_g[1], y_g), core), y_g[0], swap(y_g[1], core)]
    )
    far_u, got_d, got_q, send_e, out_parts = together(far_u, got_d, got_q, send_e, out_parts)
    out_z = swap(out_parts[1].astype(BF16), zz)

    got_e = swap(send_e, xx)
    keep_q, got_q = high_part(keep_q + got_q.astype(F32), r, high[-1], 1)
    grad_d = (keep_d + got_d.astype(F32)).reshape(outer, used, width // 2)
    keep_d, got_d = high_part(grad_d, r, high[-1], 0)
    grad_u = jnp.stack([near_u, far_u])
    grad_u = [pick(grad_u, g ^ j, 1) for j in range(4)]
    y_u = swap(jnp.stack([grad_u[2], grad_u[3]]), yy)
    y_u, got_e, got_q, grad_g, grad_kv, keep_o = together(
        y_u, got_e, got_q, grad_g, grad_kv, keep_o
    )

    grad_e = (keep_e + got_e.astype(F32)).reshape(outer, used, width // 2)
    keep_e, got_e = high_part(grad_e, r, high[-1], 0)
    keep_o, got_o = part(keep_o + got_o.astype(F32), x_bit, xx, 1)
    grad_kv = grad_kv[0].astype(BF16)
    y_kv = swap(jnp.stack([grad_kv[2], grad_kv[3]]), yy)
    grad_u = jnp.stack(
        [grad_u[0], swap(after(grad_u[1], y_u), core), y_u[0], swap(y_u[1], core)]
    )
    d_wq = high_rest(keep_q, got_q, r, high, 1).astype(BF16)
    d_wq = [pick(d_wq, g ^ j, 0) for j in range(4)]
    y_q = swap(jnp.stack([d_wq[2], d_wq[3]]), yy)
    y_q, y_kv, grad_u, got_o, got_d, got_e, out_z = together(
        y_q, y_kv, grad_u, got_o, got_d, got_e, out_z
    )

    keep_o, got_o = high_part(keep_o + got_o.astype(F32), r, high[-1], 0)
    c_q, cy_q = swap(after(d_wq[1], y_q), core), swap(y_q[1], core)
    d_wq = absolute([d_wq[0], c_q, y_q[0], cy_q], g)
    d_wquery = jnp.concatenate(d_wq, axis=1).astype(F32)
    grad_kv = [grad_kv[0], swap(after(grad_kv[1], y_kv), core), y_kv[0], swap(y_kv[1], core)]
    grad_kv = absolute(grad_kv, g)
    d_keys = jnp.concatenate([piece[:, :HD] for piece in grad_kv], axis=1)
    d_values = jnp.concatenate([piece[:, HD:] for piece in grad_kv], axis=1)
    output = (resid + out_parts[0] + out_z.astype(F32)).astype(BF16)
    d_wout = high_rest(keep_o, got_o, r, high, 0)
    d_wdown = jnp.concatenate(
        [high_rest(keep_d, got_d, r, high, 0), high_rest(keep_e, got_e, r, high, 0)], axis=1
    )[:chunk]

    def own_rows(value):
        return lax.dynamic_slice_in_dim(value, r * out_rows, out_rows, 0)

    gain_at = (g * reps + r) * out_rows
    gain_rows = lax.dynamic_slice_in_dim(gain_ffn, gain_at, out_rows, 0)[:, None]
    d_wgate, d_wup, d_gain_two = unpack(
        info, grad_g, grad_u, w_gate, w_up, gain_rows, outer, chunk, wide
    )
    gain_rows = lax.dynamic_slice_in_dim(gain_attn, gain_at, out_rows, 0)
    d_gain_one = jnp.sum(d_wquery * own_rows(w_query).astype(F32), axis=1) / gain_rows
    return (
        output,
        d_tokens,
        d_gain_one,
        d_gain_two[:, 0],
        d_wquery,
        d_wout,
        d_wgate,
        d_wup,
        d_wdown,
        d_keys,
        d_values,
    )


def solution(mesh):
    spread = P(BOTH, None)
    member = P("grp", None)
    in_specs = (
        spread,
        spread,
        P(),
        P(),
        member,
        member,
        member,
        member,
        member,
        spread,
        spread,
        P(),
    )
    out_specs = (
        spread,
        spread,
        P(BOTH),
        P(BOTH),
        spread,
        spread,
        spread,
        spread,
        spread,
        spread,
        spread,
    )
    return jax.shard_map(
        on_device, mesh=mesh, in_specs=in_specs, out_specs=out_specs, check_vma=False
    )
```
